32 devices in a mesh: dp: 8 (over y, x, core), fsdp: 4 (over z).
Axes of the slice: x: 2, y: 2, z: 4, core: 2. Of those that a mesh axis runs over, the one named last changes fastest.
Arguments:
- hidden_in: bfloat16 [32768, 768], P(('dp', 'fsdp')), may hold values from -6 to 6
- cotangent: bfloat16 [32768, 768], P(('dp', 'fsdp')), may hold values from -6 to 6
- seq_lengths: int32 [32, 4], P(('dp', 'fsdp')), may hold values from 0 to 1024, as said below
- in_weight: float32 [2, 768, 3352], P(None, ('dp', 'fsdp')), may hold values from -0.21875 to 0.21875
- out_weight: float32 [2, 1536, 768], P(None, ('dp', 'fsdp')), may hold values from -0.15625 to 0.15625
- vector_weight: float32 [2, 11264], P(None, ('dp', 'fsdp'))
- head_weight: float32 [2, 3, 24], replicated
- in_row_moment: float32 [2, 768], P(None, ('dp', 'fsdp')), may hold values from 819 to 8192
- in_col_moment: float32 [2, 3352], replicated, may hold values from 163 to 1638
- out_row_moment: float32 [2, 1536], P(None, ('dp', 'fsdp')), may hold values from 16384 to 65536
- out_col_moment: float32 [2, 768], replicated, may hold values from 16384 to 65536
- vector_moment: float32 [2, 11264], P(None, ('dp', 'fsdp')), may hold values from 16384 to 65536
- head_moment: float32 [2, 3, 24], replicated, may hold values from 163 to 1638
Outputs:
- layer_out: bfloat16 [32768, 768], P(('dp', 'fsdp'))
- input_grad: float32 [32768, 768], P(('dp', 'fsdp'))
- in_grad: float32 [2, 768, 3352], P(None, ('dp', 'fsdp'))
- out_grad: float32 [2, 1536, 768], P(None, ('dp', 'fsdp'))
- vector_grad: float32 [2, 11264], P(None, ('dp', 'fsdp'))
- head_grad: float32 [2, 3, 24], replicated
- new_in_weight: float32 [2, 768, 3352], P(None, ('dp', 'fsdp'))
- new_out_weight: float32 [2, 1536, 768], P(None, ('dp', 'fsdp'))
- new_vector_weight: float32 [2, 11264], P(None, ('dp', 'fsdp'))
- new_head_weight: float32 [2, 3, 24], replicated
- in_copy: bfloat16 [2, 768, 3352], P(None, ('dp', 'fsdp'))
- out_copy: bfloat16 [2, 1536, 768], P(None, ('dp', 'fsdp'))
- vector_copy: bfloat16 [2, 11264], P(None, ('dp', 'fsdp'))
- head_copy: bfloat16 [2, 3, 24], replicated
- new_in_row: float32 [2, 768], P(None, ('dp', 'fsdp'))
- new_in_col: float32 [2, 3352], replicated
- new_out_row: float32 [2, 1536], P(None, ('dp', 'fsdp'))
- new_out_col: float32 [2, 768], replicated
- new_vector_moment: float32 [2, 11264], P(None, ('dp', 'fsdp'))
- new_head_moment: float32 [2, 3, 24], replicated
- update_rms: float32 [2, 4], replicated
The draws below stay inside these ranges and needn't reach their ends.
Inputs may be any that keep to these rules, and one draw needn't show every extreme that they name: `seq_lengths`: each slot lists the lengths of its 1 to 3 sequences in its first entries and zeros after them; each length is at least 256, a slot's lengths add up to more than 512 and at most 1024; positions after them are padding.
All inputs are finite; a program needn't handle non-finite values.
Results may differ from the reference program's by a relative error of at most 0.0085.
The reference program's roundings to bfloat16 on the way count: a program that leaves them out, or rounds other values in their place, can miss the bound.
Values may be sent and summed in bfloat16 or wider, within the bound.
No kernel may reach another device: no remote copies, remote signals or barrier semaphores. Data moves between devices by JAX's collectives and lax.ppermute only.
A program may use at most 384 MiB of HBM per device.

```python
import math
from functools import partial
import jax
import jax.numpy as jnp
from jax import lax

D = 768
NHEADS = 24
HEADDIM = 64
STATE = 128
SPAN = 256
SLOT = 1024
MAXSEQ = 4
LAYERS = 2
INNER = 1536
CH = 1792
P_SIZE = 3352
VEC = 11264
SLOTS = 32
TOKENS = 32768


def draw_seq_lengths(key, part):
    key_one, key_two = jax.random.split(key)
    how_many = jax.random.randint(key_one, (SLOTS, 1), 1, 4)
    raw_bits = jax.random.randint(key_two, (SLOTS, MAXSEQ), 0, 1 << 20)
    low_end = jnp.where(how_many == 1, SLOT // 2 + 1, jnp.where(how_many == 2, SLOT // 4 + 1, SLOT // 4))
    high_end = SLOT // how_many
    lengths = low_end + raw_bits % (high_end - low_end + 1)
    column = jnp.arange(MAXSEQ)[None, :]
    lengths = jnp.where(column < how_many, lengths, 0)
    first_row = jnp.where(jnp.arange(MAXSEQ) == 0, SLOT, 0)
    lengths = lengths.at[0].set(first_row)
    return lengths.astype(jnp.int32)


def gain_rise(position, top_ratio):
    norm_place = jnp.where(position < D, position / D, (position - D) / INNER).astype(jnp.float32)
    return jnp.exp(jnp.log(top_ratio) * (norm_place - 0.5))


def draw_vector_weight(key, part):
    key_one, key_two = jax.random.split(key)
    position = jnp.arange(VEC)[None, :]
    gain_part = gain_rise(position, 3.0) * jax.random.uniform(key_one, (LAYERS, VEC), jnp.float32, 0.7, 1.3)
    spread = 0.5 * jax.random.normal(key_two, (LAYERS, VEC), jnp.float32)
    taps_end = D + INNER + 4 * CH
    bias_part = 0.5 * jnp.clip(spread, -1.0, 1.0)
    values = jnp.where(position < D + INNER, gain_part, jnp.where(position < taps_end, spread, bias_part))
    return values.astype(jnp.float32)


def draw_head_weight(key, part):
    key_one, key_two, key_three = jax.random.split(key, 3)
    step_bias = jax.random.uniform(key_one, (LAYERS, NHEADS), jnp.float32, -6.0, -2.5)
    rate_log = jax.random.uniform(key_two, (LAYERS, NHEADS), jnp.float32, 0.0, 2.5)
    skip_part = jax.random.uniform(key_three, (LAYERS, NHEADS), jnp.float32, 0.5, 1.5)
    return jnp.stack([step_bias, rate_log, skip_part], axis=1)


def levels(own_key, dims, cuts, smallest, top_value):
    gain = 1.0
    for dim, shards_of in cuts:
        draws = jax.random.uniform(jax.random.fold_in(jax.random.fold_in(own_key, 6), dim), (shards_of,), jnp.float32, smallest / len(cuts), top_value / len(cuts))
        gain = gain * jnp.repeat(jnp.exp(draws), dims[dim] // shards_of).reshape((-1,) + (1,) * (len(dims) - 1 - dim))
    return gain


def bell_draw(own_key, dims, scale, limit, cuts=(), kind=jnp.bfloat16):
    entries = jax.random.normal(own_key, dims, jnp.float32) * scale
    if len(cuts) > 0:
        entries = levels(own_key, dims, cuts, -0.22, 0.18) * entries
    return jnp.clip(entries, min=-limit, max=limit).astype(kind)


def setup_inputs(seed: int = 0) -> dict:
    streams_of = jax.random.split(jax.random.key(seed), 14)
    return {
        "hidden_in": bell_draw(streams_of[0], (TOKENS, D), 1.0, 6.0, ((0, 32),)),
        "cotangent": bell_draw(streams_of[1], (TOKENS, D), 1.0, 6.0, ((0, 32),)),
        "seq_lengths": draw_seq_lengths(jax.random.fold_in(streams_of[13], 71), 0),
        "in_weight": bell_draw(streams_of[3], (LAYERS, D, P_SIZE), D ** -0.5, 0.21875, ((1, 32),), jnp.float32),
        "out_weight": bell_draw(streams_of[4], (LAYERS, INNER, D), INNER ** -0.5, 0.15625, ((1, 32),), jnp.float32),
        "vector_weight": draw_vector_weight(jax.random.fold_in(streams_of[13], 71), 0),
        "head_weight": draw_head_weight(jax.random.fold_in(streams_of[13], 71), 0),
        "in_row_moment": jnp.clip(jnp.exp(math.log(8192.0) - 2.3028293 * jax.random.uniform(streams_of[7], (LAYERS, D), jnp.float32) ** levels(streams_of[7], (LAYERS, D), ((1, 32),), -0.2, 0.2)), 819.0, 8192.0),
        "in_col_moment": jnp.clip(jnp.exp(jax.random.uniform(streams_of[8], (LAYERS, P_SIZE), jnp.float32, math.log(163.0), math.log(1638.0))), 163.0, 1638.0),
        "out_row_moment": jnp.clip(jnp.exp(math.log(65536.0) - 1.3862944 * jax.random.uniform(streams_of[9], (LAYERS, INNER), jnp.float32) ** levels(streams_of[9], (LAYERS, INNER), ((1, 32),), -0.2, 0.2)), 16384.0, 65536.0),
        "out_col_moment": jnp.clip(jnp.exp(jax.random.uniform(streams_of[10], (LAYERS, D), jnp.float32, math.log(16384.0), math.log(65536.0))), 16384.0, 65536.0),
        "vector_moment": jnp.clip(jnp.exp(math.log(65536.0) - 1.3862944 * jax.random.uniform(streams_of[11], (LAYERS, VEC), jnp.float32) ** levels(streams_of[11], (LAYERS, VEC), ((1, 32),), -0.2, 0.2)), 16384.0, 65536.0),
        "head_moment": jnp.clip(jnp.exp(jax.random.uniform(streams_of[12], (LAYERS, 3, NHEADS), jnp.float32, math.log(163.0), math.log(1638.0))), 163.0, 1638.0),
    }


@jax.custom_vjp
def low(v):
    return lax.optimization_barrier(v.astype(jnp.bfloat16)).astype(jnp.float32)

@jax.custom_vjp
def low_back(v):
    return v

def low_keep(v):
    return (low(v), None)

def low_pass(kept, grad):
    return (grad,)

def back_keep(v):
    return (v, None)

def back_low(kept, grad):
    return (low(grad),)
low.defvjp(low_keep, low_pass)
low_back.defvjp(back_keep, back_low)
EPSILON = 1e-05
MOMENT_DECAY = 0.5
CLIP_LIMIT = 1.0
RELATIVE_STEP = 0.5
PRECISE = lax.Precision.HIGHEST

def segment_ids(lengths, token_count):
    ends_at = jnp.cumsum(lengths).astype(jnp.int32)
    position = jnp.arange(token_count, dtype=jnp.int32)
    segments = lax.optimization_barrier(jnp.sum((position[:, None] >= ends_at[None, :]).astype(jnp.int32), axis=1)).astype(jnp.int32)
    valid_mask = (position < ends_at[-1]).astype(jnp.float32)
    return (segments, valid_mask)

def rms_norm(values, scales):
    return values * lax.rsqrt(lax.optimization_barrier(jnp.mean(values * values, axis=-1, keepdims=True)) + EPSILON) * scales

def causal_conv(inputs, segments, kernel, offset):
    channels = inputs.shape[1]
    result = offset[None, :] + kernel[3][None, :] * inputs
    for lag_rows in range(1, 4):
        earlier = jnp.concatenate([jnp.zeros((lag_rows, channels), jnp.float32), inputs[:-lag_rows]], axis=0)
        earlier_seg = jnp.concatenate([jnp.full((lag_rows,), -1, jnp.int32), segments[:-lag_rows]], axis=0)
        result = result + kernel[3 - lag_rows][None, :] * jnp.where((earlier_seg == segments)[:, None], earlier, 0.0)
    return result

def span_terms(block_items):
    span_x, span_b, span_c, cumlog, span_dt, span_seg = block_items
    places = jnp.arange(span_seg.shape[0])
    allowed = (span_seg[:, None] == span_seg[None, :]) & (places[:, None] >= places[None, :])
    intersections = jnp.dot(span_c, span_b.T, precision=PRECISE)
    head_cum = cumlog.T
    log_gaps = jnp.where(allowed[None], head_cum[:, :, None] - head_cum[:, None, :], 0.0)
    mixing = jnp.where(allowed[None], jnp.exp(log_gaps), 0.0) * intersections[None] * span_dt.T[:, None, :]
    within = jnp.einsum('hij,jhp->ihp', mixing, span_x, precision=PRECISE)
    to_end = jnp.where((span_seg == span_seg[-1])[:, None], jnp.exp(cumlog[-1][None, :] - cumlog), 0.0) * span_dt
    local_state = jnp.einsum('js,jhp->hsp', span_b, span_x * to_end[:, :, None], precision=PRECISE)
    return (within, local_state)

def state_space(inputs_x, inputs_b, inputs_c, log_rate, steps_dt, segments):
    token_count, head_count, head_dim = inputs_x.shape
    blocks = token_count // SPAN
    span_x = inputs_x.reshape(blocks, SPAN, head_count, head_dim)
    span_b = inputs_b.reshape(blocks, SPAN, STATE)
    span_c = inputs_c.reshape(blocks, SPAN, STATE)
    span_rate = log_rate.reshape(blocks, SPAN, head_count)
    span_dt = steps_dt.reshape(blocks, SPAN, head_count)
    span_seg = segments.reshape(blocks, SPAN)
    cumlog = jnp.cumsum(span_rate, axis=1)
    within, local_state = lax.map(jax.checkpoint(span_terms), (span_x, span_b, span_c, cumlog, span_dt, span_seg))
    last_seg = span_seg[:, -1]
    prior_seg = jnp.concatenate([jnp.full((1,), -1, jnp.int32), last_seg[:-1]], axis=0)
    linked = last_seg == prior_seg

    def advance(state_in, step_items):
        local_one, cum_last, link_one = step_items
        carried = jnp.where(link_one, jnp.exp(cum_last), 0.0)[:, None, None] * state_in
        return (carried + local_one, state_in)
    start_state = jnp.zeros((head_count, STATE, head_dim), jnp.float32)
    final_state, entering = lax.scan(advance, start_state, (local_state, cumlog[:, -1, :], linked))
    inflow = jnp.einsum('cis,chsp->cihp', span_c, entering, precision=PRECISE)
    reach_in = jnp.where((span_seg == prior_seg[:, None])[:, :, None], jnp.exp(cumlog), 0.0)
    result = within + inflow * reach_in[..., None]
    return result.reshape(token_count, head_count, head_dim)

def mixer(in_proj, vector_w, head_w, segments):
    token_count = in_proj.shape[0]
    gate_in = in_proj[:, :INNER]
    conv_in = in_proj[:, INNER:INNER + CH]
    rate_in = in_proj[:, INNER + CH:]
    kernel = vector_w[D + INNER:D + INNER + 4 * CH].reshape(4, CH)
    offset = vector_w[D + INNER + 4 * CH:]
    mixed_out = jax.nn.silu(causal_conv(conv_in, segments, kernel, offset))
    inputs_x = mixed_out[:, :INNER].reshape(token_count, NHEADS, HEADDIM)
    inputs_b = mixed_out[:, INNER:INNER + STATE]
    inputs_c = mixed_out[:, INNER + STATE:]
    steps_dt = jax.nn.softplus(rate_in + head_w[0][None, :])
    log_rate = -jnp.exp(head_w[1])[None, :] * steps_dt
    output = state_space(inputs_x, inputs_b, inputs_c, log_rate, steps_dt, segments) + head_w[2][None, :, None] * inputs_x
    gated_out = output.reshape(token_count, INNER) * jax.nn.silu(gate_in)
    return rms_norm(gated_out, vector_w[D:D + INNER][None, :])

def block_layer(stream, segments, weight_in, weight_out, vector_part, head_part):
    normed = low(rms_norm(stream, vector_part[:D][None, :]))
    in_proj = low_back(jnp.dot(normed, weight_in, precision=PRECISE))
    mixed_out = low(mixer(in_proj, vector_part, head_part, segments))
    return stream + low_back(jnp.dot(mixed_out, weight_out, precision=PRECISE))

def factored_step(weight, gradient, row_moment, col_moment):
    squares = gradient * gradient
    new_row = MOMENT_DECAY * row_moment + (1.0 - MOMENT_DECAY) * lax.optimization_barrier(jnp.mean(squares, axis=2))
    new_col = MOMENT_DECAY * col_moment + (1.0 - MOMENT_DECAY) * lax.optimization_barrier(jnp.mean(squares, axis=1))
    estimate = new_row[:, :, None] * new_col[:, None, :] / lax.optimization_barrier(jnp.mean(new_row, axis=1))[:, None, None]
    update = gradient * lax.rsqrt(estimate)
    update_norm = jnp.sqrt(lax.optimization_barrier(jnp.mean(update * update, axis=(1, 2))))
    step_size = RELATIVE_STEP * jnp.sqrt(lax.optimization_barrier(jnp.mean(weight * weight, axis=(1, 2)))) / jnp.maximum(1.0, update_norm / CLIP_LIMIT)
    return (weight - step_size[:, None, None] * update, new_row, new_col, update_norm)

def plain_step(weight, gradient, moment, axes_list):
    new_moment = MOMENT_DECAY * moment + (1.0 - MOMENT_DECAY) * gradient * gradient
    update = gradient * lax.rsqrt(new_moment)
    update_norm = jnp.sqrt(lax.optimization_barrier(jnp.mean(update * update, axis=axes_list)))
    step_size = RELATIVE_STEP * jnp.sqrt(lax.optimization_barrier(jnp.mean(weight * weight, axis=axes_list))) / jnp.maximum(1.0, update_norm / CLIP_LIMIT)
    shaped = step_size.reshape(step_size.shape + (1,) * len(axes_list))
    return (weight - shaped * update, new_moment, update_norm)

def reference(hidden_in, cotangent, seq_lengths, in_weight, out_weight, vector_weight, head_weight, in_row_moment, in_col_moment, out_row_moment, out_col_moment, vector_moment, head_moment):
    slot_count = seq_lengths.shape[0]
    segments, valid_mask = jax.vmap(lambda lengths: segment_ids(lengths, SLOT))(seq_lengths)
    group_size = max(1, min(slot_count, 4096 // SLOT))
    group_count = slot_count // group_size
    start_hidden = hidden_in.astype(jnp.float32).reshape(group_count, group_size, SLOT, D)
    seg_groups = segments.reshape(group_count, group_size, SLOT)

    def forward(start_hidden, in_weight, out_weight, vector_weight, head_weight):
        weight_in = low(in_weight)
        weight_out = low(out_weight)
        vector_part = low(vector_weight)

        def run_group(group_items):
            stream, seg_block = group_items
            for layer_idx in range(LAYERS):
                stream = jax.vmap(partial(block_layer, weight_in=weight_in[layer_idx], weight_out=weight_out[layer_idx], vector_part=vector_part[layer_idx], head_part=head_weight[layer_idx]))(stream, seg_block)
            return stream
        return lax.map(jax.checkpoint(run_group), (start_hidden, seg_groups))
    outputs, pullback = jax.vjp(forward, start_hidden, in_weight, out_weight, vector_weight, head_weight)
    seed_grad = cotangent.astype(jnp.float32).reshape(group_count, group_size, SLOT, D) * valid_mask.reshape(group_count, group_size, SLOT)[..., None]
    hidden_grad, in_grad, out_grad, vector_grad, head_grad = pullback(seed_grad)
    new_in, new_in_row, new_in_col, norm_in = factored_step(in_weight, in_grad, in_row_moment, in_col_moment)
    new_out, new_out_row, new_out_col, norm_out = factored_step(out_weight, out_grad, out_row_moment, out_col_moment)
    new_vector, new_vector_moment, norm_vector = plain_step(vector_weight, vector_grad, vector_moment, (1,))
    new_head, new_head_moment, norm_head = plain_step(head_weight, head_grad, head_moment, (1, 2))
    update_rms = jnp.stack([norm_in, norm_out, norm_vector, norm_head], axis=1)
    layer_out = outputs.reshape(slot_count * SLOT, D).astype(jnp.bfloat16)
    input_grad = hidden_grad.reshape(slot_count * SLOT, D)
    return (layer_out, input_grad, in_grad, out_grad, vector_grad, head_grad, new_in, new_out, new_vector, new_head, new_in.astype(jnp.bfloat16), new_out.astype(jnp.bfloat16), new_vector.astype(jnp.bfloat16), new_head.astype(jnp.bfloat16), new_in_row, new_in_col, new_out_row, new_out_col, new_vector_moment, new_head_moment, update_rms)
```

```python
from functools import partial

import jax
import jax.numpy as jnp
from jax import lax
from jax.experimental import pallas as pl
from jax.experimental.pallas import tpu as pltpu
from jax.sharding import PartitionSpec as P

D = 768
NHEADS = 24
HEADDIM = 64
STATE = 128
LAYERS = 2
INNER = 1536
CH = 1792
P_SIZE = 3352
VEC = 11264

EPSILON = 1e-05
MOMENT_DECAY = 0.5
CLIP_LIMIT = 1.0
RELATIVE_STEP = 0.5

SPAN = 128
GROUP = 256
GROUPS = INNER // GROUP
LANES = 128
LOG2E = 1.4426950408889634
VMEM_LIMIT = 60 * 1024 * 1024
F32 = jnp.float32
BF16 = jnp.bfloat16
NN = ((1,), (0,))
NT = ((1,), (1,))
TN = ((0,), (0,))

PASS_PAIR = 3
PASS_STATE = 3
PASS_RED = 2


def halves(v):
    high = v.astype(BF16)
    return high, (v - high.astype(F32)).astype(BF16)


def raw_dot(a, b, dims):
    return lax.dot_general(a, b, (dims, ((), ())), preferred_element_type=F32)


def mm(a, b, dims, passes):
    if passes == 1:
        return raw_dot(a.astype(BF16), b.astype(BF16), dims)
    a_hi, a_lo = halves(a)
    b_hi, b_lo = halves(b)
    return raw_dot(a_hi, b_hi, dims) + (raw_dot(a_lo, b_hi, dims) + raw_dot(a_hi, b_lo, dims))


def exact_left(a01, b):
    hi, lo = halves(b)
    rest = (b - hi.astype(F32) - lo.astype(F32)).astype(BF16)
    return raw_dot(a01, hi, NN) + (raw_dot(a01, lo, NN) + raw_dot(a01, rest, NN))


def reduce_right(a, b01, passes):
    if passes == 1:
        return raw_dot(a.astype(BF16), b01, NN)
    hi, lo = halves(a)
    return raw_dot(hi, b01, NN) + raw_dot(lo, b01, NN)


def sigmoid(v):
    return 0.5 * jnp.tanh(0.5 * v) + 0.5


def partial8(v):
    return jnp.sum(v.reshape(v.shape[0] // 8, 8, v.shape[1]), axis=0)


def segment_of(place, ends_ref):
    total = (place >= ends_ref[0]).astype(jnp.int32)
    for k in range(1, 4):
        total = total + (place >= ends_ref[k]).astype(jnp.int32)
    return total


def scalar_segment(place, ends_ref):
    total = jnp.int32(0)
    for k in range(4):
        total = total + jnp.where(place >= ends_ref[k], 1, 0).astype(jnp.int32)
    return total


def block_terms(base, ends_ref, hw_ref, rate_in):
    shape = (SPAN, LANES)
    place = base + lax.broadcasted_iota(jnp.int32, shape, 0)
    seg = segment_of(place, ends_ref)
    first_seg = jnp.where(base > 0, scalar_segment(base - 1, ends_ref), -1)
    last_seg = scalar_segment(base + SPAN - 1, ends_ref)
    pre = rate_in + hw_ref[0:1, :]
    head_ok = lax.broadcasted_iota(jnp.int32, shape, 1) < NHEADS
    steps = jnp.where(head_ok, jnp.maximum(pre, 0.0) + jnp.log1p(jnp.exp(-jnp.abs(pre))), 0.0)
    log_rate = hw_ref[1:2, :] * steps
    rows = lax.broadcasted_iota(jnp.int32, (SPAN, SPAN), 0)
    cols = lax.broadcasted_iota(jnp.int32, (SPAN, SPAN), 1)
    lower = jnp.where(rows >= cols, 1.0, 0.0)
    cum = exact_left(lower.astype(BF16), log_rate * LOG2E)
    reach = jnp.where(seg == first_seg, jnp.exp2(cum), 0.0)
    to_end = jnp.where(seg == last_seg, jnp.exp2(cum[SPAN - 1 : SPAN, :] - cum), 0.0)
    seg_row = segment_of(base + cols, ends_ref)
    seg_col = segment_of(base + rows, ends_ref)
    same = seg_row == seg_col
    return place, seg, pre, steps, log_rate, cum, reach, to_end, rows, cols, same


def lag_mask(place, seg, ends_ref, lag):
    other = place + lag
    ok = (segment_of(other, ends_ref) == seg) & (other >= 0)
    return jnp.where(ok, 1.0, 0.0)


def two_parts(v):
    hi, lo = halves(v)
    return jnp.concatenate([hi, lo], axis=1)


def lane_split(v):
    first = lax.broadcasted_iota(jnp.int32, v.shape, 1) < HEADDIM
    return jnp.concatenate([jnp.where(first, v, 0.0), jnp.where(first, 0.0, v)], axis=0)


def pair_columns(cum, head):
    one = jnp.broadcast_to(cum[:, head : head + 1], (SPAN, SPAN))
    two = jnp.broadcast_to(cum[:, head + 1 : head + 2], (SPAN, SPAN))
    return jnp.concatenate([one, two], axis=1)


def pair_rows(cum_t, head):
    return jnp.concatenate([cum_t[head : head + 1, :], cum_t[head + 1 : head + 2, :]], axis=1)


def forward_kernel(
    ends_ref, zx_ref, par_ref, gain_ref, hw_ref, spread_ref, gn_ref, ys_ref, st_ref, buf, act, pad, state, yg
):
    block = pl.program_id(0)
    base = block * SPAN

    @pl.when(block == 0)
    def _():
        buf[0:8, :] = jnp.zeros((8, CH), F32)
        state[...] = jnp.zeros_like(state)
        pad[...] = jnp.zeros_like(pad)

    pad[:, 0:NHEADS] = zx_ref[:, INNER + CH : P_SIZE]
    place, seg, pre, steps, log_rate, cum, reach, to_end, rows, cols, same = block_terms(
        base, ends_ref, hw_ref, pad[...]
    )
    masks = [lag_mask(place, seg, ends_ref, -k) for k in range(1, 4)]
    for c in range(CH // LANES):
        cs = slice(LANES * c, LANES * (c + 1))
        now = zx_ref[:, INNER + LANES * c : INNER + LANES * (c + 1)]
        buf[8 : 8 + SPAN, cs] = now
        conv = par_ref[4:5, cs] + par_ref[3:4, cs] * now
        for k in range(1, 4):
            conv = conv + par_ref[3 - k : 4 - k, cs] * (masks[k - 1] * buf[8 - k : 8 - k + SPAN, cs])
        buf[0:8, cs] = now[SPAN - 8 : SPAN, :]
        act[:, cs] = conv * sigmoid(conv)
    bm = act[:, INNER : INNER + STATE]
    cm = act[:, INNER + STATE : CH]
    gram = mm(cm, bm, NT, 3)
    gram2 = jnp.concatenate([gram, gram], axis=1)
    bias = jnp.where(same & (rows >= cols), 0.0, -1e30)
    bias2 = jnp.concatenate([bias, bias], axis=1)
    cum_t = cum.T
    bm_t = bm.T
    steps2, reach2, to_end2 = two_parts(steps), two_parts(reach), two_parts(to_end)
    st_ref[0] = state[...]
    squares = jnp.zeros((SPAN, LANES), F32)
    for g in range(GROUPS):
        gs = slice(GROUP * g, GROUP * (g + 1))
        spread = spread_ref[:, gs]
        x = act[:, gs]
        xd = x * raw_dot(steps2, spread, NN)
        within = []
        for q in range(2):
            head = 4 * g + 2 * q
            mix = jnp.exp2(pair_columns(cum, head) - pair_rows(cum_t, head) + bias2) * gram2
            within.append(mm(mix, lane_split(xd[:, LANES * q : LANES * (q + 1)]), NN, PASS_PAIR))
        reach_g = raw_dot(reach2, spread, NN)
        before = state[:, gs]
        scan = jnp.concatenate(within, axis=1) + mm(cm, before, NN, PASS_STATE) * reach_g
        ys_ref[:, gs] = scan
        state[:, gs] = before * reach_g[SPAN - 1 : SPAN, :] + mm(
            bm_t, xd * raw_dot(to_end2, spread, NN), NN, PASS_STATE
        )
        z = zx_ref[:, gs]
        gated = (scan + gain_ref[1:2, gs] * x) * (z * sigmoid(z))
        yg[:, gs] = gated
        gated = gated * gated
        squares = squares + gated[:, :LANES] + gated[:, LANES:]
    scale = lax.rsqrt(jnp.sum(squares, axis=1, keepdims=True) / INNER + EPSILON)
    for g in range(GROUPS):
        gs = slice(GROUP * g, GROUP * (g + 1))
        gn_ref[:, gs] = (yg[:, gs] * scale * gain_ref[0:1, gs]).astype(BF16)


def backward_kernel(
    ends_ref, zx_ref, halo_ref, dgn_ref, ys_ref, st_ref, par_ref, gain_ref, hw_ref, spread_ref, gather_ref,
    dzx_ref, dpar_ref, dgain_ref, dhw_ref,
    buf, act, slope, dact, dcv, pad, rgrad, yg, dgram,
):
    step = pl.program_id(0)
    block = pl.num_programs(0) - 1 - step
    base = block * SPAN

    @pl.when(step == 0)
    def _():
        dcv[0:8, :] = jnp.zeros((8, CH), F32)
        rgrad[...] = jnp.zeros_like(rgrad)
        pad[...] = jnp.zeros_like(pad)
        dpar_ref[...] = jnp.zeros_like(dpar_ref)
        dgain_ref[...] = jnp.zeros_like(dgain_ref)
        dhw_ref[...] = jnp.zeros_like(dhw_ref)

    pad[:, 0:NHEADS] = zx_ref[:, INNER + CH : P_SIZE]
    place, seg, pre, steps, log_rate, cum, reach, to_end, rows, cols, same = block_terms(
        base, ends_ref, hw_ref, pad[...]
    )
    back_masks = [lag_mask(place, seg, ends_ref, -k) for k in range(1, 4)]
    fore_masks = [lag_mask(place, seg, ends_ref, k) for k in range(1, 4)]
    for c in range(CH // LANES):
        cs = slice(LANES * c, LANES * (c + 1))
        zs = slice(INNER + LANES * c, INNER + LANES * (c + 1))
        now = zx_ref[:, zs]
        buf[0:8, cs] = halo_ref[:, zs]
        buf[8 : 8 + SPAN, cs] = now
        conv = par_ref[4:5, cs] + par_ref[3:4, cs] * now
        for k in range(1, 4):
            conv = conv + par_ref[3 - k : 4 - k, cs] * (back_masks[k - 1] * buf[8 - k : 8 - k + SPAN, cs])
        gate = sigmoid(conv)
        act[:, cs] = conv * gate
        slope[:, cs] = gate * (1.0 + conv * (1.0 - gate))
        dcv[SPAN : SPAN + 8, cs] = dcv[0:8, cs]
    bm = act[:, INNER : INNER + STATE]
    cm = act[:, INNER + STATE : CH]
    gram_t = mm(cm, bm, NT, 3).T
    gram2 = jnp.concatenate([gram_t, gram_t], axis=1)
    bias = jnp.where(same & (rows <= cols), 0.0, -1e30)
    bias2 = jnp.concatenate([bias, bias], axis=1)
    cum_t = cum.T
    cm_t = cm.T
    steps2, reach2, to_end2 = two_parts(steps), two_parts(reach), two_parts(to_end)

    squares = jnp.zeros((SPAN, LANES), F32)
    overlap = jnp.zeros((SPAN, LANES), F32)
    for g in range(GROUPS):
        gs = slice(GROUP * g, GROUP * (g + 1))
        z = zx_ref[:, gs]
        gated = (ys_ref[:, gs] + gain_ref[1:2, gs] * act[:, gs]) * (z * sigmoid(z))
        yg[:, gs] = gated
        shared = gated * (dgn_ref[:, gs] * gain_ref[0:1, gs])
        gated = gated * gated
        squares = squares + gated[:, :LANES] + gated[:, LANES:]
        overlap = overlap + shared[:, :LANES] + shared[:, LANES:]
    scale = lax.rsqrt(jnp.sum(squares, axis=1, keepdims=True) / INNER + EPSILON)
    pull = jnp.sum(overlap, axis=1, keepdims=True) * (scale * scale * scale) / INNER

    dgram[...] = jnp.zeros_like(dgram)
    dbm = jnp.zeros((SPAN, STATE), F32)
    dcm = jnp.zeros((SPAN, STATE), F32)
    red_rate = jnp.zeros((SPAN, LANES), F32)
    red_tail = jnp.zeros((SPAN, LANES), F32)
    red_step = jnp.zeros((SPAN, LANES), F32)
    red_through = jnp.zeros((8, LANES), F32)
    for g in range(GROUPS):
        gs = slice(GROUP * g, GROUP * (g + 1))
        spread = spread_ref[:, gs]
        gather = gather_ref[gs, :]
        x = act[:, gs]
        z = zx_ref[:, gs]
        gate = sigmoid(z)
        soft = z * gate
        scan = ys_ref[:, gs]
        skip = gain_ref[1:2, gs]
        y = scan + skip * x
        gated = yg[:, gs]
        dgn = dgn_ref[:, gs]
        dgated = scale * (dgn * gain_ref[0:1, gs]) - gated * pull
        dgain_ref[0:8, gs] += partial8(dgn * (gated * scale))
        dy = dgated * soft
        dzx_ref[:, gs] = (dgated * y * (gate * (1.0 + z * (1.0 - gate)))).astype(BF16)
        dgain_ref[8:16, gs] += partial8(dy * x)
        steps_g = raw_dot(steps2, spread, NN)
        reach_g = raw_dot(reach2, spread, NN)
        to_end_g = raw_dot(to_end2, spread, NN)
        xd = x * steps_g
        dxd_in = []
        for q in range(2):
            head = 4 * g + 2 * q
            qs = slice(LANES * q, LANES * (q + 1))
            decay = jnp.exp2(pair_rows(cum_t, head) - pair_columns(cum, head) + bias2)
            dy_two = lane_split(dy[:, qs])
            dxd_in.append(mm(decay * gram2, dy_two, NN, PASS_PAIR))
            dgram[...] += decay * mm(xd[:, qs], dy_two, NT, PASS_PAIR)
        dxd_in = jnp.concatenate(dxd_in, axis=1)
        later = rgrad[:, gs]
        before = st_ref[0, :, gs]
        dxd_out = mm(bm, later, NN, PASS_STATE) * to_end_g
        dbm = dbm + mm(xd * to_end_g, later, NT, PASS_STATE)
        dy_reach = dy * reach_g
        dcm = dcm + mm(dy_reach, before, NT, PASS_STATE)
        fade = reach_g[SPAN - 1 : SPAN, :]
        red_through = red_through + reduce_right(partial8(before * later) * fade, gather, 2)
        rgrad[:, gs] = later * fade + mm(cm_t, dy_reach, NN, PASS_STATE)
        if PASS_PAIR == 1:
            dy_seen, xd_seen = dy.astype(BF16).astype(F32), xd.astype(BF16).astype(F32)
        else:
            dy_seen, xd_seen = dy, xd
        dxd = dxd_in + dxd_out
        red_rate = red_rate + reduce_right(dy_seen * scan - xd_seen * dxd_in, gather, 2)
        red_tail = red_tail + reduce_right(x * dxd_out, gather, PASS_RED)
        red_step = red_step + reduce_right(x * dxd, gather, PASS_RED)
        dact[:, gs] = skip * dy + steps_g * dxd
    dgram_t = dgram[:, :SPAN] + dgram[:, SPAN:]
    dact[:, INNER : INNER + STATE] = dbm + mm(dgram_t, cm, NN, 3)
    dact[:, INNER + STATE : CH] = dcm + mm(dgram_t.T, bm, NN, 3)

    upper = jnp.where(rows <= cols, 1.0, 0.0).astype(BF16)
    strict = jnp.where(rows > cols, 1.0, 0.0).astype(BF16)
    through = jnp.sum(red_through, axis=0, keepdims=True)
    drate = exact_left(upper, red_rate) + exact_left(strict, steps * red_tail) + through
    dsteps = red_step + drate * hw_ref[1:2, :]
    dpre = dsteps * sigmoid(pre)
    dhw_ref[0:8, :] += partial8(dpre)
    dhw_ref[8:16, :] += partial8(drate * log_rate)
    dzx_ref[:, INNER + CH : P_SIZE] = dpre[:, :NHEADS].astype(BF16)

    for c in range(CH // LANES):
        cs = slice(LANES * c, LANES * (c + 1))
        dconv = dact[:, cs] * slope[:, cs]
        dcv[0:SPAN, cs] = dconv
        dxbc = par_ref[3:4, cs] * dconv
        dpar_ref[24:32, cs] += partial8(dconv * buf[8 : 8 + SPAN, cs])
        dpar_ref[32:40, cs] += partial8(dconv)
        for k in range(1, 4):
            dxbc = dxbc + par_ref[3 - k : 4 - k, cs] * (fore_masks[k - 1] * dcv[k : k + SPAN, cs])
            dpar_ref[24 - 8 * k : 32 - 8 * k, cs] += partial8(
                dconv * (back_masks[k - 1] * buf[8 - k : 8 - k + SPAN, cs])
            )
        dzx_ref[:, INNER + LANES * c : INNER + LANES * (c + 1)] = dxbc.astype(BF16)


def spread_matrices():
    heads = lax.broadcasted_iota(jnp.int32, (LANES, INNER), 0)
    lanes = lax.broadcasted_iota(jnp.int32, (LANES, INNER), 1) // HEADDIM
    one = (heads == lanes).astype(BF16)
    return jnp.concatenate([one, one], axis=0), one.T


def kernel_params(vector, head):
    taps = vector[D + INNER :].reshape(5, CH)
    par = jnp.concatenate([taps, jnp.zeros((3, CH), F32)], axis=0)
    gain = jnp.stack([vector[D : D + INNER], jnp.repeat(head[2], HEADDIM)])
    gain = jnp.concatenate([gain, jnp.zeros((6, INNER), F32)], axis=0)
    hw = jnp.stack([head[0], -jnp.exp(head[1])])
    hw = jnp.pad(hw, ((0, 6), (0, LANES - NHEADS)))
    return par, gain, hw


def whole(shape):
    return pl.BlockSpec(shape, lambda i: (0,) * len(shape))


SMEM = pl.BlockSpec(memory_space=pltpu.SMEM)


def mixer_forward(ends, zx, par, gain, hw, spread):
    tokens = zx.shape[0]
    blocks = tokens // SPAN
    rows = lambda width: pl.BlockSpec((SPAN, width), lambda i: (i, 0))
    return pl.pallas_call(
        forward_kernel,
        grid=(blocks,),
        in_specs=[SMEM, rows(P_SIZE), whole((8, CH)), whole((8, INNER)), whole((8, LANES)), whole((256, INNER))],
        out_specs=[rows(INNER), rows(INNER), pl.BlockSpec((1, STATE, INNER), lambda i: (i, 0, 0))],
        out_shape=[
            jax.ShapeDtypeStruct((tokens, INNER), BF16),
            jax.ShapeDtypeStruct((tokens, INNER), F32),
            jax.ShapeDtypeStruct((blocks, STATE, INNER), F32),
        ],
        scratch_shapes=[
            pltpu.VMEM((SPAN + 8, CH), F32),
            pltpu.VMEM((SPAN, CH), F32),
            pltpu.VMEM((SPAN, LANES), F32),
            pltpu.VMEM((STATE, INNER), F32),
            pltpu.VMEM((SPAN, INNER), F32),
        ],
        compiler_params=pltpu.CompilerParams(vmem_limit_bytes=VMEM_LIMIT),
        cost_estimate=pl.CostEstimate(flops=20_000_000_000, bytes_accessed=30_000_000, transcendentals=6_000_000),
        name="mixer_forward",
    )(ends, zx, par, gain, hw, spread)


def mixer_backward(ends, zx, dgn, ys, st, par, gain, hw, spread, gather):
    tokens = zx.shape[0]
    blocks = tokens // SPAN
    back = lambda width: pl.BlockSpec((SPAN, width), lambda i: (blocks - 1 - i, 0))
    halo = pl.BlockSpec((8, P_SIZE), lambda i: (jnp.maximum((blocks - 1 - i) * (SPAN // 8) - 1, 0), 0))
    return pl.pallas_call(
        backward_kernel,
        grid=(blocks,),
        in_specs=[
            SMEM,
            back(P_SIZE),
            halo,
            back(INNER),
            back(INNER),
            pl.BlockSpec((1, STATE, INNER), lambda i: (blocks - 1 - i, 0, 0)),
            whole((8, CH)),
            whole((8, INNER)),
            whole((8, LANES)),
            whole((256, INNER)),
            whole((INNER, LANES)),
        ],
        out_specs=[back(P_SIZE), whole((40, CH)), whole((16, INNER)), whole((16, LANES))],
        out_shape=[
            jax.ShapeDtypeStruct((tokens, P_SIZE), BF16),
            jax.ShapeDtypeStruct((40, CH), F32),
            jax.ShapeDtypeStruct((16, INNER), F32),
            jax.ShapeDtypeStruct((16, LANES), F32),
        ],
        scratch_shapes=[
            pltpu.VMEM((SPAN + 8, CH), F32),
            pltpu.VMEM((SPAN, CH), F32),
            pltpu.VMEM((SPAN, CH), F32),
            pltpu.VMEM((SPAN, CH), F32),
            pltpu.VMEM((SPAN + 8, CH), F32),
            pltpu.VMEM((SPAN, LANES), F32),
            pltpu.VMEM((STATE, INNER), F32),
            pltpu.VMEM((SPAN, INNER), F32),
            pltpu.VMEM((SPAN, 2 * SPAN), F32),
        ],
        compiler_params=pltpu.CompilerParams(vmem_limit_bytes=VMEM_LIMIT),
        cost_estimate=pl.CostEstimate(flops=60_000_000_000, bytes_accessed=60_000_000, transcendentals=9_000_000),
        name="mixer_backward",
    )(ends, zx, zx, dgn, ys, st, par, gain, hw, spread, gather)


def finish_params(dpar, dgain, dhw):
    dtaps = jnp.sum(dpar.reshape(5, 8, CH), axis=1).reshape(5 * CH)
    dgate = jnp.sum(dgain[0:8], axis=0)
    dskip = jnp.sum(dgain[8:16].reshape(8, NHEADS, HEADDIM), axis=(0, 2))
    dh = jnp.sum(dhw.reshape(2, 8, LANES), axis=1)[:, :NHEADS]
    return jnp.concatenate([dgate, dtaps]), jnp.concatenate([dh, dskip[None]], axis=0)


AXES = ("dp", "fsdp")


def rms_norm(values, scales):
    return values * lax.rsqrt(jnp.mean(values * values, axis=-1, keepdims=True) + EPSILON) * scales


def norm_part(stream, gain):
    return rms_norm(stream, gain[None, :])


def on_device(
    hidden_in,
    cotangent,
    seq_lengths,
    in_weight,
    out_weight,
    vector_weight,
    head_weight,
    in_row_moment,
    in_col_moment,
    out_row_moment,
    out_col_moment,
    vector_moment,
    head_moment,
):
    token_count = hidden_in.shape[0]
    lengths = seq_lengths[0]
    e0 = lengths[0]
    e1 = e0 + lengths[1]
    e2 = e1 + lengths[2]
    e3 = e2 + lengths[3]
    ends = jnp.stack([e0, e1, e2, e3])
    valid = (jnp.arange(token_count, dtype=jnp.int32) < e3).astype(F32)
    spread, gather = spread_matrices()
    vector_full = lax.all_gather(vector_weight.astype(BF16), AXES, axis=1, tiled=True).astype(F32)
    stream = hidden_in.astype(F32)
    stored = []
    for l in range(LAYERS):
        full_in = lax.all_gather(in_weight[l].astype(BF16), AXES, axis=0, tiled=True)
        full_out = lax.all_gather(out_weight[l].astype(BF16), AXES, axis=0, tiled=True)
        tables = kernel_params(vector_full[l], head_weight[l])
        normed, norm_pull = jax.vjp(norm_part, stream, vector_full[l, :D])
        normed = normed.astype(BF16)
        zx = jnp.dot(normed, full_in, preferred_element_type=F32)
        gn, ys, st = mixer_forward(ends, zx, *tables, spread)
        stream = stream + jnp.dot(gn, full_out, preferred_element_type=F32)
        stored.append((norm_pull, normed, zx, gn, ys, st, tables, full_in, full_out))
    layer_out = stream.astype(BF16)
    flowing = cotangent.astype(F32) * valid[:, None]
    in_parts = [None] * LAYERS
    out_parts = [None] * LAYERS
    vector_parts = [None] * LAYERS
    head_parts = [None] * LAYERS
    for l in reversed(range(LAYERS)):
        norm_pull, normed, zx, gn, ys, st, tables, full_in, full_out = stored[l]
        gb = flowing.astype(BF16)
        grad_out = jnp.einsum("te,td->ed", gn, gb, preferred_element_type=F32)
        dgn = jnp.einsum("td,ed->te", gb, full_out, preferred_element_type=F32)
        dzx, dpar, dgain, dhw = mixer_backward(ends, zx, dgn, ys, st, *tables, spread, gather)
        grad_in = jnp.einsum("td,tp->dp", normed, dzx, preferred_element_type=F32)
        dxn = jnp.einsum("tp,dp->td", dzx, full_in, preferred_element_type=F32)
        grad_stream, dnorm = norm_pull(dxn)
        flowing = flowing + grad_stream
        dvec, head_parts[l] = finish_params(dpar, dgain, dhw)
        vector_parts[l] = jnp.concatenate([dnorm, dvec])
        in_parts[l] = lax.psum_scatter(grad_in, AXES, scatter_dimension=0, tiled=True)
        out_parts[l] = lax.psum_scatter(grad_out, AXES, scatter_dimension=0, tiled=True)
    grad_in = jnp.stack(in_parts)
    grad_out = jnp.stack(out_parts)
    grad_vector = lax.psum_scatter(jnp.stack(vector_parts), AXES, scatter_dimension=1, tiled=True)
    head_part = jnp.stack(head_parts)
    squares_in = grad_in * grad_in
    squares_out = grad_out * grad_out
    row_in = MOMENT_DECAY * in_row_moment + (1.0 - MOMENT_DECAY) * jnp.mean(squares_in, axis=2)
    row_out = MOMENT_DECAY * out_row_moment + (1.0 - MOMENT_DECAY) * jnp.mean(squares_out, axis=2)
    vector_new = MOMENT_DECAY * vector_moment + (1.0 - MOMENT_DECAY) * grad_vector * grad_vector
    vector_update = grad_vector * lax.rsqrt(vector_new)
    totals = jnp.stack(
        [
            jnp.sum(row_in, axis=1),
            jnp.sum(row_out, axis=1),
            jnp.sum(in_weight * in_weight, axis=(1, 2)),
            jnp.sum(out_weight * out_weight, axis=(1, 2)),
            jnp.sum(vector_weight * vector_weight, axis=1),
            jnp.sum(vector_update * vector_update, axis=1),
        ],
        axis=1,
    )
    local = (
        jnp.sum(squares_in, axis=1),
        jnp.sum(squares_out, axis=1),
        jnp.sum(squares_in / row_in[:, :, None], axis=1),
        jnp.sum(squares_out / row_out[:, :, None], axis=1),
        head_part.reshape(LAYERS, 3 * NHEADS),
        totals,
    )
    widths = [v.shape[1] for v in local]
    summed = lax.psum(jnp.concatenate(local, axis=1), AXES)
    column_in, column_out, scaled_in, scaled_out, head_total, totals = jnp.split(
        summed, [sum(widths[: i + 1]) for i in range(5)], axis=1
    )
    head_total = head_total.reshape(LAYERS, 3, NHEADS)
    col_in = MOMENT_DECAY * in_col_moment + (1.0 - MOMENT_DECAY) * column_in / D
    col_out = MOMENT_DECAY * out_col_moment + (1.0 - MOMENT_DECAY) * column_out / INNER
    mean_in = totals[:, 0] / D
    mean_out = totals[:, 1] / INNER
    norm_in = jnp.sqrt(mean_in * jnp.sum(scaled_in / col_in, axis=1) / (D * P_SIZE))
    norm_out = jnp.sqrt(mean_out * jnp.sum(scaled_out / col_out, axis=1) / (INNER * D))
    norm_vector = jnp.sqrt(totals[:, 5] / VEC)
    head_new = MOMENT_DECAY * head_moment + (1.0 - MOMENT_DECAY) * head_total * head_total
    head_update = head_total * lax.rsqrt(head_new)
    norm_head = jnp.sqrt(jnp.mean(head_update * head_update, axis=(1, 2)))

    def step_of(square_mean, norm):
        return RELATIVE_STEP * jnp.sqrt(square_mean) / jnp.maximum(1.0, norm / CLIP_LIMIT)

    step_in = step_of(totals[:, 2] / (D * P_SIZE), norm_in)
    step_out = step_of(totals[:, 3] / (INNER * D), norm_out)
    step_vector = step_of(totals[:, 4] / VEC, norm_vector)
    step_head = step_of(jnp.mean(head_weight * head_weight, axis=(1, 2)), norm_head)
    update_in = grad_in * lax.rsqrt(row_in[:, :, None] * col_in[:, None, :] / mean_in[:, None, None])
    update_out = grad_out * lax.rsqrt(row_out[:, :, None] * col_out[:, None, :] / mean_out[:, None, None])
    new_in = in_weight - step_in[:, None, None] * update_in
    new_out = out_weight - step_out[:, None, None] * update_out
    new_vector = vector_weight - step_vector[:, None] * vector_update
    new_head = head_weight - step_head[:, None, None] * head_update
    update_rms = jnp.stack([norm_in, norm_out, norm_vector, norm_head], axis=1)
    return (
        layer_out,
        flowing,
        grad_in,
        grad_out,
        grad_vector,
        head_total,
        new_in,
        new_out,
        new_vector,
        new_head,
        new_in.astype(BF16),
        new_out.astype(BF16),
        new_vector.astype(BF16),
        new_head.astype(BF16),
        row_in,
        col_in,
        row_out,
        col_out,
        vector_new,
        head_new,
        update_rms,
    )


def solution(mesh):
    rows = P(AXES, None)
    mat = P(None, AXES, None)
    vec = P(None, AXES)
    one = P()
    return jax.shard_map(
        on_device,
        mesh=mesh,
        in_specs=(rows, rows, rows, mat, mat, vec, one, vec, one, vec, one, vec, one),
        out_specs=(
            rows, rows, mat, mat, vec, one, mat, mat, vec, one, mat, mat, vec, one, vec, one, vec, one, vec, one, one,
        ),
        check_vma=False,
    )
```

```python
from functools import partial

import jax
import jax.numpy as jnp
from jax import lax
from jax.experimental import pallas as pl
from jax.experimental.pallas import tpu as pltpu
from jax.sharding import PartitionSpec as P

D = 768
NHEADS = 24
HEADDIM = 64
STATE = 128
LAYERS = 2
INNER = 1536
CH = 1792
P_SIZE = 3352
XR = 1920
VEC = 11264

EPSILON = 1e-05
MOMENT_DECAY = 0.5
CLIP_LIMIT = 1.0
RELATIVE_STEP = 0.5

SPAN = 128
GROUP = 256
GROUPS = INNER // GROUP
LANES = 128
LOG2E = 1.4426950408889634
VMEM_LIMIT = 60 * 1024 * 1024
F32 = jnp.float32
BF16 = jnp.bfloat16
NN = ((1,), (0,))
NT = ((1,), (1,))
TN = ((0,), (0,))

PASS_PAIR = 3
PASS_STATE = 3
PASS_RED = 2


def halves(v):
    high = v.astype(BF16)
    return high, (v - high.astype(F32)).astype(BF16)


def raw_dot(a, b, dims):
    return lax.dot_general(a, b, (dims, ((), ())), preferred_element_type=F32)


def mm(a, b, dims, passes):
    if passes == 1:
        return raw_dot(a.astype(BF16), b.astype(BF16), dims)
    a_hi, a_lo = halves(a)
    b_hi, b_lo = halves(b)
    return raw_dot(a_hi, b_hi, dims) + (raw_dot(a_lo, b_hi, dims) + raw_dot(a_hi, b_lo, dims))


def exact_left(a01, b):
    hi, lo = halves(b)
    rest = (b - hi.astype(F32) - lo.astype(F32)).astype(BF16)
    return raw_dot(a01, hi, NN) + (raw_dot(a01, lo, NN) + raw_dot(a01, rest, NN))


def reduce_right(a, b01, passes):
    if passes == 1:
        return raw_dot(a.astype(BF16), b01, NN)
    hi, lo = halves(a)
    return raw_dot(hi, b01, NN) + raw_dot(lo, b01, NN)


def sigmoid(v):
    return 0.5 * jnp.tanh(0.5 * v) + 0.5


def partial8(v):
    return jnp.sum(v.reshape(v.shape[0] // 8, 8, v.shape[1]), axis=0)


def segment_of(place, ends_ref):
    total = (place >= ends_ref[0]).astype(jnp.int32)
    for k in range(1, 4):
        total = total + (place >= ends_ref[k]).astype(jnp.int32)
    return total


def scalar_segment(place, ends_ref):
    total = jnp.int32(0)
    for k in range(4):
        total = total + jnp.where(place >= ends_ref[k], 1, 0).astype(jnp.int32)
    return total


def block_terms(base, ends_ref, hw_ref, rate_in):
    shape = (SPAN, LANES)
    place = base + lax.broadcasted_iota(jnp.int32, shape, 0)
    seg = segment_of(place, ends_ref)
    first_seg = jnp.where(base > 0, scalar_segment(base - 1, ends_ref), -1)
    last_seg = scalar_segment(base + SPAN - 1, ends_ref)
    pre = rate_in + hw_ref[0:1, :]
    head_ok = lax.broadcasted_iota(jnp.int32, shape, 1) < NHEADS
    steps = jnp.where(head_ok, jnp.maximum(pre, 0.0) + jnp.log1p(jnp.exp(-jnp.abs(pre))), 0.0)
    log_rate = hw_ref[1:2, :] * steps
    rows = lax.broadcasted_iota(jnp.int32, (SPAN, SPAN), 0)
    cols = lax.broadcasted_iota(jnp.int32, (SPAN, SPAN), 1)
    lower = jnp.where(rows >= cols, 1.0, 0.0)
    cum = exact_left(lower.astype(BF16), log_rate * LOG2E)
    reach = jnp.where(seg == first_seg, jnp.exp2(cum), 0.0)
    to_end = jnp.where(seg == last_seg, jnp.exp2(cum[SPAN - 1 : SPAN, :] - cum), 0.0)
    seg_row = segment_of(base + cols, ends_ref)
    seg_col = segment_of(base + rows, ends_ref)
    same = seg_row == seg_col
    return place, seg, pre, steps, log_rate, cum, reach, to_end, rows, cols, same


def lag_mask(place, seg, ends_ref, lag):
    other = place + lag
    ok = (segment_of(other, ends_ref) == seg) & (other >= 0)
    return jnp.where(ok, 1.0, 0.0)


def two_parts(v):
    hi, lo = halves(v)
    return jnp.concatenate([hi, lo], axis=1)


def lane_split(v):
    first = lax.broadcasted_iota(jnp.int32, v.shape, 1) < HEADDIM
    return jnp.concatenate([jnp.where(first, v, 0.0), jnp.where(first, 0.0, v)], axis=0)


def pair_columns(cum, head):
    one = jnp.broadcast_to(cum[:, head : head + 1], (SPAN, SPAN))
    two = jnp.broadcast_to(cum[:, head + 1 : head + 2], (SPAN, SPAN))
    return jnp.concatenate([one, two], axis=1)


def pair_rows(cum_t, head):
    return jnp.concatenate([cum_t[head : head + 1, :], cum_t[head + 1 : head + 2, :]], axis=1)


def forward_kernel(
    ends_ref, z_ref, xr_ref, par_ref, gain_ref, hw_ref, spread_ref, gn_ref, ys_ref, st_ref, buf, act, state, yg
):
    block = pl.program_id(0)
    base = block * SPAN

    @pl.when(block == 0)
    def _():
        buf[0:8, :] = jnp.zeros((8, CH), F32)
        state[...] = jnp.zeros_like(state)

    place, seg, pre, steps, log_rate, cum, reach, to_end, rows, cols, same = block_terms(
        base, ends_ref, hw_ref, xr_ref[:, CH:XR]
    )
    masks = [lag_mask(place, seg, ends_ref, -k) for k in range(1, 4)]
    for c in range(CH // LANES):
        cs = slice(LANES * c, LANES * (c + 1))
        now = xr_ref[:, cs]
        buf[8 : 8 + SPAN, cs] = now
        conv = par_ref[4:5, cs] + par_ref[3:4, cs] * now
        for k in range(1, 4):
            conv = conv + par_ref[3 - k : 4 - k, cs] * (masks[k - 1] * buf[8 - k : 8 - k + SPAN, cs])
        buf[0:8, cs] = now[SPAN - 8 : SPAN, :]
        act[:, cs] = conv * sigmoid(conv)
    bm = act[:, INNER : INNER + STATE]
    cm = act[:, INNER + STATE : CH]
    gram = mm(cm, bm, NT, 3)
    gram2 = jnp.concatenate([gram, gram], axis=1)
    bias = jnp.where(same & (rows >= cols), 0.0, -1e30)
    bias2 = jnp.concatenate([bias, bias], axis=1)
    cum_t = cum.T
    bm_t = bm.T
    steps2, reach2, to_end2 = two_parts(steps), two_parts(reach), two_parts(to_end)
    st_ref[0] = state[...]
    squares = jnp.zeros((SPAN, LANES), F32)
    for g in range(GROUPS):
        gs = slice(GROUP * g, GROUP * (g + 1))
        spread = spread_ref[:, gs]
        x = act[:, gs]
        xd = x * raw_dot(steps2, spread, NN)
        within = []
        for q in range(2):
            head = 4 * g + 2 * q
            mix = jnp.exp2(pair_columns(cum, head) - pair_rows(cum_t, head) + bias2) * gram2
            within.append(mm(mix, lane_split(xd[:, LANES * q : LANES * (q + 1)]), NN, PASS_PAIR))
        reach_g = raw_dot(reach2, spread, NN)
        before = state[:, gs]
        scan = jnp.concatenate(within, axis=1) + mm(cm, before, NN, PASS_STATE) * reach_g
        ys_ref[:, gs] = scan
        state[:, gs] = before * reach_g[SPAN - 1 : SPAN, :] + mm(
            bm_t, xd * raw_dot(to_end2, spread, NN), NN, PASS_STATE
        )
        z = z_ref[:, gs]
        gated = (scan + gain_ref[1:2, gs] * x) * (z * sigmoid(z))
        yg[:, gs] = gated
        gated = gated * gated
        squares = squares + gated[:, :LANES] + gated[:, LANES:]
    scale = lax.rsqrt(jnp.sum(squares, axis=1, keepdims=True) / INNER + EPSILON)
    for g in range(GROUPS):
        gs = slice(GROUP * g, GROUP * (g + 1))
        gn_ref[:, gs] = (yg[:, gs] * scale * gain_ref[0:1, gs]).astype(BF16)


def backward_kernel(
    top, ends_ref, z_ref, xr_ref, halo_ref, dgn_ref, ys_ref, st_ref, par_ref, gain_ref, hw_ref, spread_ref, gather_ref,
    *refs,
):
    (
        rgrad_in, dcv_in, dz_ref, dxr_ref, dpar_ref, dgain_ref, dhw_ref, rgrad, dcv_out,
        buf, act, slope, dact, dcv, yg, dgram,
    ) = refs[-16:]
    step = pl.program_id(0)
    block = top - step
    base = block * SPAN

    @pl.when(step == 0)
    def _():
        dcv[0:8, :] = dcv_in[...]
        rgrad[...] = rgrad_in[...]
        dpar_ref[...] = jnp.zeros_like(dpar_ref)
        dgain_ref[...] = jnp.zeros_like(dgain_ref)
        dhw_ref[...] = jnp.zeros_like(dhw_ref)

    place, seg, pre, steps, log_rate, cum, reach, to_end, rows, cols, same = block_terms(
        base, ends_ref, hw_ref, xr_ref[:, CH:XR]
    )
    back_masks = [lag_mask(place, seg, ends_ref, -k) for k in range(1, 4)]
    fore_masks = [lag_mask(place, seg, ends_ref, k) for k in range(1, 4)]
    for c in range(CH // LANES):
        cs = slice(LANES * c, LANES * (c + 1))
        now = xr_ref[:, cs]
        buf[0:8, cs] = halo_ref[:, cs]
        buf[8 : 8 + SPAN, cs] = now
        conv = par_ref[4:5, cs] + par_ref[3:4, cs] * now
        for k in range(1, 4):
            conv = conv + par_ref[3 - k : 4 - k, cs] * (back_masks[k - 1] * buf[8 - k : 8 - k + SPAN, cs])
        gate = sigmoid(conv)
        act[:, cs] = conv * gate
        slope[:, cs] = gate * (1.0 + conv * (1.0 - gate))
        dcv[SPAN : SPAN + 8, cs] = dcv[0:8, cs]
    bm = act[:, INNER : INNER + STATE]
    cm = act[:, INNER + STATE : CH]
    gram_t = mm(cm, bm, NT, 3).T
    gram2 = jnp.concatenate([gram_t, gram_t], axis=1)
    bias = jnp.where(same & (rows <= cols), 0.0, -1e30)
    bias2 = jnp.concatenate([bias, bias], axis=1)
    cum_t = cum.T
    cm_t = cm.T
    steps2, reach2, to_end2 = two_parts(steps), two_parts(reach), two_parts(to_end)

    squares = jnp.zeros((SPAN, LANES), F32)
    overlap = jnp.zeros((SPAN, LANES), F32)
    for g in range(GROUPS):
        gs = slice(GROUP * g, GROUP * (g + 1))
        z = z_ref[:, gs]
        gated = (ys_ref[:, gs] + gain_ref[1:2, gs] * act[:, gs]) * (z * sigmoid(z))
        yg[:, gs] = gated
        shared = gated * (dgn_ref[:, gs] * gain_ref[0:1, gs])
        gated = gated * gated
        squares = squares + gated[:, :LANES] + gated[:, LANES:]
        overlap = overlap + shared[:, :LANES] + shared[:, LANES:]
    scale = lax.rsqrt(jnp.sum(squares, axis=1, keepdims=True) / INNER + EPSILON)
    pull = jnp.sum(overlap, axis=1, keepdims=True) * (scale * scale * scale) / INNER

    dgram[...] = jnp.zeros_like(dgram)
    dbm = jnp.zeros((SPAN, STATE), F32)
    dcm = jnp.zeros((SPAN, STATE), F32)
    red_rate = jnp.zeros((SPAN, LANES), F32)
    red_tail = jnp.zeros((SPAN, LANES), F32)
    red_step = jnp.zeros((SPAN, LANES), F32)
    red_through = jnp.zeros((8, LANES), F32)
    for g in range(GROUPS):
        gs = slice(GROUP * g, GROUP * (g + 1))
        spread = spread_ref[:, gs]
        gather = gather_ref[gs, :]
        x = act[:, gs]
        z = z_ref[:, gs]
        gate = sigmoid(z)
        soft = z * gate
        scan = ys_ref[:, gs]
        skip = gain_ref[1:2, gs]
        y = scan + skip * x
        gated = yg[:, gs]
        dgn = dgn_ref[:, gs]
        dgated = scale * (dgn * gain_ref[0:1, gs]) - gated * pull
        dgain_ref[0:8, gs] += partial8(dgn * (gated * scale))
        dy = dgated * soft
        dz_ref[:, gs] = (dgated * y * (gate * (1.0 + z * (1.0 - gate)))).astype(BF16)
        dgain_ref[8:16, gs] += partial8(dy * x)
        steps_g = raw_dot(steps2, spread, NN)
        reach_g = raw_dot(reach2, spread, NN)
        to_end_g = raw_dot(to_end2, spread, NN)
        xd = x * steps_g
        dxd_in = []
        for q in range(2):
            head = 4 * g + 2 * q
            qs = slice(LANES * q, LANES * (q + 1))
            decay = jnp.exp2(pair_rows(cum_t, head) - pair_columns(cum, head) + bias2)
            dy_two = lane_split(dy[:, qs])
            dxd_in.append(mm(decay * gram2, dy_two, NN, PASS_PAIR))
            dgram[...] += decay * mm(xd[:, qs], dy_two, NT, PASS_PAIR)
        dxd_in = jnp.concatenate(dxd_in, axis=1)
        later = rgrad[:, gs]
        before = st_ref[0, :, gs]
        dxd_out = mm(bm, later, NN, PASS_STATE) * to_end_g
        dbm = dbm + mm(xd * to_end_g, later, NT, PASS_STATE)
        dy_reach = dy * reach_g
        dcm = dcm + mm(dy_reach, before, NT, PASS_STATE)
        fade = reach_g[SPAN - 1 : SPAN, :]
        red_through = red_through + reduce_right(partial8(before * later) * fade, gather, 2)
        rgrad[:, gs] = later * fade + mm(cm_t, dy_reach, NN, PASS_STATE)
        if PASS_PAIR == 1:
            dy_seen, xd_seen = dy.astype(BF16).astype(F32), xd.astype(BF16).astype(F32)
        else:
            dy_seen, xd_seen = dy, xd
        dxd = dxd_in + dxd_out
        red_rate = red_rate + reduce_right(dy_seen * scan - xd_seen * dxd_in, gather, 2)
        red_tail = red_tail + reduce_right(x * dxd_out, gather, PASS_RED)
        red_step = red_step + reduce_right(x * dxd, gather, PASS_RED)
        dact[:, gs] = skip * dy + steps_g * dxd
    dgram_t = dgram[:, :SPAN] + dgram[:, SPAN:]
    dact[:, INNER : INNER + STATE] = dbm + mm(dgram_t, cm, NN, 3)
    dact[:, INNER + STATE : CH] = dcm + mm(dgram_t.T, bm, NN, 3)

    upper = jnp.where(rows <= cols, 1.0, 0.0).astype(BF16)
    strict = jnp.where(rows > cols, 1.0, 0.0).astype(BF16)
    through = jnp.sum(red_through, axis=0, keepdims=True)
    drate = exact_left(upper, red_rate) + exact_left(strict, steps * red_tail) + through
    dsteps = red_step + drate * hw_ref[1:2, :]
    dpre = dsteps * sigmoid(pre)
    dhw_ref[0:8, :] += partial8(dpre)
    dhw_ref[8:16, :] += partial8(drate * log_rate)
    dxr_ref[:, CH:XR] = dpre.astype(BF16)

    for c in range(CH // LANES):
        cs = slice(LANES * c, LANES * (c + 1))
        dconv = dact[:, cs] * slope[:, cs]
        dcv[0:SPAN, cs] = dconv
        dxbc = par_ref[3:4, cs] * dconv
        dpar_ref[24:32, cs] += partial8(dconv * buf[8 : 8 + SPAN, cs])
        dpar_ref[32:40, cs] += partial8(dconv)
        for k in range(1, 4):
            dxbc = dxbc + par_ref[3 - k : 4 - k, cs] * (fore_masks[k - 1] * dcv[k : k + SPAN, cs])
            dpar_ref[24 - 8 * k : 32 - 8 * k, cs] += partial8(
                dconv * (back_masks[k - 1] * buf[8 - k : 8 - k + SPAN, cs])
            )
        dxr_ref[:, cs] = dxbc.astype(BF16)
    dcv_out[...] = dcv[0:8, :]


def spread_matrices():
    heads = lax.broadcasted_iota(jnp.int32, (LANES, INNER), 0)
    lanes = lax.broadcasted_iota(jnp.int32, (LANES, INNER), 1) // HEADDIM
    one = (heads == lanes).astype(BF16)
    return jnp.concatenate([one, one], axis=0), one.T


def kernel_params(vector, head):
    taps = vector[D + INNER :].reshape(5, CH)
    par = jnp.concatenate([taps, jnp.zeros((3, CH), F32)], axis=0)
    gain = jnp.stack([vector[D : D + INNER], jnp.repeat(head[2], HEADDIM)])
    gain = jnp.concatenate([gain, jnp.zeros((6, INNER), F32)], axis=0)
    hw = jnp.stack([head[0], -jnp.exp(head[1])])
    hw = jnp.pad(hw, ((0, 6), (0, LANES - NHEADS)))
    return par, gain, hw


def whole(shape):
    return pl.BlockSpec(shape, lambda i: (0,) * len(shape))


SMEM = pl.BlockSpec(memory_space=pltpu.SMEM)


def mixer_forward(ends, z, xr, par, gain, hw, spread):
    tokens = z.shape[0]
    blocks = tokens // SPAN
    rows = lambda width: pl.BlockSpec((SPAN, width), lambda i: (i, 0))
    return pl.pallas_call(
        forward_kernel,
        grid=(blocks,),
        in_specs=[SMEM, rows(INNER), rows(XR), whole((8, CH)), whole((8, INNER)), whole((8, LANES)), whole((256, INNER))],
        out_specs=[rows(INNER), rows(INNER), pl.BlockSpec((1, STATE, INNER), lambda i: (i, 0, 0))],
        out_shape=[
            jax.ShapeDtypeStruct((tokens, INNER), BF16),
            jax.ShapeDtypeStruct((tokens, INNER), F32),
            jax.ShapeDtypeStruct((blocks, STATE, INNER), F32),
        ],
        scratch_shapes=[
            pltpu.VMEM((SPAN + 8, CH), F32),
            pltpu.VMEM((SPAN, CH), F32),
            pltpu.VMEM((STATE, INNER), F32),
            pltpu.VMEM((SPAN, INNER), F32),
        ],
        compiler_params=pltpu.CompilerParams(vmem_limit_bytes=VMEM_LIMIT),
        cost_estimate=pl.CostEstimate(flops=20_000_000_000, bytes_accessed=30_000_000, transcendentals=6_000_000),
        name="mixer_forward",
    )(ends, z, xr, par, gain, hw, spread)


def mixer_backward(ends, z, xr, dgn, ys, st, par, gain, hw, spread, gather, first, last, earlier=None):
    tokens = z.shape[0]
    top = last - 1
    back = lambda width: pl.BlockSpec((SPAN, width), lambda i: (top - i, 0))
    halo = pl.BlockSpec((8, XR), lambda i: (jnp.maximum((top - i) * (SPAN // 8) - 1, 0), 0))
    if earlier is None:
        held, carried = [], [jnp.zeros((STATE, INNER), F32), jnp.zeros((8, CH), F32)]
    else:
        held, carried = list(earlier[:2]), list(earlier[5:])
    return pl.pallas_call(
        partial(backward_kernel, top),
        grid=(last - first,),
        in_specs=[
            SMEM,
            back(INNER),
            back(XR),
            halo,
            back(INNER),
            back(INNER),
            pl.BlockSpec((1, STATE, INNER), lambda i: (top - i, 0, 0)),
            whole((8, CH)),
            whole((8, INNER)),
            whole((8, LANES)),
            whole((256, INNER)),
            whole((INNER, LANES)),
        ]
        + [pl.BlockSpec(memory_space=pl.ANY)] * len(held)
        + [whole((STATE, INNER)), whole((8, CH))],
        out_specs=[
            back(INNER),
            back(XR),
            whole((40, CH)),
            whole((16, INNER)),
            whole((16, LANES)),
            whole((STATE, INNER)),
            whole((8, CH)),
        ],
        out_shape=[
            jax.ShapeDtypeStruct((tokens, INNER), BF16),
            jax.ShapeDtypeStruct((tokens, XR), BF16),
            jax.ShapeDtypeStruct((40, CH), F32),
            jax.ShapeDtypeStruct((16, INNER), F32),
            jax.ShapeDtypeStruct((16, LANES), F32),
            jax.ShapeDtypeStruct((STATE, INNER), F32),
            jax.ShapeDtypeStruct((8, CH), F32),
        ],
        input_output_aliases={12 + k: k for k in range(len(held))},
        scratch_shapes=[
            pltpu.VMEM((SPAN + 8, CH), F32),
            pltpu.VMEM((SPAN, CH), F32),
            pltpu.VMEM((SPAN, CH), F32),
            pltpu.VMEM((SPAN, CH), F32),
            pltpu.VMEM((SPAN + 8, CH), F32),
            pltpu.VMEM((SPAN, INNER), F32),
            pltpu.VMEM((SPAN, 2 * SPAN), F32),
        ],
        compiler_params=pltpu.CompilerParams(vmem_limit_bytes=VMEM_LIMIT),
        cost_estimate=pl.CostEstimate(
            flops=7_500_000_000 * (last - first), bytes_accessed=6_000_000 * (last - first), transcendentals=0
        ),
        name="mixer_backward",
    )(ends, z, xr, xr, dgn, ys, st, par, gain, hw, spread, gather, *held, *carried)


def finish_params(dpar, dgain, dhw):
    dtaps = jnp.sum(dpar.reshape(5, 8, CH), axis=1).reshape(5 * CH)
    dgate = jnp.sum(dgain[0:8], axis=0)
    dskip = jnp.sum(dgain[8:16].reshape(8, NHEADS, HEADDIM), axis=(0, 2))
    dh = jnp.sum(dhw.reshape(2, 8, LANES), axis=1)[:, :NHEADS]
    return jnp.concatenate([dgate, dtaps]), jnp.concatenate([dh, dskip[None]], axis=0)


class Net:
    def __init__(self, mesh):
        side = round((mesh.shape["dp"] // 2) ** 0.5)
        self.sizes = {"y": mesh.shape["dp"] // (2 * side), "x": side, "core": 2, "z": mesh.shape["fsdp"]}
        self.order = ("y", "x", "core", "z")

    def coordinates(self):
        at = lax.axis_index("dp")
        return {
            "y": at // (2 * self.sizes["x"]),
            "x": (at // 2) % self.sizes["x"],
            "core": at % 2,
            "z": lax.axis_index("fsdp"),
        }

    def shift(self, value, axis, by):
        n = self.sizes[axis]
        if axis == "z":
            return lax.ppermute(value, "fsdp", [(i, (i + by) % n) for i in range(n)])
        inner = {"y": 2 * self.sizes["x"], "x": 2, "core": 1}[axis]
        pairs = []
        for i in range(2 * self.sizes["y"] * self.sizes["x"]):
            at = (i // inner) % n
            pairs.append((i, i + ((at + by) % n - at) * inner))
        return lax.ppermute(value, "dp", pairs)

    def gather_axis(self, value, axis, at):
        n, dim = self.sizes[axis], self.order.index(axis)
        pieces = [value] + [self.shift(value, axis, d) for d in range(1, n)]
        rows = []
        for j in range(n):
            row = pieces[-j % n]
            for i in range(1, n):
                row = jnp.where(at == i, pieces[(i - j) % n], row)
            rows.append(row)
        return jnp.concatenate(rows, axis=dim)

    def gather(self, shard, axes):
        at = self.coordinates()
        value = shard[None, None, None, None]
        for axis in axes:
            value = self.gather_axis(value, axis, at[axis])
        return value.reshape(-1, shard.shape[1])

    def shift_xy(self, value, dy, dx):
        ny, nx = self.sizes["y"], self.sizes["x"]
        pairs = []
        for y in range(ny):
            for x in range(nx):
                for c in range(2):
                    pairs.append(((y * nx + x) * 2 + c, ((y + dy) % ny * nx + (x + dx) % nx) * 2 + c))
        return lax.ppermute(value, "dp", pairs)

    def steps_xy(self):
        return [(dy, dx) for dy in range(self.sizes["y"]) for dx in range(self.sizes["x"]) if dy or dx]

    def scatter_axis(self, value, axis, at, wire=F32):
        if axis == "xy":
            ny, nx = self.sizes["y"], self.sizes["x"]

            def block(dy, dx):
                row = lax.dynamic_index_in_dim(value, (at["y"] + dy) % ny, 0)
                return lax.dynamic_index_in_dim(row, (at["x"] + dx) % nx, 1)

            total = block(0, 0)
            for dy, dx in self.steps_xy():
                total = total + self.shift_xy(block(dy, dx).astype(wire), dy, dx).astype(F32)
            return total
        n, dim = self.sizes[axis], self.order.index(axis)
        total = lax.dynamic_index_in_dim(value, at[axis], dim)
        for d in range(1, n):
            part = lax.dynamic_index_in_dim(value, (at[axis] + d) % n, dim)
            total = total + self.shift(part.astype(wire), axis, d).astype(F32)
        return total

    def blocks(self, whole):
        s = self.sizes
        return whole.reshape(s["y"], s["x"], s["core"], s["z"], -1, whole.shape[1])

    def total(self, value):
        value = value + self.shift(value, "core", 1)
        value = value + sum(self.shift_xy(value, dy, dx) for dy, dx in self.steps_xy())
        return value + sum(self.shift(value, "z", d) for d in range(1, self.sizes["z"]))


AXES = ("dp", "fsdp")


def rms_norm(values, scales):
    return values * lax.rsqrt(jnp.mean(values * values, axis=-1, keepdims=True) + EPSILON) * scales


def side_by_side(value):
    r = value.shape[-2] // 2
    return jnp.concatenate([value[..., :r, :], value[..., r:, :]], axis=-1)


def norm_part(stream, gain):
    return rms_norm(stream, gain[None, :])


def on_device(
    net,
    hidden_in,
    cotangent,
    seq_lengths,
    in_weight,
    out_weight,
    vector_weight,
    head_weight,
    in_row_moment,
    in_col_moment,
    out_row_moment,
    out_col_moment,
    vector_moment,
    head_moment,
):
    token_count = hidden_in.shape[0]
    lengths = seq_lengths[0]
    e0 = lengths[0]
    e1 = e0 + lengths[1]
    e2 = e1 + lengths[2]
    e3 = e2 + lengths[3]
    ends = jnp.stack([e0, e1, e2, e3])
    valid = (jnp.arange(token_count, dtype=jnp.int32) < e3).astype(F32)
    spread, gather = spread_matrices()
    shard_rows = in_weight.shape[1]
    in_low = jnp.pad(in_weight.astype(BF16), ((0, 0), (0, 0), (0, INNER + XR - P_SIZE)))
    out_low = out_weight.astype(BF16).reshape(LAYERS, 2, shard_rows, D)
    vec_low = vector_weight.astype(BF16).reshape(-1)
    vec_low = jnp.pad(vec_low, (0, shard_rows * LANES - vec_low.shape[0])).reshape(shard_rows, LANES)
    first = net.gather(jnp.concatenate([in_low[0, :, INNER:], vec_low], axis=1), ("z", "x", "y", "core"))
    first_z = net.gather(in_low[0, :, :INNER], ("z", "y", "x", "core"))
    rest = lax.all_gather(
        jnp.concatenate([out_low[0, 0], out_low[0, 1], in_low[1], out_low[1, 0], out_low[1, 1]], axis=1),
        AXES,
        axis=0,
        tiled=True,
    )
    devices = rest.shape[0] // shard_rows

    def out_rows(columns):
        return columns.reshape(devices, shard_rows, 2, D).swapaxes(1, 2).reshape(INNER, D)

    in_from = 2 * D
    out_from = in_from + INNER + XR
    ins = [
        (first_z, first[:, :XR]),
        (rest[:, in_from : in_from + INNER], rest[:, in_from + INNER : out_from]),
    ]
    outs = [out_rows(rest[:, :in_from]), out_rows(rest[:, out_from:])]
    vector_full = first[:, XR:].reshape(devices, -1)[:, : LAYERS * VEC // devices]
    vector_full = vector_full.reshape(devices, LAYERS, -1).swapaxes(0, 1).reshape(LAYERS, VEC).astype(F32)
    stream = hidden_in.astype(F32)
    stored = []
    for l in range(LAYERS):
        tables = kernel_params(vector_full[l], head_weight[l])
        normed, norm_pull = jax.vjp(norm_part, stream, vector_full[l, :D])
        normed = normed.astype(BF16)
        z = jnp.dot(normed, ins[l][0], preferred_element_type=F32)
        xr = jnp.dot(normed, ins[l][1], preferred_element_type=F32)
        gn, ys, st = mixer_forward(ends, z, xr, *tables, spread)
        stream = stream + jnp.dot(gn, outs[l], preferred_element_type=F32)
        stored.append((norm_pull, normed, z, xr, gn, ys, st, tables))
    layer_out = stream.astype(BF16)
    flowing = cotangent.astype(F32) * valid[:, None]
    arrived = [None] * LAYERS
    small_parts = [None] * LAYERS
    travelling = []
    at = net.coordinates()
    blocks = token_count // SPAN
    for l in reversed(range(LAYERS)):
        norm_pull, normed, z, xr, gn, ys, st, tables = stored[l]
        gb = flowing.astype(BF16)
        grad_out = jnp.einsum("te,td->ed", gn, gb, preferred_element_type=F32)
        gb, grad_out = lax.optimization_barrier((gb, grad_out))
        out_sum = side_by_side(net.scatter_axis(net.blocks(grad_out), "core", at))
        travelling = jnp.concatenate(travelling + [out_sum], axis=-1)
        dgn = jnp.einsum("td,ed->te", gb, outs[l], preferred_element_type=F32)
        dgn, travelling = lax.optimization_barrier((dgn, travelling))
        travelling = net.scatter_axis(travelling, "xy", at, BF16)
        dz, dxr, *sums = mixer_backward(ends, z, xr, dgn, ys, st, *tables, spread, gather, 0, blocks)[:5]
        dz, dxr, travelling = lax.optimization_barrier((dz, dxr, travelling))
        arrived[l] = net.scatter_axis(travelling, "z", at, BF16)
        grad_x = jnp.einsum("td,tp->dp", normed, dxr, preferred_element_type=F32)
        dz, dxr, grad_x = lax.optimization_barrier((dz, dxr, grad_x))
        grad_z = jnp.einsum("td,tp->dp", normed, dz, preferred_element_type=F32)
        dz, dxr, grad_z = lax.optimization_barrier((dz, dxr, grad_z))
        travelling = [net.scatter_axis(net.blocks(g), "core", at) for g in (grad_x, grad_z)]
        dxn = jnp.einsum("tp,dp->td", dz, ins[l][0], preferred_element_type=F32) + jnp.einsum(
            "tp,dp->td", dxr, ins[l][1], preferred_element_type=F32
        )
        grad_stream, dnorm = norm_pull(dxn)
        flowing = flowing + grad_stream
        dvec, dhead = finish_params(*sums)
        small_parts[l] = jnp.concatenate([dnorm, dvec, dhead.reshape(-1)])
    travelling_late = travelling
    for axis in ("xy", "z"):
        travelling = [net.scatter_axis(v, axis, at, BF16) for v in travelling]
    flat = [v.reshape(-1, v.shape[-1]) for v in (arrived[1], arrived[0], *travelling)]
    in_parts = [
        jnp.concatenate([flat[3], flat[2]], axis=1)[:, :P_SIZE],
        jnp.concatenate([flat[1][:, XR : XR + INNER], flat[1][:, :XR]], axis=1)[:, :P_SIZE],
    ]
    out_parts = [
        jnp.concatenate([v[:, -2 * D : -D], v[:, -D:]], axis=0) for v in (flat[1], flat[0])
    ]
    late, _ = lax.optimization_barrier(((in_weight, out_weight, vector_weight), travelling_late))
    weight_squares = [jnp.sum(w * w, axis=tuple(range(1, w.ndim))) for w in late]
    small = jnp.stack(small_parts)
    small = net.total(jnp.pad(small, ((0, 0), (0, -small.shape[1] % LANES))).reshape(-1, LANES))
    small = small.reshape(LAYERS, -1)
    head_total = small[:, VEC : VEC + 3 * NHEADS].reshape(LAYERS, 3, NHEADS)
    share = VEC // devices
    mine = lax.axis_index("dp") * lax.axis_size("fsdp") + lax.axis_index("fsdp")
    grad_vector = lax.dynamic_slice(small, (0, mine * share), (LAYERS, share))
    grad_in = jnp.stack(in_parts)
    grad_out = jnp.stack(out_parts)
    squares_in = grad_in * grad_in
    squares_out = grad_out * grad_out
    row_in = MOMENT_DECAY * in_row_moment + (1.0 - MOMENT_DECAY) * jnp.mean(squares_in, axis=2)
    row_out = MOMENT_DECAY * out_row_moment + (1.0 - MOMENT_DECAY) * jnp.mean(squares_out, axis=2)
    vector_new = MOMENT_DECAY * vector_moment + (1.0 - MOMENT_DECAY) * grad_vector * grad_vector
    vector_update = grad_vector * lax.rsqrt(vector_new)
    totals = jnp.stack(
        [
            jnp.sum(row_in, axis=1),
            jnp.sum(row_out, axis=1),
            *weight_squares,
            jnp.sum(vector_update * vector_update, axis=1),
        ],
        axis=1,
    )
    local = (
        jnp.sum(squares_in, axis=1),
        jnp.sum(squares_out, axis=1),
        jnp.sum(squares_in / row_in[:, :, None], axis=1),
        jnp.sum(squares_out / row_out[:, :, None], axis=1),
        totals,
    )
    edges = [0]
    for v in local:
        edges.append(edges[-1] + v.shape[1])
    summed = jnp.concatenate(local, axis=1)
    summed = jnp.pad(summed, ((0, 0), (0, -edges[-1] % LANES))).reshape(-1, LANES)
    summed = net.total(summed).reshape(LAYERS, -1)
    column_in, column_out, scaled_in, scaled_out, totals = [
        summed[:, a:b] for a, b in zip(edges[:-1], edges[1:])
    ]
    col_in = MOMENT_DECAY * in_col_moment + (1.0 - MOMENT_DECAY) * column_in / D
    col_out = MOMENT_DECAY * out_col_moment + (1.0 - MOMENT_DECAY) * column_out / INNER
    mean_in = totals[:, 0] / D
    mean_out = totals[:, 1] / INNER
    norm_in = jnp.sqrt(mean_in * jnp.sum(scaled_in / col_in, axis=1) / (D * P_SIZE))
    norm_out = jnp.sqrt(mean_out * jnp.sum(scaled_out / col_out, axis=1) / (INNER * D))
    norm_vector = jnp.sqrt(totals[:, 5] / VEC)
    head_new = MOMENT_DECAY * head_moment + (1.0 - MOMENT_DECAY) * head_total * head_total
    head_update = head_total * lax.rsqrt(head_new)
    norm_head = jnp.sqrt(jnp.mean(head_update * head_update, axis=(1, 2)))

    def step_of(square_mean, norm):
        return RELATIVE_STEP * jnp.sqrt(square_mean) / jnp.maximum(1.0, norm / CLIP_LIMIT)

    step_in = step_of(totals[:, 2] / (D * P_SIZE), norm_in)
    step_out = step_of(totals[:, 3] / (INNER * D), norm_out)
    step_vector = step_of(totals[:, 4] / VEC, norm_vector)
    step_head = step_of(jnp.mean(head_weight * head_weight, axis=(1, 2)), norm_head)
    update_in = grad_in * lax.rsqrt(row_in[:, :, None] * col_in[:, None, :] / mean_in[:, None, None])
    update_out = grad_out * lax.rsqrt(row_out[:, :, None] * col_out[:, None, :] / mean_out[:, None, None])
    new_in = in_weight - step_in[:, None, None] * update_in
    new_out = out_weight - step_out[:, None, None] * update_out
    new_vector = vector_weight - step_vector[:, None] * vector_update
    new_head = head_weight - step_head[:, None, None] * head_update
    update_rms = jnp.stack([norm_in, norm_out, norm_vector, norm_head], axis=1)
    return (
        layer_out,
        flowing,
        grad_in,
        grad_out,
        grad_vector,
        head_total,
        new_in,
        new_out,
        new_vector,
        new_head,
        new_in.astype(BF16),
        new_out.astype(BF16),
        new_vector.astype(BF16),
        new_head.astype(BF16),
        row_in,
        col_in,
        row_out,
        col_out,
        vector_new,
        head_new,
        update_rms,
    )


def solution(mesh):
    rows = P(AXES, None)
    mat = P(None, AXES, None)
    vec = P(None, AXES)
    one = P()
    return jax.shard_map(
        partial(on_device, Net(mesh)),
        mesh=mesh,
        in_specs=(rows, rows, rows, mat, mat, vec, one, vec, one, vec, one, vec, one),
        out_specs=(
            rows, rows, mat, mat, vec, one, mat, mat, vec, one, mat, mat, vec, one, vec, one, vec, one, vec, one, one,
        ),
        check_vma=False,
    )
```

```python
from functools import partial

import jax
import jax.numpy as jnp
import ml_dtypes
import numpy as np
from jax import lax
from jax.experimental import pallas as pl
from jax.experimental.pallas import tpu as pltpu
from jax.sharding import PartitionSpec as P

D = 768
NHEADS = 24
HEADDIM = 64
STATE = 128
LAYERS = 2
INNER = 1536
CH = 1792
P_SIZE = 3352
XR = 1920
VEC = 11264

EPSILON = 1e-05
MOMENT_DECAY = 0.5
CLIP_LIMIT = 1.0
RELATIVE_STEP = 0.5

SPAN = 128
GROUP = 256
GATE_ROWS = 64
GATE_BLOCK = 256
NORM_BLOCK = 256
GROUPS = INNER // GROUP
LANES = 128
LOG2E = 1.4426950408889634
VMEM_LIMIT = 60 * 1024 * 1024
F32 = jnp.float32
BF16 = jnp.bfloat16
NN = ((1,), (0,))
NT = ((1,), (1,))
TN = ((0,), (0,))

PASS_PAIR = 3
PASS_STATE = 3
PASS_RED = 2


def halves(v):
    high = v.astype(BF16)
    return high, (v - high.astype(F32)).astype(BF16)


def raw_dot(a, b, dims):
    return lax.dot_general(a, b, (dims, ((), ())), preferred_element_type=F32)


def mm(a, b, dims, passes, pack=None):
    if passes == 1:
        return raw_dot(a.astype(BF16), b.astype(BF16), dims)
    a_hi, a_lo = halves(a)
    b_hi, b_lo = halves(b)
    if pack == "k":
        left = jnp.concatenate([a_hi, a_lo], axis=dims[0][0])
        right = jnp.concatenate([b_hi, b_hi], axis=dims[1][0])
        return raw_dot(left, right, dims) + raw_dot(a_hi, b_lo, dims)
    if pack == "n":
        both = raw_dot(a_hi, jnp.concatenate([b_hi, b_lo], axis=1 - dims[1][0]), dims)
        half = both.shape[1] // 2
        return both[:, :half] + (both[:, half:] + raw_dot(a_lo, b_hi, dims))
    return raw_dot(a_hi, b_hi, dims) + (raw_dot(a_lo, b_hi, dims) + raw_dot(a_hi, b_lo, dims))


def exact_left(a01, b):
    hi, lo = halves(b)
    rest = (b - hi.astype(F32) - lo.astype(F32)).astype(BF16)
    return raw_dot(a01, hi, NN) + (raw_dot(a01, lo, NN) + raw_dot(a01, rest, NN))


def reduce_right(a, b01, passes):
    if passes == 1:
        return raw_dot(a.astype(BF16), b01, NN)
    hi, lo = halves(a)
    return raw_dot(hi, b01, NN) + raw_dot(lo, b01, NN)


def sigmoid(v):
    return 0.5 * jnp.tanh(0.5 * v) + 0.5


def partial8(v):
    return jnp.sum(v.reshape(v.shape[0] // 8, 8, v.shape[1]), axis=0)


def segment_of(place, ends_ref):
    total = (place >= ends_ref[0]).astype(jnp.int32)
    for k in range(1, 4):
        total = total + (place >= ends_ref[k]).astype(jnp.int32)
    return total


def scalar_segment(place, ends_ref):
    total = jnp.int32(0)
    for k in range(4):
        total = total + jnp.where(place >= ends_ref[k], 1, 0).astype(jnp.int32)
    return total


def block_terms(base, ends_ref, hw_ref, rate_in):
    shape = (SPAN, LANES)
    place = base + lax.broadcasted_iota(jnp.int32, shape, 0)
    seg = segment_of(place, ends_ref)
    first_seg = jnp.where(base > 0, scalar_segment(base - 1, ends_ref), -1)
    last_seg = scalar_segment(base + SPAN - 1, ends_ref)
    pre = rate_in + hw_ref[0:1, :]
    head_ok = lax.broadcasted_iota(jnp.int32, shape, 1) < NHEADS
    steps = jnp.where(head_ok, jnp.maximum(pre, 0.0) + jnp.log1p(jnp.exp(-jnp.abs(pre))), 0.0)
    log_rate = hw_ref[1:2, :] * steps
    rows = lax.broadcasted_iota(jnp.int32, (SPAN, SPAN), 0)
    cols = lax.broadcasted_iota(jnp.int32, (SPAN, SPAN), 1)
    lower = jnp.where(rows >= cols, 1.0, 0.0)
    cum = exact_left(lower.astype(BF16), log_rate * LOG2E)
    reach = jnp.where(seg == first_seg, jnp.exp2(cum), 0.0)
    to_end = jnp.where(seg == last_seg, jnp.exp2(cum[SPAN - 1 : SPAN, :] - cum), 0.0)
    seg_row = segment_of(base + cols, ends_ref)
    seg_col = segment_of(base + rows, ends_ref)
    same = seg_row == seg_col
    return place, seg, pre, steps, log_rate, cum, reach, to_end, rows, cols, same


def lag_mask(place, seg, ends_ref, lag):
    other = place + lag
    ok = (segment_of(other, ends_ref) == seg) & (other >= 0)
    return jnp.where(ok, 1.0, 0.0)


def two_parts(v):
    hi, lo = halves(v)
    return jnp.concatenate([hi, lo], axis=1)


def lane_split(v):
    first = lax.broadcasted_iota(jnp.int32, v.shape, 1) < HEADDIM
    return jnp.concatenate([jnp.where(first, v, 0.0), jnp.where(first, 0.0, v)], axis=0)


def pair_columns(cum, head):
    one = jnp.broadcast_to(cum[:, head : head + 1], (SPAN, SPAN))
    two = jnp.broadcast_to(cum[:, head + 1 : head + 2], (SPAN, SPAN))
    return jnp.concatenate([one, two], axis=1)


def pair_rows(cum_t, head):
    return jnp.concatenate([cum_t[head : head + 1, :], cum_t[head + 1 : head + 2, :]], axis=1)


def gate_rows(z_ref, ys_ref, gain_ref, gn_ref, yg):
    for r in range(ys_ref.shape[0] // GATE_ROWS):
        rs = slice(GATE_ROWS * r, GATE_ROWS * (r + 1))
        squares = jnp.zeros((GATE_ROWS, LANES), F32)
        for c in range(INNER // LANES):
            cs = slice(LANES * c, LANES * (c + 1))
            z = z_ref[rs, cs]
            gated = ys_ref[rs, cs] * (z * sigmoid(z))
            yg[rs, cs] = gated
            squares = squares + gated * gated
        scale = lax.rsqrt(jnp.sum(squares, axis=1, keepdims=True) / INNER + EPSILON)
        scale = jnp.broadcast_to(scale, (GATE_ROWS, LANES))
        for c in range(INNER // LANES):
            cs = slice(LANES * c, LANES * (c + 1))
            gn_ref[rs, cs] = (yg[rs, cs] * scale * gain_ref[0:1, cs]).astype(BF16)


def forward_kernel(gated, ends_ref, xr_ref, par_ref, gain_ref, hw_ref, spread_ref, *refs):
    if gated:
        z_ref, gn_ref, *refs = refs
    ys_ref, st_ref, buf, act, state, *yg = refs
    block = pl.program_id(0)
    base = block * SPAN

    @pl.when(block == 0)
    def _():
        buf[0:8, :] = jnp.zeros((8, CH), F32)
        state[...] = jnp.zeros_like(state)

    place, seg, pre, steps, log_rate, cum, reach, to_end, rows, cols, same = block_terms(
        base, ends_ref, hw_ref, xr_ref[:, CH:XR]
    )
    masks = [lag_mask(place, seg, ends_ref, -k) for k in range(1, 4)]
    for c in range(CH // LANES):
        cs = slice(LANES * c, LANES * (c + 1))
        now = xr_ref[:, cs]
        buf[8 : 8 + SPAN, cs] = now
        conv = par_ref[4:5, cs] + par_ref[3:4, cs] * now
        for k in range(1, 4):
            conv = conv + par_ref[3 - k : 4 - k, cs] * (masks[k - 1] * buf[8 - k : 8 - k + SPAN, cs])
        buf[0:8, cs] = now[SPAN - 8 : SPAN, :]
        act[:, cs] = conv * sigmoid(conv)
    bm = act[:, INNER : INNER + STATE]
    cm = act[:, INNER + STATE : CH]
    gram = mm(cm, bm, NT, 3)
    gram2 = jnp.concatenate([gram, gram], axis=1)
    bias = jnp.where(same & (rows >= cols), 0.0, -1e30)
    bias2 = jnp.concatenate([bias, bias], axis=1)
    cum_t = cum.T
    bm_t = bm.T
    steps2, reach2, to_end2 = two_parts(steps), two_parts(reach), two_parts(to_end)
    st_ref[0] = state[...]
    for g in range(GROUPS):
        gs = slice(GROUP * g, GROUP * (g + 1))
        spread = spread_ref[:, gs]
        x = act[:, gs]
        xd = x * raw_dot(steps2, spread, NN)
        within = []
        for q in range(2):
            head = 4 * g + 2 * q
            mix = jnp.exp2(pair_columns(cum, head) - pair_rows(cum_t, head) + bias2) * gram2
            within.append(mm(mix, lane_split(xd[:, LANES * q : LANES * (q + 1)]), NN, PASS_PAIR, "n"))
        reach_g = raw_dot(reach2, spread, NN)
        before = state[:, gs]
        scan = jnp.concatenate(within, axis=1) + mm(cm, before, NN, PASS_STATE, "k") * reach_g
        ys_ref[:, gs] = scan + gain_ref[1:2, gs] * x
        state[:, gs] = before * reach_g[SPAN - 1 : SPAN, :] + mm(
            bm_t, xd * raw_dot(to_end2, spread, NN), NN, PASS_STATE, "k"
        )
    if gated:
        gate_rows(z_ref, ys_ref, gain_ref, gn_ref, yg[0])


def gate_back_rows(z_ref, ys_ref, dgn_ref, gain_ref, dz_ref, dy_ref, dgain_ref, yg):
    for r in range(z_ref.shape[0] // GATE_ROWS):
        rs = slice(GATE_ROWS * r, GATE_ROWS * (r + 1))
        squares = jnp.zeros((GATE_ROWS, LANES), F32)
        overlap = jnp.zeros((GATE_ROWS, LANES), F32)
        for c in range(INNER // LANES):
            cs = slice(LANES * c, LANES * (c + 1))
            z = z_ref[rs, cs]
            gated = ys_ref[rs, cs] * (z * sigmoid(z))
            yg[rs, cs] = gated
            overlap = overlap + gated * (dgn_ref[rs, cs] * gain_ref[0:1, cs])
            squares = squares + gated * gated
        scale = lax.rsqrt(jnp.sum(squares, axis=1, keepdims=True) / INNER + EPSILON)
        pull = jnp.sum(overlap, axis=1, keepdims=True) * (scale * scale * scale) / INNER
        scale = jnp.broadcast_to(scale, (GATE_ROWS, LANES))
        pull = jnp.broadcast_to(pull, (GATE_ROWS, LANES))
        for c in range(INNER // LANES):
            cs = slice(LANES * c, LANES * (c + 1))
            z = z_ref[rs, cs]
            gate = sigmoid(z)
            gated = yg[rs, cs]
            dgn = dgn_ref[rs, cs] * scale
            dgain_ref[:, cs] += partial8(dgn * gated)
            dgated = dgn * gain_ref[0:1, cs] - gated * pull
            dy_ref[rs, cs] = dgated * (z * gate)
            dz_ref[rs, cs] = (dgated * ys_ref[rs, cs] * (gate * (1.0 + z * (1.0 - gate)))).astype(BF16)


def gate_back_kernel(z_ref, ys_ref, dgn_ref, gain_ref, dz_ref, dy_ref, dgain_ref, yg):
    @pl.when(pl.program_id(0) == 0)
    def _():
        dgain_ref[...] = jnp.zeros_like(dgain_ref)

    gate_back_rows(z_ref, ys_ref, dgn_ref, gain_ref, dz_ref, dy_ref, dgain_ref, yg)


def gate_forward(z, ys, gain):
    tokens = z.shape[0]
    rows = pl.BlockSpec((GATE_BLOCK, INNER), lambda i: (i, 0))
    return pl.pallas_call(
        gate_rows,
        grid=(tokens // GATE_BLOCK,),
        in_specs=[rows, rows, whole((8, INNER))],
        out_specs=rows,
        out_shape=jax.ShapeDtypeStruct((tokens, INNER), BF16),
        scratch_shapes=[pltpu.VMEM((GATE_BLOCK, INNER), F32)],
        compiler_params=pltpu.CompilerParams(vmem_limit_bytes=VMEM_LIMIT),
        cost_estimate=pl.CostEstimate(flops=20_000_000, bytes_accessed=20_000_000, transcendentals=0),
        name="gate_forward",
    )(z, ys, gain)


def gate_backward(z, ys, dgn, gain):
    tokens = z.shape[0]
    rows = pl.BlockSpec((GATE_BLOCK, INNER), lambda i: (i, 0))
    return pl.pallas_call(
        gate_back_kernel,
        grid=(tokens // GATE_BLOCK,),
        in_specs=[rows, rows, rows, whole((8, INNER))],
        out_specs=[rows, rows, whole((8, INNER))],
        out_shape=[
            jax.ShapeDtypeStruct((tokens, INNER), BF16),
            jax.ShapeDtypeStruct((tokens, INNER), F32),
            jax.ShapeDtypeStruct((8, INNER), F32),
        ],
        scratch_shapes=[pltpu.VMEM((GATE_BLOCK, INNER), F32)],
        compiler_params=pltpu.CompilerParams(vmem_limit_bytes=VMEM_LIMIT),
        cost_estimate=pl.CostEstimate(flops=60_000_000, bytes_accessed=30_000_000, transcendentals=0),
        name="gate_backward",
    )(z, ys, dgn, gain)


def backward_kernel(
    top, fused, ends_ref, xr_ref, halo_ref, ys_ref, st_ref, par_ref, gain_ref, hw_ref, spread_ref, gather_ref, *refs
):
    if fused:
        z_ref, dgn_ref, *refs = refs
        *refs, dz_ref, dgate_ref, dy_ref, yg = refs
    else:
        dy_ref, *refs = refs
    (
        rgrad_in, dcv_in, dxr_ref, dpar_ref, dskip_ref, dhw_ref, rgrad, dcv_out,
        buf, act, slope, dact, dcv, dgram,
    ) = refs[-14:]
    step = pl.program_id(0)
    block = top - step
    base = block * SPAN

    @pl.when(step == 0)
    def _():
        dcv[0:8, :] = dcv_in[...]
        rgrad[...] = rgrad_in[...]
        dpar_ref[...] = jnp.zeros_like(dpar_ref)
        dskip_ref[...] = jnp.zeros_like(dskip_ref)
        dhw_ref[...] = jnp.zeros_like(dhw_ref)
        if fused:
            dgate_ref[...] = jnp.zeros_like(dgate_ref)

    if fused:
        gate_back_rows(z_ref, ys_ref, dgn_ref, gain_ref, dz_ref, dy_ref, dgate_ref, yg)
    place, seg, pre, steps, log_rate, cum, reach, to_end, rows, cols, same = block_terms(
        base, ends_ref, hw_ref, xr_ref[:, CH:XR]
    )
    back_masks = [lag_mask(place, seg, ends_ref, -k) for k in range(1, 4)]
    fore_masks = [lag_mask(place, seg, ends_ref, k) for k in range(1, 4)]
    for c in range(CH // LANES):
        cs = slice(LANES * c, LANES * (c + 1))
        now = xr_ref[:, cs]
        buf[0:8, cs] = halo_ref[:, cs]
        buf[8 : 8 + SPAN, cs] = now
        conv = par_ref[4:5, cs] + par_ref[3:4, cs] * now
        for k in range(1, 4):
            conv = conv + par_ref[3 - k : 4 - k, cs] * (back_masks[k - 1] * buf[8 - k : 8 - k + SPAN, cs])
        gate = sigmoid(conv)
        act[:, cs] = conv * gate
        slope[:, cs] = gate * (1.0 + conv * (1.0 - gate))
        dcv[SPAN : SPAN + 8, cs] = dcv[0:8, cs]
    bm = act[:, INNER : INNER + STATE]
    cm = act[:, INNER + STATE : CH]
    gram_t = mm(cm, bm, NT, 3).T
    gram2 = jnp.concatenate([gram_t, gram_t], axis=1)
    bias = jnp.where(same & (rows <= cols), 0.0, -1e30)
    bias2 = jnp.concatenate([bias, bias], axis=1)
    cum_t = cum.T
    cm_t = cm.T
    steps2, reach2, to_end2 = two_parts(steps), two_parts(reach), two_parts(to_end)

    dgram[...] = jnp.zeros_like(dgram)
    dbm = jnp.zeros((SPAN, STATE), F32)
    dcm = jnp.zeros((SPAN, STATE), F32)
    red_rate = jnp.zeros((SPAN, LANES), F32)
    red_tail = jnp.zeros((SPAN, LANES), F32)
    red_step = jnp.zeros((SPAN, LANES), F32)
    red_through = jnp.zeros((8, LANES), F32)
    for g in range(GROUPS):
        gs = slice(GROUP * g, GROUP * (g + 1))
        spread = spread_ref[:, gs]
        gather = gather_ref[gs, :]
        x = act[:, gs]
        skip = gain_ref[1:2, gs]
        dy = dy_ref[:, gs]
        dskip_ref[:, gs] += partial8(dy * x)
        steps_g = raw_dot(steps2, spread, NN)
        reach_g = raw_dot(reach2, spread, NN)
        to_end_g = raw_dot(to_end2, spread, NN)
        xd = x * steps_g
        dxd_in = []
        for q in range(2):
            head = 4 * g + 2 * q
            qs = slice(LANES * q, LANES * (q + 1))
            decay = jnp.exp2(pair_rows(cum_t, head) - pair_columns(cum, head) + bias2)
            dy_two = lane_split(dy[:, qs])
            dxd_in.append(mm(decay * gram2, dy_two, NN, PASS_PAIR, "n"))
            dgram[...] += decay * mm(xd[:, qs], dy_two, NT, PASS_PAIR)
        dxd_in = jnp.concatenate(dxd_in, axis=1)
        later = rgrad[:, gs]
        before = st_ref[0, :, gs]
        dxd_out = mm(bm, later, NN, PASS_STATE) * to_end_g
        dbm = dbm + mm(xd * to_end_g, later, NT, PASS_STATE, "n")
        dy_reach = dy * reach_g
        dcm = dcm + mm(dy_reach, before, NT, PASS_STATE, "n")
        fade = reach_g[SPAN - 1 : SPAN, :]
        red_through = red_through + reduce_right(partial8(before * later) * fade, gather, 2)
        rgrad[:, gs] = later * fade + mm(cm_t, dy_reach, NN, PASS_STATE)
        if PASS_PAIR == 1:
            dy_seen, xd_seen = dy.astype(BF16).astype(F32), xd.astype(BF16).astype(F32)
        else:
            dy_seen, xd_seen = dy, xd
        dxd = dxd_in + dxd_out
        red_rate = red_rate + reduce_right(dy_seen * (ys_ref[:, gs] - skip * x) - xd_seen * dxd_in, gather, 2)
        red_tail = red_tail + reduce_right(x * dxd_out, gather, PASS_RED)
        red_step = red_step + reduce_right(x * dxd, gather, PASS_RED)
        dact[:, gs] = skip * dy + steps_g * dxd
    dgram_t = dgram[:, :SPAN] + dgram[:, SPAN:]
    dact[:, INNER : INNER + STATE] = dbm + mm(dgram_t, cm, NN, 3)
    dact[:, INNER + STATE : CH] = dcm + mm(dgram_t.T, bm, NN, 3)

    upper = jnp.where(rows <= cols, 1.0, 0.0).astype(BF16)
    strict = jnp.where(rows > cols, 1.0, 0.0).astype(BF16)
    through = jnp.sum(red_through, axis=0, keepdims=True)
    drate = exact_left(upper, red_rate) + exact_left(strict, steps * red_tail) + through
    dsteps = red_step + drate * hw_ref[1:2, :]
    dpre = dsteps * sigmoid(pre)
    dhw_ref[0:8, :] += partial8(dpre)
    dhw_ref[8:16, :] += partial8(drate * log_rate)
    dxr_ref[:, CH:XR] = dpre.astype(BF16)

    for c in range(CH // LANES):
        cs = slice(LANES * c, LANES * (c + 1))
        now = xr_ref[:, cs]
        dconv = dact[:, cs] * slope[:, cs]
        dcv[0:SPAN, cs] = dconv
        dxbc = par_ref[3:4, cs] * dconv
        dpar_ref[24:32, cs] += partial8(dconv * now)
        dpar_ref[32:40, cs] += partial8(dconv)
        for k in range(1, 4):
            ahead = fore_masks[k - 1] * dcv[k : k + SPAN, cs]
            dxbc = dxbc + par_ref[3 - k : 4 - k, cs] * ahead
            dpar_ref[24 - 8 * k : 32 - 8 * k, cs] += partial8(ahead * now)
        dxr_ref[:, cs] = dxbc.astype(BF16)
    dcv_out[...] = dcv[0:8, :]


def spread_matrices():
    one = (np.arange(LANES)[:, None] == np.arange(INNER)[None, :] // HEADDIM).astype(ml_dtypes.bfloat16)
    return jnp.asarray(np.concatenate([one, one], axis=0)), jnp.asarray(one.T)


def kernel_params(vector, head):
    taps = vector[D + INNER :].reshape(5, CH)
    par = jnp.concatenate([taps, jnp.zeros((3, CH), F32)], axis=0)
    gain = jnp.stack([vector[D : D + INNER], jnp.repeat(head[2], HEADDIM)])
    gain = jnp.concatenate([gain, jnp.zeros((6, INNER), F32)], axis=0)
    hw = jnp.stack([head[0], -jnp.exp(head[1])])
    hw = jnp.pad(hw, ((0, 6), (0, LANES - NHEADS)))
    return par, gain, hw


def whole(shape):
    return pl.BlockSpec(shape, lambda i: (0,) * len(shape))


SMEM = pl.BlockSpec(memory_space=pltpu.SMEM)


def mixer_forward(ends, xr, par, gain, hw, spread, z=None):
    tokens = xr.shape[0]
    blocks = tokens // SPAN
    rows = lambda width: pl.BlockSpec((SPAN, width), lambda i: (i, 0))
    in_specs = [SMEM, rows(XR), whole((8, CH)), whole((8, INNER)), whole((8, LANES)), whole((256, INNER))]
    out_specs = [rows(INNER), pl.BlockSpec((1, STATE, INNER), lambda i: (i, 0, 0))]
    out_shape = [
        jax.ShapeDtypeStruct((tokens, INNER), F32),
        jax.ShapeDtypeStruct((blocks, STATE, INNER), F32),
    ]
    scratch = [
        pltpu.VMEM((SPAN + 8, CH), F32),
        pltpu.VMEM((SPAN, CH), F32),
        pltpu.VMEM((STATE, INNER), F32),
    ]
    more = []
    if z is not None:
        more = [z]
        in_specs.append(rows(INNER))
        out_specs.insert(0, rows(INNER))
        out_shape.insert(0, jax.ShapeDtypeStruct((tokens, INNER), BF16))
        scratch.append(pltpu.VMEM((SPAN, INNER), F32))
    return pl.pallas_call(
        partial(forward_kernel, z is not None),
        grid=(blocks,),
        in_specs=in_specs,
        out_specs=out_specs,
        out_shape=out_shape,
        scratch_shapes=scratch,
        compiler_params=pltpu.CompilerParams(vmem_limit_bytes=VMEM_LIMIT),
        cost_estimate=pl.CostEstimate(flops=30_000_000_000, bytes_accessed=30_000_000, transcendentals=0),
        name="mixer_forward",
    )(ends, xr, par, gain, hw, spread, *more)


def mixer_backward(ends, xr, ys, st, par, gain, hw, spread, gather, grads, first, last, earlier=None):
    tokens = xr.shape[0]
    top = last - 1
    fused = len(grads) == 2
    back = lambda width: pl.BlockSpec((SPAN, width), lambda i: (top - i, 0))
    halo = pl.BlockSpec((8, XR), lambda i: (jnp.maximum((top - i) * (SPAN // 8) - 1, 0), 0))
    if earlier is None:
        held, carried = [], [jnp.zeros((STATE, INNER), F32), jnp.zeros((8, CH), F32)]
    else:
        held, carried = list(earlier[:1]), list(earlier[4:6])
    in_specs = [
        SMEM,
        back(XR),
        halo,
        back(INNER),
        pl.BlockSpec((1, STATE, INNER), lambda i: (top - i, 0, 0)),
        whole((8, CH)),
        whole((8, INNER)),
        whole((8, LANES)),
        whole((256, INNER)),
        whole((INNER, LANES)),
    ]
    in_specs += [back(INNER)] * len(grads)
    held_at = len(in_specs)
    in_specs += [pl.BlockSpec(memory_space=pl.ANY)] * len(held)
    in_specs += [whole((STATE, INNER)), whole((8, CH))]
    outs = [
        (back(XR), (tokens, XR), BF16),
        (whole((40, CH)), (40, CH), F32),
        (whole((8, INNER)), (8, INNER), F32),
        (whole((16, LANES)), (16, LANES), F32),
        (whole((STATE, INNER)), (STATE, INNER), F32),
        (whole((8, CH)), (8, CH), F32),
    ]
    scratch = [
        pltpu.VMEM((SPAN + 8, CH), F32),
        pltpu.VMEM((SPAN, CH), F32),
        pltpu.VMEM((SPAN, CH), F32),
        pltpu.VMEM((SPAN, CH), F32),
        pltpu.VMEM((SPAN + 8, CH), F32),
        pltpu.VMEM((SPAN, 2 * SPAN), F32),
    ]
    if fused:
        outs += [(back(INNER), (tokens, INNER), BF16), (whole((8, INNER)), (8, INNER), F32)]
        scratch += [pltpu.VMEM((SPAN, INNER), F32)] * 2
    kernel = partial(backward_kernel, top, fused)
    if fused:
        def kernel(*refs):
            plain, (dz_ref, dgate_ref), used, last_two = refs[: -10], refs[-10:-8], refs[-8:-2], refs[-2:]
            backward_kernel(top, fused, *plain, *used, dz_ref, dgate_ref, *last_two)

    return pl.pallas_call(
        kernel,
        grid=(last - first,),
        in_specs=in_specs,
        out_specs=[o[0] for o in outs],
        out_shape=[jax.ShapeDtypeStruct(o[1], o[2]) for o in outs],
        input_output_aliases={held_at + k: k for k in range(len(held))},
        scratch_shapes=scratch,
        compiler_params=pltpu.CompilerParams(vmem_limit_bytes=VMEM_LIMIT),
        cost_estimate=pl.CostEstimate(
            flops=7_000_000_000 * (last - first), bytes_accessed=5_000_000 * (last - first), transcendentals=0
        ),
        name="mixer_backward",
    )(ends, xr, xr, ys, st, par, gain, hw, spread, gather, *grads, *held, *carried)


def norm_back_kernel(dz_ref, dxr_ref, wz_ref, wx_ref, h_ref, flow_ref, gain_ref, out_ref, dgain_ref):
    @pl.when(pl.program_id(0) == 0)
    def _():
        dgain_ref[...] = jnp.zeros_like(dgain_ref)

    dxn = raw_dot(dz_ref[...], wz_ref[...], NT) + raw_dot(dxr_ref[...], wx_ref[...], NT)
    h = h_ref[...].astype(F32)
    scale = lax.rsqrt(jnp.sum(h * h, axis=1, keepdims=True) / D + EPSILON)
    scaled = dxn * gain_ref[0:1, :]
    pull = jnp.sum(scaled * h, axis=1, keepdims=True) * (scale * scale * scale) / D
    out_ref[...] = flow_ref[...] + (scale * scaled - h * pull)
    dgain_ref[...] += partial8(dxn * (h * scale))


def norm_backward(dz, dxr, wz, wx, h, flowing, gain):
    tokens = dz.shape[0]
    rows = lambda width: pl.BlockSpec((NORM_BLOCK, width), lambda i: (i, 0))
    return pl.pallas_call(
        norm_back_kernel,
        grid=(tokens // NORM_BLOCK,),
        in_specs=[rows(INNER), rows(XR), whole((D, INNER)), whole((D, XR)), rows(D), rows(D), whole((8, D))],
        out_specs=[rows(D), whole((8, D))],
        out_shape=[jax.ShapeDtypeStruct((tokens, D), F32), jax.ShapeDtypeStruct((8, D), F32)],
        compiler_params=pltpu.CompilerParams(vmem_limit_bytes=VMEM_LIMIT),
        cost_estimate=pl.CostEstimate(flops=1_000_000, bytes_accessed=1_000_000, transcendentals=0),
        name="norm_backward",
    )(dz, dxr, wz, wx, h, flowing, gain)


def finish_params(dgate, dpar, dskip, dhw):
    dtaps = jnp.sum(dpar.reshape(5, 8, CH), axis=1).reshape(5 * CH)
    dgate = jnp.sum(dgate, axis=0)
    dskip = jnp.sum(dskip.reshape(8, NHEADS, HEADDIM), axis=(0, 2))
    dh = jnp.sum(dhw.reshape(2, 8, LANES), axis=1)[:, :NHEADS]
    return jnp.concatenate([dgate, dtaps]), jnp.concatenate([dh, dskip[None]], axis=0)


class Net:
    def __init__(self, mesh):
        side = round((mesh.shape["dp"] // 2) ** 0.5)
        self.sizes = {"y": mesh.shape["dp"] // (2 * side), "x": side, "core": 2, "z": mesh.shape["fsdp"]}
        self.order = ("y", "x", "core", "z")

    def coordinates(self):
        at = lax.axis_index("dp")
        return {
            "y": at // (2 * self.sizes["x"]),
            "x": (at // 2) % self.sizes["x"],
            "core": at % 2,
            "z": lax.axis_index("fsdp"),
        }

    def shift(self, value, axis, by):
        n = self.sizes[axis]
        if axis == "z":
            return lax.ppermute(value, "fsdp", [(i, (i + by) % n) for i in range(n)])
        inner = {"y": 2 * self.sizes["x"], "x": 2, "core": 1}[axis]
        pairs = []
        for i in range(2 * self.sizes["y"] * self.sizes["x"]):
            at = (i // inner) % n
            pairs.append((i, i + ((at + by) % n - at) * inner))
        return lax.ppermute(value, "dp", pairs)

    def gather_axis(self, value, axis, at):
        n, dim = self.sizes[axis], self.order.index(axis)
        pieces = [value] + [self.shift(value, axis, d) for d in range(1, n)]
        rows = []
        for j in range(n):
            row = pieces[-j % n]
            for i in range(1, n):
                row = jnp.where(at == i, pieces[(i - j) % n], row)
            rows.append(row)
        return jnp.concatenate(rows, axis=dim)

    def gather(self, shard, axes):
        at = self.coordinates()
        value = shard[None, None, None, None]
        for axis in axes:
            value = self.gather_axis(value, axis, at[axis])
        return value.reshape(-1, shard.shape[1])

    def shift_xy(self, value, dy, dx):
        ny, nx = self.sizes["y"], self.sizes["x"]
        pairs = []
        for y in range(ny):
            for x in range(nx):
                for c in range(2):
                    pairs.append(((y * nx + x) * 2 + c, ((y + dy) % ny * nx + (x + dx) % nx) * 2 + c))
        return lax.ppermute(value, "dp", pairs)

    def steps_xy(self):
        return [(dy, dx) for dy in range(self.sizes["y"]) for dx in range(self.sizes["x"]) if dy or dx]

    def xy_sum(self, value, wire=F32):
        plane = self.sizes["y"] * self.sizes["x"]
        groups = [[2 * k + c for k in range(plane)] for c in range(2)]
        value = value.reshape(plane, *value.shape[3:]).astype(wire)
        got = lax.all_to_all(value, "dp", 0, 0, axis_index_groups=groups)
        return jnp.sum(got.astype(F32), axis=0)

    def z_sum(self, value, wire=F32):
        count, at = self.sizes["z"], lax.axis_index("fsdp")
        total = lax.dynamic_index_in_dim(value, at, 0, keepdims=False)
        for d in range(1, count):
            part = lax.dynamic_index_in_dim(value, (at + d) % count, 0, keepdims=False)
            total = total + self.shift(part.astype(wire), "z", d).astype(F32)
        return total

    def core_send(self, value, at):
        return self.shift(lax.dynamic_index_in_dim(value, 1 - at["core"], 2), "core", 1)

    def core_sum(self, value, got, at):
        return lax.dynamic_index_in_dim(value, at["core"], 2) + got

    def blocks(self, whole):
        s = self.sizes
        return whole.reshape(s["y"], s["x"], s["core"], s["z"], -1, whole.shape[1])

    def total_core(self, value):
        return value + self.shift(value, "core", 1)

    def total_xy(self, value):
        return value + sum(self.shift_xy(value, dy, dx) for dy, dx in self.steps_xy())

    def total_z(self, value):
        return value + sum(self.shift(value, "z", d) for d in range(1, self.sizes["z"]))


AXES = ("dp", "fsdp")


def rms_norm(values, scales):
    return values * lax.rsqrt(jnp.mean(values * values, axis=-1, keepdims=True) + EPSILON) * scales


def side_by_side(value):
    r = value.shape[-2] // 2
    return jnp.concatenate([value[..., :r, :], value[..., r:, :]], axis=-1)


def norm_part(stream, gain):
    return rms_norm(stream, gain[None, :])


def on_device(
    net,
    hidden_in,
    cotangent,
    seq_lengths,
    in_weight,
    out_weight,
    vector_weight,
    head_weight,
    in_row_moment,
    in_col_moment,
    out_row_moment,
    out_col_moment,
    vector_moment,
    head_moment,
):
    token_count = hidden_in.shape[0]
    lengths = seq_lengths[0]
    e0 = lengths[0]
    e1 = e0 + lengths[1]
    e2 = e1 + lengths[2]
    e3 = e2 + lengths[3]
    ends = jnp.stack([e0, e1, e2, e3])
    valid = (jnp.arange(token_count, dtype=jnp.int32) < e3).astype(F32)
    spread, gather = spread_matrices()
    shard_rows = in_weight.shape[1]
    in_low = jnp.pad(in_weight.astype(BF16), ((0, 0), (0, 0), (0, INNER + XR - P_SIZE)))
    out_low = out_weight.astype(BF16).reshape(LAYERS, 2, shard_rows, D)
    vec_low = vector_weight.astype(BF16).reshape(-1)
    vec_low = jnp.pad(vec_low, (0, shard_rows * LANES - vec_low.shape[0])).reshape(shard_rows, LANES)
    first = net.gather(jnp.concatenate([in_low[0, :, INNER:], vec_low], axis=1), ("z", "x", "y", "core"))
    first_z = net.gather(in_low[0, :, :INNER], ("z", "y", "x", "core"))
    rest = lax.all_gather(
        jnp.concatenate([out_low[0, 0], out_low[0, 1], in_low[1], out_low[1, 0], out_low[1, 1]], axis=1),
        AXES,
        axis=0,
        tiled=True,
    )
    devices = rest.shape[0] // shard_rows

    def out_rows(columns):
        columns = columns.reshape(devices, 1, shard_rows, 2 * D)
        return jnp.concatenate([columns[..., :D], columns[..., D:]], axis=1).reshape(INNER, D)

    in_from = 2 * D
    out_from = in_from + INNER + XR
    ins = [
        (first_z, first[:, :XR]),
        (rest[:, in_from : in_from + INNER], rest[:, in_from + INNER : out_from]),
    ]
    outs = [out_rows(rest[:, :in_from]), out_rows(rest[:, out_from:])]
    vector_full = first[:, XR:].reshape(devices, -1)[:, : LAYERS * VEC // devices]
    vector_full = vector_full.reshape(devices, LAYERS, -1).swapaxes(0, 1).reshape(LAYERS, VEC).astype(F32)
    stream = hidden_in.astype(F32)
    stored = []
    for l in range(LAYERS):
        tables = kernel_params(vector_full[l], head_weight[l])
        normed_from = hidden_in if l == 0 else stream
        normed = norm_part(stream, vector_full[l, :D]).astype(BF16)
        z = jnp.dot(normed, ins[l][0], preferred_element_type=F32)
        xr = jnp.dot(normed, ins[l][1], preferred_element_type=F32)
        gn, ys, st = mixer_forward(ends, xr, *tables, spread, z)
        stream = stream + jnp.dot(gn, outs[l], preferred_element_type=F32)
        stored.append((normed_from, normed, z, xr, gn, ys, st, tables))
    fence = lax.optimization_barrier
    blocks = token_count // SPAN
    at = net.coordinates()
    flowing = cotangent.astype(F32) * valid[:, None]
    small_parts = [None] * LAYERS
    arrived = [None] * LAYERS
    in_sums = []

    def product(a, b):
        return jnp.einsum("td,tp->dp", a, b, preferred_element_type=F32)

    for l in reversed(range(LAYERS)):
        normed_from, normed, z, xr, gn, ys, st, tables = stored[l]
        wire = BF16 if l == 0 else F32
        gb = flowing.astype(BF16)
        grad_out = product(gn, gb)
        gb, grad_out = fence((gb, grad_out))
        got = net.core_send(net.blocks(grad_out), at)
        dgn = jnp.einsum("td,ed->te", gb, outs[l], preferred_element_type=F32)
        dgn, grad_out, got = fence((dgn, grad_out, got))
        out_sum = side_by_side(net.core_sum(net.blocks(grad_out), got, at))
        waiting = jnp.concatenate(in_sums + [out_sum], axis=-1).astype(wire)
        dgn, waiting, arrived = fence((dgn, waiting, arrived))
        waiting = net.xy_sum(waiting, wire)
        back = mixer_backward(ends, xr, ys, st, *tables, spread, gather, (z, dgn), 0, blocks)
        back, waiting = fence((back, waiting))
        if l > 0:
            arrived[l] = net.z_sum(waiting, wire)
        dxr, dz = back[0], back[6]
        grads = [product(normed, dxr), product(normed, dz)]
        dz, dxr, grads = fence((dz, dxr, grads))
        got = [net.core_send(net.blocks(g), at) for g in grads]
        if l == 0:
            grads, got, in_late, out_late, vector_late = fence((grads, got, in_weight, out_weight, vector_weight))
            in_sums = [net.core_sum(net.blocks(g), v, at) for g, v in zip(grads, got)]
            in_zero = jnp.concatenate(in_sums, axis=-1).astype(BF16)
            dz, dxr, in_zero, waiting = fence((dz, dxr, in_zero, waiting))
            in_zero = net.xy_sum(in_zero, BF16)
            arrived[0] = net.z_sum(waiting, wire)
        gain = jnp.broadcast_to(vector_full[l, None, :D], (8, D))
        flowing, dnorm = norm_backward(dz, dxr, *ins[l], normed_from, flowing, gain)
        if l > 0:
            flowing, grads, got = fence((flowing, grads, got))
            in_sums = [net.core_sum(net.blocks(g), v, at) for g, v in zip(grads, got)]
        dvec, dhead = finish_params(back[7], *back[1:4])
        small_parts[l] = jnp.concatenate([jnp.sum(dnorm, axis=0), dvec, dhead.reshape(-1)])
    small = jnp.stack(small_parts)
    small = jnp.pad(small, ((0, 0), (0, -small.shape[1] % LANES))).reshape(-1, LANES)
    layer_out = stream.astype(BF16)
    weight_squares = [jnp.sum(w * w, axis=tuple(range(1, w.ndim))) for w in (in_late, out_late, vector_late)]
    small = net.total_core(small)
    small, in_zero, arrived, flowing, layer_out, weight_squares = fence(
        (small, in_zero, arrived, flowing, layer_out, weight_squares)
    )
    in_zero = net.z_sum(in_zero, BF16)
    small = net.total_xy(small)
    in_zero, small = fence((in_zero, small))
    small = net.total_z(small).reshape(LAYERS, -1)
    head_total = small[:, VEC : VEC + 3 * NHEADS].reshape(LAYERS, 3, NHEADS)
    share = VEC // devices
    mine = lax.axis_index("dp") * lax.axis_size("fsdp") + lax.axis_index("fsdp")
    grad_vector = lax.dynamic_slice(small, (0, mine * share), (LAYERS, share))
    grad_in = jnp.stack(
        [jnp.concatenate([v[:, XR : XR + INNER], v[:, : P_SIZE - INNER]], axis=1) for v in (in_zero, arrived[0])]
    )
    grad_out = jnp.stack([jnp.concatenate([v[:, -2 * D : -D], v[:, -D:]], axis=0) for v in arrived])
    squares_in = grad_in * grad_in
    squares_out = grad_out * grad_out
    row_in = MOMENT_DECAY * in_row_moment + (1.0 - MOMENT_DECAY) * jnp.mean(squares_in, axis=2)
    row_out = MOMENT_DECAY * out_row_moment + (1.0 - MOMENT_DECAY) * jnp.mean(squares_out, axis=2)
    vector_new = MOMENT_DECAY * vector_moment + (1.0 - MOMENT_DECAY) * grad_vector * grad_vector
    vector_update = grad_vector * lax.rsqrt(vector_new)
    totals = jnp.stack(
        [
            jnp.sum(row_in, axis=1),
            jnp.sum(row_out, axis=1),
            *weight_squares,
            jnp.sum(vector_update * vector_update, axis=1),
        ],
        axis=1,
    )
    local = (
        jnp.sum(squares_in, axis=1),
        jnp.sum(squares_out, axis=1),
        jnp.sum(squares_in / row_in[:, :, None], axis=1),
        jnp.sum(squares_out / row_out[:, :, None], axis=1),
        totals,
    )
    edges = [0]
    for v in local:
        edges.append(edges[-1] + v.shape[1])
    summed = jnp.concatenate(local, axis=1)
    summed = jnp.pad(summed, ((0, 0), (0, -edges[-1] % LANES))).reshape(-1, LANES)
    summed = net.total_z(net.total_xy(net.total_core(summed))).reshape(LAYERS, -1)
    column_in, column_out, scaled_in, scaled_out, totals = [
        summed[:, a:b] for a, b in zip(edges[:-1], edges[1:])
    ]
    col_in = MOMENT_DECAY * in_col_moment + (1.0 - MOMENT_DECAY) * column_in / D
    col_out = MOMENT_DECAY * out_col_moment + (1.0 - MOMENT_DECAY) * column_out / INNER
    mean_in = totals[:, 0] / D
    mean_out = totals[:, 1] / INNER
    norm_in = jnp.sqrt(mean_in * jnp.sum(scaled_in / col_in, axis=1) / (D * P_SIZE))
    norm_out = jnp.sqrt(mean_out * jnp.sum(scaled_out / col_out, axis=1) / (INNER * D))
    norm_vector = jnp.sqrt(totals[:, 5] / VEC)
    head_new = MOMENT_DECAY * head_moment + (1.0 - MOMENT_DECAY) * head_total * head_total
    head_update = head_total * lax.rsqrt(head_new)
    norm_head = jnp.sqrt(jnp.mean(head_update * head_update, axis=(1, 2)))

    def step_of(square_mean, norm):
        return RELATIVE_STEP * jnp.sqrt(square_mean) / jnp.maximum(1.0, norm / CLIP_LIMIT)

    step_in = step_of(totals[:, 2] / (D * P_SIZE), norm_in)
    step_out = step_of(totals[:, 3] / (INNER * D), norm_out)
    step_vector = step_of(totals[:, 4] / VEC, norm_vector)
    step_head = step_of(jnp.mean(head_weight * head_weight, axis=(1, 2)), norm_head)
    update_in = grad_in * lax.rsqrt(row_in[:, :, None] * col_in[:, None, :] / mean_in[:, None, None])
    update_out = grad_out * lax.rsqrt(row_out[:, :, None] * col_out[:, None, :] / mean_out[:, None, None])
    new_in = in_weight - step_in[:, None, None] * update_in
    new_out = out_weight - step_out[:, None, None] * update_out
    new_vector = vector_weight - step_vector[:, None] * vector_update
    new_head = head_weight - step_head[:, None, None] * head_update
    update_rms = jnp.stack([norm_in, norm_out, norm_vector, norm_head], axis=1)
    return (
        layer_out,
        flowing,
        grad_in,
        grad_out,
        grad_vector,
        head_total,
        new_in,
        new_out,
        new_vector,
        new_head,
        new_in.astype(BF16),
        new_out.astype(BF16),
        new_vector.astype(BF16),
        new_head.astype(BF16),
        row_in,
        col_in,
        row_out,
        col_out,
        vector_new,
        head_new,
        update_rms,
    )


def solution(mesh):
    rows = P(AXES, None)
    mat = P(None, AXES, None)
    vec = P(None, AXES)
    one = P()
    return jax.shard_map(
        partial(on_device, Net(mesh)),
        mesh=mesh,
        in_specs=(rows, rows, rows, mat, mat, vec, one, vec, one, vec, one, vec, one),
        out_specs=(
            rows, rows, mat, mat, vec, one, mat, mat, vec, one, mat, mat, vec, one, vec, one, vec, one, vec, one, one,
        ),
        check_vma=False,
    )
```

```python
from functools import partial

import jax
import jax.numpy as jnp
import ml_dtypes
import numpy as np
from jax import lax
from jax.experimental import pallas as pl
from jax.experimental.pallas import tpu as pltpu
from jax.sharding import PartitionSpec as P

D = 768
NHEADS = 24
HEADDIM = 64
STATE = 128
LAYERS = 2
INNER = 1536
CH = 1792
P_SIZE = 3352
XR = 1920
VEC = 11264

EPSILON = 1e-05
MOMENT_DECAY = 0.5
CLIP_LIMIT = 1.0
RELATIVE_STEP = 0.5

SPAN = 128
GROUP = 256
GATE_ROWS = 64
GATE_BLOCK = 256
NORM_BLOCK = 256
GROUPS = INNER // GROUP
LANES = 128
LOG2E = 1.4426950408889634
VMEM_LIMIT = 60 * 1024 * 1024
F32 = jnp.float32
BF16 = jnp.bfloat16
NN = ((1,), (0,))
NT = ((1,), (1,))
TN = ((0,), (0,))

PASS_PAIR = 3
PASS_STATE = 3
PASS_RED = 2


def halves(v):
    high = v.astype(BF16)
    return high, (v - high.astype(F32)).astype(BF16)


def raw_dot(a, b, dims):
    return lax.dot_general(a, b, (dims, ((), ())), preferred_element_type=F32)


def mm(a, b, dims, passes, pack=None):
    if passes == 1:
        return raw_dot(a.astype(BF16), b.astype(BF16), dims)
    a_hi, a_lo = halves(a)
    b_hi, b_lo = halves(b)
    if pack == "k":
        left = jnp.concatenate([a_hi, a_lo], axis=dims[0][0])
        right = jnp.concatenate([b_hi, b_hi], axis=dims[1][0])
        return raw_dot(left, right, dims) + raw_dot(a_hi, b_lo, dims)
    if pack == "n":
        both = raw_dot(a_hi, jnp.concatenate([b_hi, b_lo], axis=1 - dims[1][0]), dims)
        half = both.shape[1] // 2
        return both[:, :half] + (both[:, half:] + raw_dot(a_lo, b_hi, dims))
    return raw_dot(a_hi, b_hi, dims) + (raw_dot(a_lo, b_hi, dims) + raw_dot(a_hi, b_lo, dims))


def exact_left(a01, b):
    hi, lo = halves(b)
    rest = (b - hi.astype(F32) - lo.astype(F32)).astype(BF16)
    return raw_dot(a01, hi, NN) + (raw_dot(a01, lo, NN) + raw_dot(a01, rest, NN))


def reduce_right(a, b01, passes):
    if passes == 1:
        return raw_dot(a.astype(BF16), b01, NN)
    hi, lo = halves(a)
    return raw_dot(hi, b01, NN) + raw_dot(lo, b01, NN)


def sigmoid(v):
    return 0.5 * jnp.tanh(0.5 * v) + 0.5


def partial8(v):
    return jnp.sum(v.reshape(v.shape[0] // 8, 8, v.shape[1]), axis=0)


def segment_of(place, ends_ref):
    total = (place >= ends_ref[0]).astype(jnp.int32)
    for k in range(1, 4):
        total = total + (place >= ends_ref[k]).astype(jnp.int32)
    return total


def scalar_segment(place, ends_ref):
    total = jnp.int32(0)
    for k in range(4):
        total = total + jnp.where(place >= ends_ref[k], 1, 0).astype(jnp.int32)
    return total


def block_terms(base, ends_ref, hw_ref, rate_in):
    shape = (SPAN, LANES)
    place = base + lax.broadcasted_iota(jnp.int32, shape, 0)
    seg = segment_of(place, ends_ref)
    first_seg = jnp.where(base > 0, scalar_segment(base - 1, ends_ref), -1)
    last_seg = scalar_segment(base + SPAN - 1, ends_ref)
    pre = rate_in + hw_ref[0:1, :]
    head_ok = lax.broadcasted_iota(jnp.int32, shape, 1) < NHEADS
    steps = jnp.where(head_ok, jnp.maximum(pre, 0.0) + jnp.log1p(jnp.exp(-jnp.abs(pre))), 0.0)
    log_rate = hw_ref[1:2, :] * steps
    rows = lax.broadcasted_iota(jnp.int32, (SPAN, SPAN), 0)
    cols = lax.broadcasted_iota(jnp.int32, (SPAN, SPAN), 1)
    lower = jnp.where(rows >= cols, 1.0, 0.0)
    cum = exact_left(lower.astype(BF16), log_rate * LOG2E)
    reach = jnp.where(seg == first_seg, jnp.exp2(cum), 0.0)
    to_end = jnp.where(seg == last_seg, jnp.exp2(cum[SPAN - 1 : SPAN, :] - cum), 0.0)
    seg_row = segment_of(base + cols, ends_ref)
    seg_col = segment_of(base + rows, ends_ref)
    same = seg_row == seg_col
    return place, seg, pre, steps, log_rate, cum, reach, to_end, rows, cols, same


def lag_mask(place, seg, ends_ref, lag):
    other = place + lag
    ok = (segment_of(other, ends_ref) == seg) & (other >= 0)
    return jnp.where(ok, 1.0, 0.0)


def two_parts(v):
    hi, lo = halves(v)
    return jnp.concatenate([hi, lo], axis=1)


def lane_split(v):
    first = lax.broadcasted_iota(jnp.int32, v.shape, 1) < HEADDIM
    return jnp.concatenate([jnp.where(first, v, 0.0), jnp.where(first, 0.0, v)], axis=0)


def pair_columns(cum, head):
    one = jnp.broadcast_to(cum[:, head : head + 1], (SPAN, SPAN))
    two = jnp.broadcast_to(cum[:, head + 1 : head + 2], (SPAN, SPAN))
    return jnp.concatenate([one, two], axis=1)


def pair_rows(cum_t, head):
    return jnp.concatenate([cum_t[head : head + 1, :], cum_t[head + 1 : head + 2, :]], axis=1)


def gate_rows(z_ref, ys_ref, gain_ref, gn_ref, yg):
    for r in range(ys_ref.shape[0] // GATE_ROWS):
        rs = slice(GATE_ROWS * r, GATE_ROWS * (r + 1))
        squares = jnp.zeros((GATE_ROWS, LANES), F32)
        for c in range(INNER // LANES):
            cs = slice(LANES * c, LANES * (c + 1))
            z = z_ref[rs, cs]
            gated = ys_ref[rs, cs] * (z * sigmoid(z))
            yg[rs, cs] = gated
            squares = squares + gated * gated
        scale = lax.rsqrt(jnp.sum(squares, axis=1, keepdims=True) / INNER + EPSILON)
        scale = jnp.broadcast_to(scale, (GATE_ROWS, LANES))
        for c in range(INNER // LANES):
            cs = slice(LANES * c, LANES * (c + 1))
            gn_ref[rs, cs] = (yg[rs, cs] * scale * gain_ref[0:1, cs]).astype(BF16)


def forward_kernel(gated, ends_ref, xr_ref, par_ref, gain_ref, hw_ref, spread_ref, *refs):
    if gated:
        z_ref, gn_ref, *refs = refs
    ys_ref, st_ref, buf, act, state, *yg = refs
    block = pl.program_id(0)
    base = block * SPAN

    @pl.when(block == 0)
    def _():
        buf[0:8, :] = jnp.zeros((8, CH), F32)
        state[...] = jnp.zeros_like(state)

    place, seg, pre, steps, log_rate, cum, reach, to_end, rows, cols, same = block_terms(
        base, ends_ref, hw_ref, xr_ref[:, CH:XR]
    )
    masks = [lag_mask(place, seg, ends_ref, -k) for k in range(1, 4)]
    for c in range(CH // LANES):
        cs = slice(LANES * c, LANES * (c + 1))
        now = xr_ref[:, cs]
        buf[8 : 8 + SPAN, cs] = now
        conv = par_ref[4:5, cs] + par_ref[3:4, cs] * now
        for k in range(1, 4):
            conv = conv + par_ref[3 - k : 4 - k, cs] * (masks[k - 1] * buf[8 - k : 8 - k + SPAN, cs])
        buf[0:8, cs] = now[SPAN - 8 : SPAN, :]
        act[:, cs] = conv * sigmoid(conv)
    bm = act[:, INNER : INNER + STATE]
    cm = act[:, INNER + STATE : CH]
    gram = mm(cm, bm, NT, 3)
    gram2 = jnp.concatenate([gram, gram], axis=1)
    bias = jnp.where(same & (rows >= cols), 0.0, -1e30)
    bias2 = jnp.concatenate([bias, bias], axis=1)
    cum_t = cum.T
    bm_t = bm.T
    steps2, reach2, to_end2 = two_parts(steps), two_parts(reach), two_parts(to_end)
    st_ref[0] = state[...]
    for g in range(GROUPS):
        gs = slice(GROUP * g, GROUP * (g + 1))
        spread = spread_ref[:, gs]
        x = act[:, gs]
        xd = x * raw_dot(steps2, spread, NN)
        within = []
        for q in range(2):
            head = 4 * g + 2 * q
            mix = jnp.exp2(pair_columns(cum, head) - pair_rows(cum_t, head) + bias2) * gram2
            within.append(mm(mix, lane_split(xd[:, LANES * q : LANES * (q + 1)]), NN, PASS_PAIR, "n"))
        reach_g = raw_dot(reach2, spread, NN)
        before = state[:, gs]
        scan = jnp.concatenate(within, axis=1) + mm(cm, before, NN, PASS_STATE, "k") * reach_g
        ys_ref[:, gs] = scan + gain_ref[1:2, gs] * x
        state[:, gs] = before * reach_g[SPAN - 1 : SPAN, :] + mm(
            bm_t, xd * raw_dot(to_end2, spread, NN), NN, PASS_STATE, "k"
        )
    if gated:
        gate_rows(z_ref, ys_ref, gain_ref, gn_ref, yg[0])


def gate_back_rows(z_ref, ys_ref, dgn_ref, gain_ref, dz_ref, dy_ref, dgain_ref, yg):
    for r in range(z_ref.shape[0] // GATE_ROWS):
        rs = slice(GATE_ROWS * r, GATE_ROWS * (r + 1))
        squares = jnp.zeros((GATE_ROWS, LANES), F32)
        overlap = jnp.zeros((GATE_ROWS, LANES), F32)
        for c in range(INNER // LANES):
            cs = slice(LANES * c, LANES * (c + 1))
            z = z_ref[rs, cs]
            gated = ys_ref[rs, cs] * (z * sigmoid(z))
            yg[rs, cs] = gated
            overlap = overlap + gated * (dgn_ref[rs, cs] * gain_ref[0:1, cs])
            squares = squares + gated * gated
        scale = lax.rsqrt(jnp.sum(squares, axis=1, keepdims=True) / INNER + EPSILON)
        pull = jnp.sum(overlap, axis=1, keepdims=True) * (scale * scale * scale) / INNER
        scale = jnp.broadcast_to(scale, (GATE_ROWS, LANES))
        pull = jnp.broadcast_to(pull, (GATE_ROWS, LANES))
        for c in range(INNER // LANES):
            cs = slice(LANES * c, LANES * (c + 1))
            z = z_ref[rs, cs]
            gate = sigmoid(z)
            gated = yg[rs, cs]
            dgn = dgn_ref[rs, cs] * scale
            dgain_ref[:, cs] += partial8(dgn * gated)
            dgated = dgn * gain_ref[0:1, cs] - gated * pull
            dy_ref[rs, cs] = dgated * (z * gate)
            dz_ref[rs, cs] = (dgated * ys_ref[rs, cs] * (gate * (1.0 + z * (1.0 - gate)))).astype(BF16)


def gate_back_kernel(z_ref, ys_ref, dgn_ref, gain_ref, dz_ref, dy_ref, dgain_ref, yg):
    @pl.when(pl.program_id(0) == 0)
    def _():
        dgain_ref[...] = jnp.zeros_like(dgain_ref)

    gate_back_rows(z_ref, ys_ref, dgn_ref, gain_ref, dz_ref, dy_ref, dgain_ref, yg)


def gate_forward(z, ys, gain):
    tokens = z.shape[0]
    rows = pl.BlockSpec((GATE_BLOCK, INNER), lambda i: (i, 0))
    return pl.pallas_call(
        gate_rows,
        grid=(tokens // GATE_BLOCK,),
        in_specs=[rows, rows, whole((8, INNER))],
        out_specs=rows,
        out_shape=jax.ShapeDtypeStruct((tokens, INNER), BF16),
        scratch_shapes=[pltpu.VMEM((GATE_BLOCK, INNER), F32)],
        compiler_params=pltpu.CompilerParams(vmem_limit_bytes=VMEM_LIMIT),
        cost_estimate=pl.CostEstimate(flops=20_000_000, bytes_accessed=20_000_000, transcendentals=0),
        name="gate_forward",
    )(z, ys, gain)


def gate_backward(z, ys, dgn, gain):
    tokens = z.shape[0]
    rows = pl.BlockSpec((GATE_BLOCK, INNER), lambda i: (i, 0))
    return pl.pallas_call(
        gate_back_kernel,
        grid=(tokens // GATE_BLOCK,),
        in_specs=[rows, rows, rows, whole((8, INNER))],
        out_specs=[rows, rows, whole((8, INNER))],
        out_shape=[
            jax.ShapeDtypeStruct((tokens, INNER), BF16),
            jax.ShapeDtypeStruct((tokens, INNER), F32),
            jax.ShapeDtypeStruct((8, INNER), F32),
        ],
        scratch_shapes=[pltpu.VMEM((GATE_BLOCK, INNER), F32)],
        compiler_params=pltpu.CompilerParams(vmem_limit_bytes=VMEM_LIMIT),
        cost_estimate=pl.CostEstimate(flops=60_000_000, bytes_accessed=30_000_000, transcendentals=0),
        name="gate_backward",
    )(z, ys, dgn, gain)


def backward_kernel(
    top, fused, ends_ref, xr_ref, halo_ref, ys_ref, st_ref, par_ref, gain_ref, hw_ref, spread_ref, gather_ref, *refs
):
    if fused:
        z_ref, dgn_ref, *refs = refs
        *refs, dz_ref, dgate_ref, dy_ref, yg = refs
    else:
        dy_ref, *refs = refs
    (
        rgrad_in, dcv_in, dxr_ref, dpar_ref, dskip_ref, dhw_ref, rgrad, dcv_out,
        buf, act, slope, dact, dcv, dgram,
    ) = refs[-14:]
    step = pl.program_id(0)
    block = top - step
    base = block * SPAN

    @pl.when(step == 0)
    def _():
        dcv[0:8, :] = dcv_in[...]
        rgrad[...] = rgrad_in[...]
        dpar_ref[...] = jnp.zeros_like(dpar_ref)
        dskip_ref[...] = jnp.zeros_like(dskip_ref)
        dhw_ref[...] = jnp.zeros_like(dhw_ref)
        if fused:
            dgate_ref[...] = jnp.zeros_like(dgate_ref)

    if fused:
        gate_back_rows(z_ref, ys_ref, dgn_ref, gain_ref, dz_ref, dy_ref, dgate_ref, yg)
    place, seg, pre, steps, log_rate, cum, reach, to_end, rows, cols, same = block_terms(
        base, ends_ref, hw_ref, xr_ref[:, CH:XR]
    )
    back_masks = [lag_mask(place, seg, ends_ref, -k) for k in range(1, 4)]
    fore_masks = [lag_mask(place, seg, ends_ref, k) for k in range(1, 4)]
    for c in range(CH // LANES):
        cs = slice(LANES * c, LANES * (c + 1))
        now = xr_ref[:, cs]
        buf[0:8, cs] = halo_ref[:, cs]
        buf[8 : 8 + SPAN, cs] = now
        conv = par_ref[4:5, cs] + par_ref[3:4, cs] * now
        for k in range(1, 4):
            conv = conv + par_ref[3 - k : 4 - k, cs] * (back_masks[k - 1] * buf[8 - k : 8 - k + SPAN, cs])
        gate = sigmoid(conv)
        act[:, cs] = conv * gate
        slope[:, cs] = gate * (1.0 + conv * (1.0 - gate))
        dcv[SPAN : SPAN + 8, cs] = dcv[0:8, cs]
    bm = act[:, INNER : INNER + STATE]
    cm = act[:, INNER + STATE : CH]
    gram_t = mm(cm, bm, NT, 3).T
    gram2 = jnp.concatenate([gram_t, gram_t], axis=1)
    bias = jnp.where(same & (rows <= cols), 0.0, -1e30)
    bias2 = jnp.concatenate([bias, bias], axis=1)
    cum_t = cum.T
    cm_t = cm.T
    steps2, reach2, to_end2 = two_parts(steps), two_parts(reach), two_parts(to_end)

    dgram[...] = jnp.zeros_like(dgram)
    dbm = jnp.zeros((SPAN, STATE), F32)
    dcm = jnp.zeros((SPAN, STATE), F32)
    red_rate = jnp.zeros((SPAN, LANES), F32)
    red_tail = jnp.zeros((SPAN, LANES), F32)
    red_step = jnp.zeros((SPAN, LANES), F32)
    red_through = jnp.zeros((8, LANES), F32)
    for g in range(GROUPS):
        gs = slice(GROUP * g, GROUP * (g + 1))
        spread = spread_ref[:, gs]
        gather = gather_ref[gs, :]
        x = act[:, gs]
        skip = gain_ref[1:2, gs]
        dy = dy_ref[:, gs]
        dskip_ref[:, gs] += partial8(dy * x)
        steps_g = raw_dot(steps2, spread, NN)
        reach_g = raw_dot(reach2, spread, NN)
        to_end_g = raw_dot(to_end2, spread, NN)
        xd = x * steps_g
        dxd_in = []
        for q in range(2):
            head = 4 * g + 2 * q
            qs = slice(LANES * q, LANES * (q + 1))
            decay = jnp.exp2(pair_rows(cum_t, head) - pair_columns(cum, head) + bias2)
            dy_two = lane_split(dy[:, qs])
            dxd_in.append(mm(decay * gram2, dy_two, NN, PASS_PAIR, "n"))
            dgram[...] += decay * mm(xd[:, qs], dy_two, NT, PASS_PAIR)
        dxd_in = jnp.concatenate(dxd_in, axis=1)
        later = rgrad[:, gs]
        before = st_ref[0, :, gs]
        dxd_out = mm(bm, later, NN, PASS_STATE) * to_end_g
        dbm = dbm + mm(xd * to_end_g, later, NT, PASS_STATE, "n")
        dy_reach = dy * reach_g
        dcm = dcm + mm(dy_reach, before, NT, PASS_STATE, "n")
        fade = reach_g[SPAN - 1 : SPAN, :]
        red_through = red_through + reduce_right(partial8(before * later) * fade, gather, 2)
        rgrad[:, gs] = later * fade + mm(cm_t, dy_reach, NN, PASS_STATE)
        if PASS_PAIR == 1:
            dy_seen, xd_seen = dy.astype(BF16).astype(F32), xd.astype(BF16).astype(F32)
        else:
            dy_seen, xd_seen = dy, xd
        dxd = dxd_in + dxd_out
        red_rate = red_rate + reduce_right(dy_seen * (ys_ref[:, gs] - skip * x) - xd_seen * dxd_in, gather, 2)
        red_tail = red_tail + reduce_right(x * dxd_out, gather, PASS_RED)
        red_step = red_step + reduce_right(x * dxd, gather, PASS_RED)
        dact[:, gs] = skip * dy + steps_g * dxd
    dgram_t = dgram[:, :SPAN] + dgram[:, SPAN:]
    dact[:, INNER : INNER + STATE] = dbm + mm(dgram_t, cm, NN, 3)
    dact[:, INNER + STATE : CH] = dcm + mm(dgram_t.T, bm, NN, 3)

    upper = jnp.where(rows <= cols, 1.0, 0.0).astype(BF16)
    strict = jnp.where(rows > cols, 1.0, 0.0).astype(BF16)
    through = jnp.sum(red_through, axis=0, keepdims=True)
    drate = exact_left(upper, red_rate) + exact_left(strict, steps * red_tail) + through
    dsteps = red_step + drate * hw_ref[1:2, :]
    dpre = dsteps * sigmoid(pre)
    dhw_ref[0:8, :] += partial8(dpre)
    dhw_ref[8:16, :] += partial8(drate * log_rate)
    dxr_ref[:, CH:XR] = dpre.astype(BF16)

    for c in range(CH // LANES):
        cs = slice(LANES * c, LANES * (c + 1))
        now = xr_ref[:, cs]
        dconv = dact[:, cs] * slope[:, cs]
        dcv[0:SPAN, cs] = dconv
        dxbc = par_ref[3:4, cs] * dconv
        dpar_ref[24:32, cs] += partial8(dconv * now)
        dpar_ref[32:40, cs] += partial8(dconv)
        for k in range(1, 4):
            ahead = fore_masks[k - 1] * dcv[k : k + SPAN, cs]
            dxbc = dxbc + par_ref[3 - k : 4 - k, cs] * ahead
            dpar_ref[24 - 8 * k : 32 - 8 * k, cs] += partial8(ahead * now)
        dxr_ref[:, cs] = dxbc.astype(BF16)
    dcv_out[...] = dcv[0:8, :]


def spread_matrices():
    one = (np.arange(LANES)[:, None] == np.arange(INNER)[None, :] // HEADDIM).astype(ml_dtypes.bfloat16)
    return jnp.asarray(np.concatenate([one, one], axis=0)), jnp.asarray(one.T)


def kernel_params(vector, head):
    taps = vector[D + INNER :].reshape(5, CH)
    par = jnp.concatenate([taps, jnp.zeros((3, CH), F32)], axis=0)
    gain = jnp.stack([vector[D : D + INNER], jnp.repeat(head[2], HEADDIM)])
    gain = jnp.concatenate([gain, jnp.zeros((6, INNER), F32)], axis=0)
    hw = jnp.stack([head[0], -jnp.exp(head[1])])
    hw = jnp.pad(hw, ((0, 6), (0, LANES - NHEADS)))
    return par, gain, hw


def whole(shape):
    return pl.BlockSpec(shape, lambda i: (0,) * len(shape))


SMEM = pl.BlockSpec(memory_space=pltpu.SMEM)


def mixer_forward(ends, xr, par, gain, hw, spread, z=None):
    tokens = xr.shape[0]
    blocks = tokens // SPAN
    rows = lambda width: pl.BlockSpec((SPAN, width), lambda i: (i, 0))
    in_specs = [SMEM, rows(XR), whole((8, CH)), whole((8, INNER)), whole((8, LANES)), whole((256, INNER))]
    out_specs = [rows(INNER), pl.BlockSpec((1, STATE, INNER), lambda i: (i, 0, 0))]
    out_shape = [
        jax.ShapeDtypeStruct((tokens, INNER), F32),
        jax.ShapeDtypeStruct((blocks, STATE, INNER), F32),
    ]
    scratch = [
        pltpu.VMEM((SPAN + 8, CH), F32),
        pltpu.VMEM((SPAN, CH), F32),
        pltpu.VMEM((STATE, INNER), F32),
    ]
    more = []
    if z is not None:
        more = [z]
        in_specs.append(rows(INNER))
        out_specs.insert(0, rows(INNER))
        out_shape.insert(0, jax.ShapeDtypeStruct((tokens, INNER), BF16))
        scratch.append(pltpu.VMEM((SPAN, INNER), F32))
    return pl.pallas_call(
        partial(forward_kernel, z is not None),
        grid=(blocks,),
        in_specs=in_specs,
        out_specs=out_specs,
        out_shape=out_shape,
        scratch_shapes=scratch,
        compiler_params=pltpu.CompilerParams(vmem_limit_bytes=VMEM_LIMIT),
        cost_estimate=pl.CostEstimate(flops=30_000_000_000, bytes_accessed=30_000_000, transcendentals=0),
        name="mixer_forward",
    )(ends, xr, par, gain, hw, spread, *more)


def mixer_backward(ends, xr, ys, st, par, gain, hw, spread, gather, grads, first, last, earlier=None):
    tokens = xr.shape[0]
    top = last - 1
    fused = len(grads) == 2
    back = lambda width: pl.BlockSpec((SPAN, width), lambda i: (top - i, 0))
    halo = pl.BlockSpec((8, XR), lambda i: (jnp.maximum((top - i) * (SPAN // 8) - 1, 0), 0))
    if earlier is None:
        held, carried = [], [jnp.zeros((STATE, INNER), F32), jnp.zeros((8, CH), F32)]
    else:
        held, carried = list(earlier[:1]), list(earlier[4:6])
    in_specs = [
        SMEM,
        back(XR),
        halo,
        back(INNER),
        pl.BlockSpec((1, STATE, INNER), lambda i: (top - i, 0, 0)),
        whole((8, CH)),
        whole((8, INNER)),
        whole((8, LANES)),
        whole((256, INNER)),
        whole((INNER, LANES)),
    ]
    in_specs += [back(INNER)] * len(grads)
    held_at = len(in_specs)
    in_specs += [pl.BlockSpec(memory_space=pl.ANY)] * len(held)
    in_specs += [whole((STATE, INNER)), whole((8, CH))]
    outs = [
        (back(XR), (tokens, XR), BF16),
        (whole((40, CH)), (40, CH), F32),
        (whole((8, INNER)), (8, INNER), F32),
        (whole((16, LANES)), (16, LANES), F32),
        (whole((STATE, INNER)), (STATE, INNER), F32),
        (whole((8, CH)), (8, CH), F32),
    ]
    scratch = [
        pltpu.VMEM((SPAN + 8, CH), F32),
        pltpu.VMEM((SPAN, CH), F32),
        pltpu.VMEM((SPAN, CH), F32),
        pltpu.VMEM((SPAN, CH), F32),
        pltpu.VMEM((SPAN + 8, CH), F32),
        pltpu.VMEM((SPAN, 2 * SPAN), F32),
    ]
    if fused:
        outs += [(back(INNER), (tokens, INNER), BF16), (whole((8, INNER)), (8, INNER), F32)]
        scratch += [pltpu.VMEM((SPAN, INNER), F32)] * 2
    kernel = partial(backward_kernel, top, fused)
    if fused:
        def kernel(*refs):
            plain, (dz_ref, dgate_ref), used, last_two = refs[: -10], refs[-10:-8], refs[-8:-2], refs[-2:]
            backward_kernel(top, fused, *plain, *used, dz_ref, dgate_ref, *last_two)

    return pl.pallas_call(
        kernel,
        grid=(last - first,),
        in_specs=in_specs,
        out_specs=[o[0] for o in outs],
        out_shape=[jax.ShapeDtypeStruct(o[1], o[2]) for o in outs],
        input_output_aliases={held_at + k: k for k in range(len(held))},
        scratch_shapes=scratch,
        compiler_params=pltpu.CompilerParams(vmem_limit_bytes=VMEM_LIMIT),
        cost_estimate=pl.CostEstimate(
            flops=7_000_000_000 * (last - first), bytes_accessed=5_000_000 * (last - first), transcendentals=0
        ),
        name="mixer_backward",
    )(ends, xr, xr, ys, st, par, gain, hw, spread, gather, *grads, *held, *carried)


def norm_back_kernel(dz_ref, dxr_ref, wz_ref, wx_ref, h_ref, flow_ref, gain_ref, out_ref, dgain_ref, *low_ref):
    @pl.when(pl.program_id(0) == 0)
    def _():
        dgain_ref[...] = jnp.zeros_like(dgain_ref)

    dxn = raw_dot(dz_ref[...], wz_ref[...], NT) + raw_dot(dxr_ref[...], wx_ref[...], NT)
    h = h_ref[...].astype(F32)
    scale = lax.rsqrt(jnp.sum(h * h, axis=1, keepdims=True) / D + EPSILON)
    scaled = dxn * gain_ref[0:1, :]
    pull = jnp.sum(scaled * h, axis=1, keepdims=True) * (scale * scale * scale) / D
    total = flow_ref[...] + (scale * scaled - h * pull)
    out_ref[...] = total
    if low_ref:
        low_ref[0][...] = total.astype(BF16)
    dgain_ref[...] += partial8(dxn * (h * scale))


def norm_backward(dz, dxr, wz, wx, z_at, low, h, flowing, gain):
    tokens = dz.shape[0]
    rows = lambda width: pl.BlockSpec((NORM_BLOCK, width), lambda i: (i, 0))
    return pl.pallas_call(
        norm_back_kernel,
        grid=(tokens // NORM_BLOCK,),
        in_specs=[
            rows(INNER),
            rows(XR),
            pl.BlockSpec((D, INNER), lambda i: (0, z_at)),
            whole((D, XR)),
            rows(D),
            rows(D),
            whole((8, D)),
        ],
        out_specs=[rows(D), whole((8, D))] + [rows(D)] * low,
        out_shape=[jax.ShapeDtypeStruct((tokens, D), F32), jax.ShapeDtypeStruct((8, D), F32)]
        + [jax.ShapeDtypeStruct((tokens, D), BF16)] * low,
        compiler_params=pltpu.CompilerParams(vmem_limit_bytes=VMEM_LIMIT),
        cost_estimate=pl.CostEstimate(flops=1_000_000, bytes_accessed=1_000_000, transcendentals=0),
        name="norm_backward",
    )(dz, dxr, wz, wx, h, flowing, gain)


def finish_params(dgate, dpar, dskip, dhw):
    dtaps = jnp.sum(dpar.reshape(5, 8, CH), axis=1).reshape(5 * CH)
    dgate = jnp.sum(dgate, axis=0)
    dskip = jnp.sum(dskip.reshape(8, NHEADS, HEADDIM), axis=(0, 2))
    dh = jnp.sum(dhw.reshape(2, 8, LANES), axis=1)[:, :NHEADS]
    return jnp.concatenate([dgate, dtaps]), jnp.concatenate([dh, dskip[None]], axis=0)


class Net:
    def __init__(self, mesh):
        side = round((mesh.shape["dp"] // 2) ** 0.5)
        self.sizes = {"y": mesh.shape["dp"] // (2 * side), "x": side, "core": 2, "z": mesh.shape["fsdp"]}
        self.order = ("y", "x", "core", "z")

    def coordinates(self):
        at = lax.axis_index("dp")
        return {
            "y": at // (2 * self.sizes["x"]),
            "x": (at // 2) % self.sizes["x"],
            "core": at % 2,
            "z": lax.axis_index("fsdp"),
        }

    def shift(self, value, axis, by):
        n = self.sizes[axis]
        if axis == "z":
            return lax.ppermute(value, "fsdp", [(i, (i + by) % n) for i in range(n)])
        inner = {"y": 2 * self.sizes["x"], "x": 2, "core": 1}[axis]
        pairs = []
        for i in range(2 * self.sizes["y"] * self.sizes["x"]):
            at = (i // inner) % n
            pairs.append((i, i + ((at + by) % n - at) * inner))
        return lax.ppermute(value, "dp", pairs)

    def gather_axis(self, value, axis, at):
        n, dim = self.sizes[axis], self.order.index(axis)
        pieces = [value] + [self.shift(value, axis, d) for d in range(1, n)]
        rows = []
        for j in range(n):
            row = pieces[-j % n]
            for i in range(1, n):
                row = jnp.where(at == i, pieces[(i - j) % n], row)
            rows.append(row)
        return jnp.concatenate(rows, axis=dim)

    def gather(self, shard, axes):
        at = self.coordinates()
        value = shard[None, None, None, None]
        for axis in axes:
            value = self.gather_axis(value, axis, at[axis])
        return value.reshape(-1, shard.shape[1])

    def shift_xy(self, value, dy, dx):
        ny, nx = self.sizes["y"], self.sizes["x"]
        pairs = []
        for y in range(ny):
            for x in range(nx):
                for c in range(2):
                    pairs.append(((y * nx + x) * 2 + c, ((y + dy) % ny * nx + (x + dx) % nx) * 2 + c))
        return lax.ppermute(value, "dp", pairs)

    def steps_xy(self):
        return [(dy, dx) for dy in range(self.sizes["y"]) for dx in range(self.sizes["x"]) if dy or dx]

    def xy_sum(self, value, wire=F32):
        plane = self.sizes["y"] * self.sizes["x"]
        groups = [[2 * k + c for k in range(plane)] for c in range(2)]
        value = value.reshape(plane, *value.shape[3:]).astype(wire)
        got = lax.all_to_all(value, "dp", 0, 0, axis_index_groups=groups)
        return jnp.sum(got.astype(F32), axis=0)

    def z_sends(self, value, wire=F32):
        count, at = self.sizes["z"], lax.axis_index("fsdp")
        parts = [lax.dynamic_index_in_dim(value, (at + d) % count, 0, keepdims=False) for d in range(count)]
        return parts[:1] + [self.shift(parts[d].astype(wire), "z", d) for d in range(1, count)]

    def z_sum(self, value, wire=F32):
        return sum(v.astype(F32) for v in self.z_sends(value, wire))

    def core_send(self, value, at):
        return self.shift(lax.dynamic_index_in_dim(value, 1 - at["core"], 2), "core", 1)

    def core_sum(self, value, got, at):
        return lax.dynamic_index_in_dim(value, at["core"], 2) + got

    def blocks(self, whole):
        s = self.sizes
        return whole.reshape(s["y"], s["x"], s["core"], s["z"], -1, whole.shape[1])

    def total_core(self, value):
        return value + self.shift(value, "core", 1)

    def total_xy(self, value):
        return value + sum(self.shift_xy(value, dy, dx) for dy, dx in self.steps_xy())

    def total_z(self, value):
        return value + sum(self.shift(value, "z", d) for d in range(1, self.sizes["z"]))


AXES = ("dp", "fsdp")


def rms_norm(values, scales):
    return values * lax.rsqrt(jnp.mean(values * values, axis=-1, keepdims=True) + EPSILON) * scales


def side_by_side(value):
    r = value.shape[-2] // 2
    return jnp.concatenate([value[..., :r, :], value[..., r:, :]], axis=-1)


def norm_part(stream, gain):
    return rms_norm(stream, gain[None, :])


def on_device(
    net,
    hidden_in,
    cotangent,
    seq_lengths,
    in_weight,
    out_weight,
    vector_weight,
    head_weight,
    in_row_moment,
    in_col_moment,
    out_row_moment,
    out_col_moment,
    vector_moment,
    head_moment,
):
    token_count = hidden_in.shape[0]
    lengths = seq_lengths[0]
    e0 = lengths[0]
    e1 = e0 + lengths[1]
    e2 = e1 + lengths[2]
    e3 = e2 + lengths[3]
    ends = jnp.stack([e0, e1, e2, e3])
    valid = (jnp.arange(token_count, dtype=jnp.int32) < e3).astype(F32)
    spread, gather = spread_matrices()
    shard_rows = in_weight.shape[1]
    in_low = jnp.pad(in_weight.astype(BF16), ((0, 0), (0, 0), (0, INNER + XR - P_SIZE)))
    out_low = out_weight.astype(BF16).reshape(LAYERS, 2, shard_rows, D)
    vec_low = vector_weight.astype(BF16).reshape(-1)
    vec_low = jnp.pad(vec_low, (0, shard_rows * LANES - vec_low.shape[0])).reshape(shard_rows, LANES)
    first = net.gather(jnp.concatenate([in_low[0, :, INNER:], vec_low], axis=1), ("z", "x", "y", "core"))
    first_z = net.gather(in_low[0, :, :INNER], ("z", "y", "x", "core"))
    gap = jnp.zeros((shard_rows, 2 * INNER - XR - D), BF16)
    rest = [in_low[1, :, INNER:], out_low[0, 0], gap, in_low[1, :, :INNER], out_low[0, 1], out_low[1, 0], out_low[1, 1]]
    rest = lax.all_gather(jnp.concatenate(rest, axis=1), AXES, axis=0, tiled=True)
    devices = rest.shape[0] // shard_rows

    def out_rows(*starts):
        halves_of = [rest[:, k : k + D].reshape(devices, 1, shard_rows, D) for k in starts]
        return jnp.concatenate(halves_of, axis=1).reshape(INNER, D)

    after = 3 * INNER
    ins = [(first_z, first[:, :XR]), (rest[:, 2 * INNER : after], rest[:, :XR])]
    read_from = [(first_z, first, 0), (rest, rest, 2)]
    outs = [out_rows(XR, after), out_rows(after + D, after + 2 * D)]
    vector_full = first[:, XR:].reshape(devices, -1)[:, : LAYERS * VEC // devices]
    vector_full = vector_full.reshape(devices, LAYERS, -1).swapaxes(0, 1).reshape(LAYERS, VEC).astype(F32)
    stream = hidden_in.astype(F32)
    stored = []
    for l in range(LAYERS):
        tables = kernel_params(vector_full[l], head_weight[l])
        normed_from = hidden_in if l == 0 else stream
        normed = norm_part(stream, vector_full[l, :D]).astype(BF16)
        z = jnp.dot(normed, ins[l][0], preferred_element_type=F32)
        xr = jnp.dot(normed, ins[l][1], preferred_element_type=F32)
        gn, ys, st = mixer_forward(ends, xr, *tables, spread, z)
        stream = stream + jnp.dot(gn, outs[l], preferred_element_type=F32)
        stored.append((normed_from, normed, z, xr, gn, ys, st, tables))
    fence = lax.optimization_barrier
    blocks = token_count // SPAN
    at = net.coordinates()
    flowing = cotangent.astype(F32) * valid[:, None]
    small_parts = [None] * LAYERS
    in_sums = []
    low = []

    def product(a, b):
        return jnp.einsum("td,tp->dp", a, b, preferred_element_type=F32)

    for l in reversed(range(LAYERS)):
        normed_from, normed, z, xr, gn, ys, st, tables = stored[l]
        wire = BF16 if l == 0 else F32
        gb = low[0] if low else flowing.astype(BF16)
        grad_out = product(gn, gb)
        gb, grad_out = fence((gb, grad_out))
        got = net.core_send(net.blocks(grad_out), at)
        dgn = jnp.einsum("td,ed->te", gb, outs[l], preferred_element_type=F32)
        dgn, grad_out, got = fence((dgn, grad_out, got))
        out_sum = side_by_side(net.core_sum(net.blocks(grad_out), got, at))
        waiting = jnp.concatenate(in_sums + [out_sum], axis=-1).astype(wire)
        dgn, waiting = fence((dgn, waiting))
        waiting = net.xy_sum(waiting, wire)
        back = mixer_backward(ends, xr, ys, st, *tables, spread, gather, (z, dgn), 0, blocks)
        back, waiting = fence((back, waiting))
        if l > 0:
            out_one = waiting
        dxr, dz = back[0], back[6]
        grads = [product(normed, dxr), product(normed, dz)]
        dz, dxr, grads = fence((dz, dxr, grads))
        got = [net.core_send(net.blocks(g), at) for g in grads]
        if l == 0:
            grads, got, in_late, out_late, vector_late = fence((grads, got, in_weight, out_weight, vector_weight))
            in_sums = [net.core_sum(net.blocks(g), v, at) for g, v in zip(grads, got)]
            in_zero = jnp.concatenate(in_sums, axis=-1).astype(BF16)
            waiting = jnp.concatenate([waiting, out_one], axis=-1).astype(BF16)
            dz, dxr, in_zero, waiting = fence((dz, dxr, in_zero, waiting))
            in_zero = net.xy_sum(in_zero, BF16)
            arrived = net.z_sends(waiting, BF16)
            dz, dxr, arrived[1] = fence((dz, dxr, arrived[1]))
            arrived = sum(v.astype(F32) for v in arrived)
        gain = jnp.broadcast_to(vector_full[l, None, :D], (8, D))
        flowing, dnorm, *low = norm_backward(dz, dxr, *read_from[l], l > 0, normed_from, flowing, gain)
        if l > 0:
            flowing, grads, got = fence((flowing, grads, got))
            in_sums = [net.core_sum(net.blocks(g), v, at) for g, v in zip(grads, got)]
        dvec, dhead = finish_params(back[7], *back[1:4])
        small_parts[l] = jnp.concatenate([jnp.sum(dnorm, axis=0), dvec, dhead.reshape(-1)])
    small = jnp.stack(small_parts)
    small = jnp.pad(small, ((0, 0), (0, -small.shape[1] % LANES))).reshape(-1, LANES)
    layer_out = stream.astype(BF16)
    weight_squares = [jnp.sum(w * w, axis=tuple(range(1, w.ndim))) for w in (in_late, out_late, vector_late)]
    small = net.total_core(small)
    small, in_zero, arrived, flowing, layer_out, weight_squares = fence(
        (small, in_zero, arrived, flowing, layer_out, weight_squares)
    )
    in_zero = net.z_sum(in_zero, BF16)
    small = net.total_xy(small)
    in_zero, small = fence((in_zero, small))
    small = net.total_z(small).reshape(LAYERS, -1)
    head_total = small[:, VEC : VEC + 3 * NHEADS].reshape(LAYERS, 3, NHEADS)
    share = VEC // devices
    mine = lax.axis_index("dp") * lax.axis_size("fsdp") + lax.axis_index("fsdp")
    grad_vector = lax.dynamic_slice(small, (0, mine * share), (LAYERS, share))
    grad_in = jnp.stack(
        [jnp.concatenate([v[:, XR : XR + INNER], v[:, : P_SIZE - INNER]], axis=1) for v in (in_zero, arrived)]
    )
    out_from = XR + INNER
    grad_out = jnp.stack(
        [
            jnp.concatenate([arrived[:, k : k + D], arrived[:, k + D : k + 2 * D]], axis=0)
            for k in (out_from, out_from + 2 * D)
        ]
    )
    squares_in = grad_in * grad_in
    squares_out = grad_out * grad_out
    row_in = MOMENT_DECAY * in_row_moment + (1.0 - MOMENT_DECAY) * jnp.mean(squares_in, axis=2)
    row_out = MOMENT_DECAY * out_row_moment + (1.0 - MOMENT_DECAY) * jnp.mean(squares_out, axis=2)
    vector_new = MOMENT_DECAY * vector_moment + (1.0 - MOMENT_DECAY) * grad_vector * grad_vector
    vector_update = grad_vector * lax.rsqrt(vector_new)
    totals = jnp.stack(
        [
            jnp.sum(row_in, axis=1),
            jnp.sum(row_out, axis=1),
            *weight_squares,
            jnp.sum(vector_update * vector_update, axis=1),
        ],
        axis=1,
    )
    local = (
        jnp.sum(squares_in, axis=1),
        jnp.sum(squares_out, axis=1),
        jnp.sum(squares_in / row_in[:, :, None], axis=1),
        jnp.sum(squares_out / row_out[:, :, None], axis=1),
        totals,
    )
    edges = [0]
    for v in local:
        edges.append(edges[-1] + v.shape[1])
    summed = jnp.concatenate(local, axis=1)
    summed = jnp.pad(summed, ((0, 0), (0, -edges[-1] % LANES))).reshape(-1, LANES)
    summed = net.total_z(net.total_xy(net.total_core(summed))).reshape(LAYERS, -1)
    column_in, column_out, scaled_in, scaled_out, totals = [
        summed[:, a:b] for a, b in zip(edges[:-1], edges[1:])
    ]
    col_in = MOMENT_DECAY * in_col_moment + (1.0 - MOMENT_DECAY) * column_in / D
    col_out = MOMENT_DECAY * out_col_moment + (1.0 - MOMENT_DECAY) * column_out / INNER
    mean_in = totals[:, 0] / D
    mean_out = totals[:, 1] / INNER
    norm_in = jnp.sqrt(mean_in * jnp.sum(scaled_in / col_in, axis=1) / (D * P_SIZE))
    norm_out = jnp.sqrt(mean_out * jnp.sum(scaled_out / col_out, axis=1) / (INNER * D))
    norm_vector = jnp.sqrt(totals[:, 5] / VEC)
    head_new = MOMENT_DECAY * head_moment + (1.0 - MOMENT_DECAY) * head_total * head_total
    head_update = head_total * lax.rsqrt(head_new)
    norm_head = jnp.sqrt(jnp.mean(head_update * head_update, axis=(1, 2)))

    def step_of(square_mean, norm):
        return RELATIVE_STEP * jnp.sqrt(square_mean) / jnp.maximum(1.0, norm / CLIP_LIMIT)

    step_in = step_of(totals[:, 2] / (D * P_SIZE), norm_in)
    step_out = step_of(totals[:, 3] / (INNER * D), norm_out)
    step_vector = step_of(totals[:, 4] / VEC, norm_vector)
    step_head = step_of(jnp.mean(head_weight * head_weight, axis=(1, 2)), norm_head)
    update_in = grad_in * lax.rsqrt(row_in[:, :, None] * col_in[:, None, :] / mean_in[:, None, None])
    update_out = grad_out * lax.rsqrt(row_out[:, :, None] * col_out[:, None, :] / mean_out[:, None, None])
    new_in = in_weight - step_in[:, None, None] * update_in
    new_out = out_weight - step_out[:, None, None] * update_out
    new_vector = vector_weight - step_vector[:, None] * vector_update
    new_head = head_weight - step_head[:, None, None] * head_update
    update_rms = jnp.stack([norm_in, norm_out, norm_vector, norm_head], axis=1)
    return (
        layer_out,
        flowing,
        grad_in,
        grad_out,
        grad_vector,
        head_total,
        new_in,
        new_out,
        new_vector,
        new_head,
        new_in.astype(BF16),
        new_out.astype(BF16),
        new_vector.astype(BF16),
        new_head.astype(BF16),
        row_in,
        col_in,
        row_out,
        col_out,
        vector_new,
        head_new,
        update_rms,
    )


def solution(mesh):
    rows = P(AXES, None)
    mat = P(None, AXES, None)
    vec = P(None, AXES)
    one = P()
    return jax.shard_map(
        partial(on_device, Net(mesh)),
        mesh=mesh,
        in_specs=(rows, rows, rows, mat, mat, vec, one, vec, one, vec, one, vec, one),
        out_specs=(
            rows, rows, mat, mat, vec, one, mat, mat, vec, one, mat, mat, vec, one, vec, one, vec, one, vec, one, one,
        ),
        check_vma=False,
    )
```

```python
from functools import partial

import jax
import jax.numpy as jnp
import ml_dtypes
import numpy as np
from jax import lax
from jax.experimental import pallas as pl
from jax.experimental.pallas import tpu as pltpu
from jax.sharding import PartitionSpec as P

D = 768
NHEADS = 24
HEADDIM = 64
STATE = 128
LAYERS = 2
INNER = 1536
CH = 1792
P_SIZE = 3352
XR = 1920
VEC = 11264

EPSILON = 1e-05
MOMENT_DECAY = 0.5
CLIP_LIMIT = 1.0
RELATIVE_STEP = 0.5

SPAN = 128
GROUP = 256
GATE_ROWS = 64
GATE_BLOCK = 256
NORM_BLOCK = 512
GROUPS = INNER // GROUP
LANES = 128
LOG2E = 1.4426950408889634
VMEM_LIMIT = 60 * 1024 * 1024
F32 = jnp.float32
BF16 = jnp.bfloat16
NN = ((1,), (0,))
NT = ((1,), (1,))
TN = ((0,), (0,))

PASS_PAIR = 3
PASS_STATE = 3
PASS_RED = 2


def halves(v):
    high = v.astype(BF16)
    return high, (v - high.astype(F32)).astype(BF16)


def raw_dot(a, b, dims):
    return lax.dot_general(a, b, (dims, ((), ())), preferred_element_type=F32)


def mm(a, b, dims, passes, pack=None):
    if passes == 1:
        return raw_dot(a.astype(BF16), b.astype(BF16), dims)
    a_hi, a_lo = halves(a)
    b_hi, b_lo = halves(b)
    if pack == "k":
        left = jnp.concatenate([a_hi, a_lo], axis=dims[0][0])
        right = jnp.concatenate([b_hi, b_hi], axis=dims[1][0])
        return raw_dot(left, right, dims) + raw_dot(a_hi, b_lo, dims)
    if pack == "n":
        both = raw_dot(a_hi, jnp.concatenate([b_hi, b_lo], axis=1 - dims[1][0]), dims)
        half = both.shape[1] // 2
        return both[:, :half] + (both[:, half:] + raw_dot(a_lo, b_hi, dims))
    return raw_dot(a_hi, b_hi, dims) + (raw_dot(a_lo, b_hi, dims) + raw_dot(a_hi, b_lo, dims))


def exact_left(a01, b):
    hi, lo = halves(b)
    rest = (b - hi.astype(F32) - lo.astype(F32)).astype(BF16)
    return raw_dot(a01, hi, NN) + (raw_dot(a01, lo, NN) + raw_dot(a01, rest, NN))


def reduce_right(a, b01, passes):
    if passes == 1:
        return raw_dot(a.astype(BF16), b01, NN)
    hi, lo = halves(a)
    return raw_dot(hi, b01, NN) + raw_dot(lo, b01, NN)


def sigmoid(v):
    return 0.5 * jnp.tanh(0.5 * v) + 0.5


def partial8(v):
    return jnp.sum(v.reshape(v.shape[0] // 8, 8, v.shape[1]), axis=0)


def segment_of(place, ends_ref):
    total = (place >= ends_ref[0]).astype(jnp.int32)
    for k in range(1, 4):
        total = total + (place >= ends_ref[k]).astype(jnp.int32)
    return total


def scalar_segment(place, ends_ref):
    total = jnp.int32(0)
    for k in range(4):
        total = total + jnp.where(place >= ends_ref[k], 1, 0).astype(jnp.int32)
    return total


def block_terms(base, ends_ref, hw_ref, rate_in):
    shape = (SPAN, LANES)
    place = base + lax.broadcasted_iota(jnp.int32, shape, 0)
    seg = segment_of(place, ends_ref)
    first_seg = jnp.where(base > 0, scalar_segment(base - 1, ends_ref), -1)
    last_seg = scalar_segment(base + SPAN - 1, ends_ref)
    pre = rate_in + hw_ref[0:1, :]
    head_ok = lax.broadcasted_iota(jnp.int32, shape, 1) < NHEADS
    steps = jnp.where(head_ok, jnp.maximum(pre, 0.0) + jnp.log1p(jnp.exp(-jnp.abs(pre))), 0.0)
    log_rate = hw_ref[1:2, :] * steps
    rows = lax.broadcasted_iota(jnp.int32, (SPAN, SPAN), 0)
    cols = lax.broadcasted_iota(jnp.int32, (SPAN, SPAN), 1)
    lower = jnp.where(rows >= cols, 1.0, 0.0)
    cum = exact_left(lower.astype(BF16), log_rate * LOG2E)
    reach = jnp.where(seg == first_seg, jnp.exp2(cum), 0.0)
    to_end = jnp.where(seg == last_seg, jnp.exp2(cum[SPAN - 1 : SPAN, :] - cum), 0.0)
    seg_row = segment_of(base + cols, ends_ref)
    seg_col = segment_of(base + rows, ends_ref)
    same = seg_row == seg_col
    return place, seg, pre, steps, log_rate, cum, reach, to_end, rows, cols, same


def lag_mask(place, seg, ends_ref, lag):
    other = place + lag
    ok = (segment_of(other, ends_ref) == seg) & (other >= 0)
    return jnp.where(ok, 1.0, 0.0)


def two_parts(v):
    hi, lo = halves(v)
    return jnp.concatenate([hi, lo], axis=1)


def lane_split(v):
    first = lax.broadcasted_iota(jnp.int32, v.shape, 1) < HEADDIM
    return jnp.concatenate([jnp.where(first, v, 0.0), jnp.where(first, 0.0, v)], axis=0)


def pair_columns(cum, head):
    one = jnp.broadcast_to(cum[:, head : head + 1], (SPAN, SPAN))
    two = jnp.broadcast_to(cum[:, head + 1 : head + 2], (SPAN, SPAN))
    return jnp.concatenate([one, two], axis=1)


def pair_rows(cum_t, head):
    return jnp.concatenate([cum_t[head : head + 1, :], cum_t[head + 1 : head + 2, :]], axis=1)


def gate_rows(z_ref, ys_ref, gain_ref, gn_ref, yg):
    for r in range(ys_ref.shape[0] // GATE_ROWS):
        rs = slice(GATE_ROWS * r, GATE_ROWS * (r + 1))
        squares = jnp.zeros((GATE_ROWS, LANES), F32)
        for c in range(INNER // LANES):
            cs = slice(LANES * c, LANES * (c + 1))
            z = z_ref[rs, cs]
            gated = ys_ref[rs, cs] * (z * sigmoid(z))
            yg[rs, cs] = gated
            squares = squares + gated * gated
        scale = lax.rsqrt(jnp.sum(squares, axis=1, keepdims=True) / INNER + EPSILON)
        scale = jnp.broadcast_to(scale, (GATE_ROWS, LANES))
        for c in range(INNER // LANES):
            cs = slice(LANES * c, LANES * (c + 1))
            gn_ref[rs, cs] = (yg[rs, cs] * scale * gain_ref[0:1, cs]).astype(BF16)


def forward_kernel(gated, ends_ref, xr_ref, par_ref, gain_ref, hw_ref, spread_ref, *refs):
    if gated:
        z_ref, gn_ref, *refs = refs
    ys_ref, st_ref, buf, act, state, *yg = refs
    block = pl.program_id(0)
    base = block * SPAN

    @pl.when(block == 0)
    def _():
        buf[0:8, :] = jnp.zeros((8, CH), F32)
        state[...] = jnp.zeros_like(state)

    place, seg, pre, steps, log_rate, cum, reach, to_end, rows, cols, same = block_terms(
        base, ends_ref, hw_ref, xr_ref[:, CH:XR]
    )
    masks = [lag_mask(place, seg, ends_ref, -k) for k in range(1, 4)]
    for c in range(CH // LANES):
        cs = slice(LANES * c, LANES * (c + 1))
        now = xr_ref[:, cs]
        buf[8 : 8 + SPAN, cs] = now
        conv = par_ref[4:5, cs] + par_ref[3:4, cs] * now
        for k in range(1, 4):
            conv = conv + par_ref[3 - k : 4 - k, cs] * (masks[k - 1] * buf[8 - k : 8 - k + SPAN, cs])
        buf[0:8, cs] = now[SPAN - 8 : SPAN, :]
        act[:, cs] = conv * sigmoid(conv)
    bm = act[:, INNER : INNER + STATE]
    cm = act[:, INNER + STATE : CH]
    gram = mm(cm, bm, NT, 3)
    gram2 = jnp.concatenate([gram, gram], axis=1)
    bias = jnp.where(same & (rows >= cols), 0.0, -1e30)
    bias2 = jnp.concatenate([bias, bias], axis=1)
    cum_t = cum.T
    bm_t = bm.T
    steps2, reach2, to_end2 = two_parts(steps), two_parts(reach), two_parts(to_end)
    st_ref[0] = state[...]
    for g in range(GROUPS):
        gs = slice(GROUP * g, GROUP * (g + 1))
        spread = spread_ref[:, gs]
        x = act[:, gs]
        xd = x * raw_dot(steps2, spread, NN)
        within = []
        for q in range(2):
            head = 4 * g + 2 * q
            mix = jnp.exp2(pair_columns(cum, head) - pair_rows(cum_t, head) + bias2) * gram2
            within.append(mm(mix, lane_split(xd[:, LANES * q : LANES * (q + 1)]), NN, PASS_PAIR, "n"))
        reach_g = raw_dot(reach2, spread, NN)
        before = state[:, gs]
        scan = jnp.concatenate(within, axis=1) + mm(cm, before, NN, PASS_STATE, "k") * reach_g
        ys_ref[:, gs] = scan + gain_ref[1:2, gs] * x
        state[:, gs] = before * reach_g[SPAN - 1 : SPAN, :] + mm(
            bm_t, xd * raw_dot(to_end2, spread, NN), NN, PASS_STATE, "k"
        )
    if gated:
        gate_rows(z_ref, ys_ref, gain_ref, gn_ref, yg[0])


def gate_back_rows(z_ref, ys_ref, dgn_ref, gain_ref, dz_ref, dy_ref, dgain_ref, yg):
    for r in range(z_ref.shape[0] // GATE_ROWS):
        rs = slice(GATE_ROWS * r, GATE_ROWS * (r + 1))
        squares = jnp.zeros((GATE_ROWS, LANES), F32)
        overlap = jnp.zeros((GATE_ROWS, LANES), F32)
        for c in range(INNER // LANES):
            cs = slice(LANES * c, LANES * (c + 1))
            z = z_ref[rs, cs]
            gated = ys_ref[rs, cs] * (z * sigmoid(z))
            yg[rs, cs] = gated
            overlap = overlap + gated * (dgn_ref[rs, cs] * gain_ref[0:1, cs])
            squares = squares + gated * gated
        scale = lax.rsqrt(jnp.sum(squares, axis=1, keepdims=True) / INNER + EPSILON)
        pull = jnp.sum(overlap, axis=1, keepdims=True) * (scale * scale * scale) / INNER
        scale = jnp.broadcast_to(scale, (GATE_ROWS, LANES))
        pull = jnp.broadcast_to(pull, (GATE_ROWS, LANES))
        for c in range(INNER // LANES):
            cs = slice(LANES * c, LANES * (c + 1))
            z = z_ref[rs, cs]
            gate = sigmoid(z)
            gated = yg[rs, cs]
            dgn = dgn_ref[rs, cs] * scale
            dgain_ref[:, cs] += partial8(dgn * gated)
            dgated = dgn * gain_ref[0:1, cs] - gated * pull
            dy_ref[rs, cs] = dgated * (z * gate)
            dz_ref[rs, cs] = (dgated * ys_ref[rs, cs] * (gate * (1.0 + z * (1.0 - gate)))).astype(BF16)


def gate_back_kernel(z_ref, ys_ref, dgn_ref, gain_ref, dz_ref, dy_ref, dgain_ref, yg):
    @pl.when(pl.program_id(0) == 0)
    def _():
        dgain_ref[...] = jnp.zeros_like(dgain_ref)

    gate_back_rows(z_ref, ys_ref, dgn_ref, gain_ref, dz_ref, dy_ref, dgain_ref, yg)


def gate_forward(z, ys, gain):
    tokens = z.shape[0]
    rows = pl.BlockSpec((GATE_BLOCK, INNER), lambda i: (i, 0))
    return pl.pallas_call(
        gate_rows,
        grid=(tokens // GATE_BLOCK,),
        in_specs=[rows, rows, whole((8, INNER))],
        out_specs=rows,
        out_shape=jax.ShapeDtypeStruct((tokens, INNER), BF16),
        scratch_shapes=[pltpu.VMEM((GATE_BLOCK, INNER), F32)],
        compiler_params=pltpu.CompilerParams(vmem_limit_bytes=VMEM_LIMIT),
        cost_estimate=pl.CostEstimate(flops=20_000_000, bytes_accessed=20_000_000, transcendentals=0),
        name="gate_forward",
    )(z, ys, gain)


def gate_backward(z, ys, dgn, gain):
    tokens = z.shape[0]
    rows = pl.BlockSpec((GATE_BLOCK, INNER), lambda i: (i, 0))
    return pl.pallas_call(
        gate_back_kernel,
        grid=(tokens // GATE_BLOCK,),
        in_specs=[rows, rows, rows, whole((8, INNER))],
        out_specs=[rows, rows, whole((8, INNER))],
        out_shape=[
            jax.ShapeDtypeStruct((tokens, INNER), BF16),
            jax.ShapeDtypeStruct((tokens, INNER), F32),
            jax.ShapeDtypeStruct((8, INNER), F32),
        ],
        scratch_shapes=[pltpu.VMEM((GATE_BLOCK, INNER), F32)],
        compiler_params=pltpu.CompilerParams(vmem_limit_bytes=VMEM_LIMIT),
        cost_estimate=pl.CostEstimate(flops=60_000_000, bytes_accessed=30_000_000, transcendentals=0),
        name="gate_backward",
    )(z, ys, dgn, gain)


def backward_kernel(
    top, fused, ends_ref, xr_ref, halo_ref, ys_ref, st_ref, par_ref, gain_ref, hw_ref, spread_ref, gather_ref, *refs
):
    if fused:
        z_ref, dgn_ref, *refs = refs
        *refs, dz_ref, dgate_ref, dy_ref, yg = refs
    else:
        dy_ref, *refs = refs
    (
        dxr_ref, dpar_ref, dskip_ref, dhw_ref, rgrad, dcv_out,
        buf, act, slope, dact, dcv, dgram,
    ) = refs[-12:]
    step = pl.program_id(0)
    block = top - step
    base = block * SPAN

    @pl.when(step == 0)
    def _():
        dcv[0:8, :] = jnp.zeros((8, CH), F32)
        rgrad[...] = jnp.zeros_like(rgrad)
        dpar_ref[...] = jnp.zeros_like(dpar_ref)
        dskip_ref[...] = jnp.zeros_like(dskip_ref)
        dhw_ref[...] = jnp.zeros_like(dhw_ref)
        if fused:
            dgate_ref[...] = jnp.zeros_like(dgate_ref)

    if fused:
        gate_back_rows(z_ref, ys_ref, dgn_ref, gain_ref, dz_ref, dy_ref, dgate_ref, yg)
    place, seg, pre, steps, log_rate, cum, reach, to_end, rows, cols, same = block_terms(
        base, ends_ref, hw_ref, xr_ref[:, CH:XR]
    )
    back_masks = [lag_mask(place, seg, ends_ref, -k) for k in range(1, 4)]
    fore_masks = [lag_mask(place, seg, ends_ref, k) for k in range(1, 4)]
    for c in range(CH // LANES):
        cs = slice(LANES * c, LANES * (c + 1))
        now = xr_ref[:, cs]
        buf[0:8, cs] = halo_ref[:, cs]
        buf[8 : 8 + SPAN, cs] = now
        conv = par_ref[4:5, cs] + par_ref[3:4, cs] * now
        for k in range(1, 4):
            conv = conv + par_ref[3 - k : 4 - k, cs] * (back_masks[k - 1] * buf[8 - k : 8 - k + SPAN, cs])
        gate = sigmoid(conv)
        act[:, cs] = conv * gate
        slope[:, cs] = gate * (1.0 + conv * (1.0 - gate))
        dcv[SPAN : SPAN + 8, cs] = dcv[0:8, cs]
    bm = act[:, INNER : INNER + STATE]
    cm = act[:, INNER + STATE : CH]
    gram_t = mm(cm, bm, NT, 3).T
    gram2 = jnp.concatenate([gram_t, gram_t], axis=1)
    bias = jnp.where(same & (rows <= cols), 0.0, -1e30)
    bias2 = jnp.concatenate([bias, bias], axis=1)
    cum_t = cum.T
    cm_t = cm.T
    steps2, reach2, to_end2 = two_parts(steps), two_parts(reach), two_parts(to_end)

    dgram[...] = jnp.zeros_like(dgram)
    dbm = jnp.zeros((SPAN, STATE), F32)
    dcm = jnp.zeros((SPAN, STATE), F32)
    red_rate = jnp.zeros((SPAN, LANES), F32)
    red_tail = jnp.zeros((SPAN, LANES), F32)
    red_step = jnp.zeros((SPAN, LANES), F32)
    red_through = jnp.zeros((8, LANES), F32)
    for g in range(GROUPS):
        gs = slice(GROUP * g, GROUP * (g + 1))
        spread = spread_ref[:, gs]
        gather = gather_ref[gs, :]
        x = act[:, gs]
        skip = gain_ref[1:2, gs]
        dy = dy_ref[:, gs]
        dskip_ref[:, gs] += partial8(dy * x)
        steps_g = raw_dot(steps2, spread, NN)
        reach_g = raw_dot(reach2, spread, NN)
        to_end_g = raw_dot(to_end2, spread, NN)
        xd = x * steps_g
        dxd_in = []
        for q in range(2):
            head = 4 * g + 2 * q
            qs = slice(LANES * q, LANES * (q + 1))
            decay = jnp.exp2(pair_rows(cum_t, head) - pair_columns(cum, head) + bias2)
            dy_two = lane_split(dy[:, qs])
            dxd_in.append(mm(decay * gram2, dy_two, NN, PASS_PAIR, "n"))
            dgram[...] += decay * mm(xd[:, qs], dy_two, NT, PASS_PAIR)
        dxd_in = jnp.concatenate(dxd_in, axis=1)
        later = rgrad[:, gs]
        before = st_ref[0, :, gs]
        dxd_out = mm(bm, later, NN, PASS_STATE) * to_end_g
        dbm = dbm + mm(xd * to_end_g, later, NT, PASS_STATE, "n")
        dy_reach = dy * reach_g
        dcm = dcm + mm(dy_reach, before, NT, PASS_STATE, "n")
        fade = reach_g[SPAN - 1 : SPAN, :]
        red_through = red_through + reduce_right(partial8(before * later) * fade, gather, 2)
        rgrad[:, gs] = later * fade + mm(cm_t, dy_reach, NN, PASS_STATE)
        if PASS_PAIR == 1:
            dy_seen, xd_seen = dy.astype(BF16).astype(F32), xd.astype(BF16).astype(F32)
        else:
            dy_seen, xd_seen = dy, xd
        dxd = dxd_in + dxd_out
        red_rate = red_rate + reduce_right(dy_seen * (ys_ref[:, gs] - skip * x) - xd_seen * dxd_in, gather, 2)
        red_tail = red_tail + reduce_right(x * dxd_out, gather, PASS_RED)
        red_step = red_step + reduce_right(x * dxd, gather, PASS_RED)
        dact[:, gs] = skip * dy + steps_g * dxd
    dgram_t = dgram[:, :SPAN] + dgram[:, SPAN:]
    dact[:, INNER : INNER + STATE] = dbm + mm(dgram_t, cm, NN, 3)
    dact[:, INNER + STATE : CH] = dcm + mm(dgram_t.T, bm, NN, 3)

    upper = jnp.where(rows <= cols, 1.0, 0.0).astype(BF16)
    strict = jnp.where(rows > cols, 1.0, 0.0).astype(BF16)
    through = jnp.sum(red_through, axis=0, keepdims=True)
    drate = exact_left(upper, red_rate) + exact_left(strict, steps * red_tail) + through
    dsteps = red_step + drate * hw_ref[1:2, :]
    dpre = dsteps * sigmoid(pre)
    dhw_ref[0:8, :] += partial8(dpre)
    dhw_ref[8:16, :] += partial8(drate * log_rate)
    dxr_ref[:, CH:XR] = dpre.astype(BF16)

    for c in range(CH // LANES):
        cs = slice(LANES * c, LANES * (c + 1))
        now = xr_ref[:, cs]
        dconv = dact[:, cs] * slope[:, cs]
        dcv[0:SPAN, cs] = dconv
        dxbc = par_ref[3:4, cs] * dconv
        dpar_ref[24:32, cs] += partial8(dconv * now)
        dpar_ref[32:40, cs] += partial8(dconv)
        for k in range(1, 4):
            ahead = fore_masks[k - 1] * dcv[k : k + SPAN, cs]
            dxbc = dxbc + par_ref[3 - k : 4 - k, cs] * ahead
            dpar_ref[24 - 8 * k : 32 - 8 * k, cs] += partial8(ahead * now)
        dxr_ref[:, cs] = dxbc.astype(BF16)
    dcv_out[...] = dcv[0:8, :]


def spread_matrices():
    one = (np.arange(LANES)[:, None] == np.arange(INNER)[None, :] // HEADDIM).astype(ml_dtypes.bfloat16)
    return jnp.asarray(np.concatenate([one, one], axis=0)), jnp.asarray(one.T)


def kernel_params(vector, head):
    taps = vector[D + INNER :].reshape(5, CH)
    par = jnp.concatenate([taps, jnp.zeros((3, CH), F32)], axis=0)
    gain = jnp.stack([vector[D : D + INNER], jnp.repeat(head[2], HEADDIM)])
    gain = jnp.concatenate([gain, jnp.zeros((6, INNER), F32)], axis=0)
    hw = jnp.stack([head[0], -jnp.exp(head[1])])
    hw = jnp.pad(hw, ((0, 6), (0, LANES - NHEADS)))
    return par, gain, hw


def whole(shape):
    return pl.BlockSpec(shape, lambda i: (0,) * len(shape))


SMEM = pl.BlockSpec(memory_space=pltpu.SMEM)


def mixer_forward(ends, xr, par, gain, hw, spread, z=None):
    tokens = xr.shape[0]
    blocks = tokens // SPAN
    rows = lambda width: pl.BlockSpec((SPAN, width), lambda i: (i, 0))
    in_specs = [SMEM, rows(XR), whole((8, CH)), whole((8, INNER)), whole((8, LANES)), whole((256, INNER))]
    out_specs = [rows(INNER), pl.BlockSpec((1, STATE, INNER), lambda i: (i, 0, 0))]
    out_shape = [
        jax.ShapeDtypeStruct((tokens, INNER), F32),
        jax.ShapeDtypeStruct((blocks, STATE, INNER), F32),
    ]
    scratch = [
        pltpu.VMEM((SPAN + 8, CH), F32),
        pltpu.VMEM((SPAN, CH), F32),
        pltpu.VMEM((STATE, INNER), F32),
    ]
    more = []
    if z is not None:
        more = [z]
        in_specs.append(rows(INNER))
        out_specs.insert(0, rows(INNER))
        out_shape.insert(0, jax.ShapeDtypeStruct((tokens, INNER), BF16))
        scratch.append(pltpu.VMEM((SPAN, INNER), F32))
    return pl.pallas_call(
        partial(forward_kernel, z is not None),
        grid=(blocks,),
        in_specs=in_specs,
        out_specs=out_specs,
        out_shape=out_shape,
        scratch_shapes=scratch,
        compiler_params=pltpu.CompilerParams(vmem_limit_bytes=VMEM_LIMIT),
        cost_estimate=pl.CostEstimate(flops=30_000_000_000, bytes_accessed=30_000_000, transcendentals=0),
        name="mixer_forward",
    )(ends, xr, par, gain, hw, spread, *more)


def mixer_backward(ends, xr, ys, st, par, gain, hw, spread, gather, grads, first, last):
    tokens = xr.shape[0]
    top = last - 1
    fused = len(grads) == 2
    back = lambda width: pl.BlockSpec((SPAN, width), lambda i: (top - i, 0))
    halo = pl.BlockSpec((8, XR), lambda i: (jnp.maximum((top - i) * (SPAN // 8) - 1, 0), 0))
    in_specs = [
        SMEM,
        back(XR),
        halo,
        back(INNER),
        pl.BlockSpec((1, STATE, INNER), lambda i: (top - i, 0, 0)),
        whole((8, CH)),
        whole((8, INNER)),
        whole((8, LANES)),
        whole((256, INNER)),
        whole((INNER, LANES)),
    ]
    in_specs += [back(INNER)] * len(grads)
    outs = [
        (back(XR), (tokens, XR), BF16),
        (whole((40, CH)), (40, CH), F32),
        (whole((8, INNER)), (8, INNER), F32),
        (whole((16, LANES)), (16, LANES), F32),
        (whole((STATE, INNER)), (STATE, INNER), F32),
        (whole((8, CH)), (8, CH), F32),
    ]
    scratch = [
        pltpu.VMEM((SPAN + 8, CH), F32),
        pltpu.VMEM((SPAN, CH), F32),
        pltpu.VMEM((SPAN, CH), F32),
        pltpu.VMEM((SPAN, CH), F32),
        pltpu.VMEM((SPAN + 8, CH), F32),
        pltpu.VMEM((SPAN, 2 * SPAN), F32),
    ]
    if fused:
        outs += [(back(INNER), (tokens, INNER), BF16), (whole((8, INNER)), (8, INNER), F32)]
        scratch += [pltpu.VMEM((SPAN, INNER), F32)] * 2
    kernel = partial(backward_kernel, top, fused)
    if fused:
        def kernel(*refs):
            plain, (dz_ref, dgate_ref), used, last_two = refs[: -10], refs[-10:-8], refs[-8:-2], refs[-2:]
            backward_kernel(top, fused, *plain, *used, dz_ref, dgate_ref, *last_two)

    return pl.pallas_call(
        kernel,
        grid=(last - first,),
        in_specs=in_specs,
        out_specs=[o[0] for o in outs],
        out_shape=[jax.ShapeDtypeStruct(o[1], o[2]) for o in outs],
        scratch_shapes=scratch,
        compiler_params=pltpu.CompilerParams(vmem_limit_bytes=VMEM_LIMIT),
        cost_estimate=pl.CostEstimate(
            flops=7_000_000_000 * (last - first), bytes_accessed=5_000_000 * (last - first), transcendentals=0
        ),
        name="mixer_backward",
    )(ends, xr, xr, ys, st, par, gain, hw, spread, gather, *grads)


def norm_back_kernel(dz_ref, dxr_ref, wz_ref, wx_ref, h_ref, flow_ref, gain_ref, out_ref, dgain_ref, *low_ref):
    @pl.when(pl.program_id(0) == 0)
    def _():
        dgain_ref[...] = jnp.zeros_like(dgain_ref)

    dxn = raw_dot(dz_ref[...], wz_ref[...], NT) + raw_dot(dxr_ref[...], wx_ref[...], NT)
    h = h_ref[...].astype(F32)
    scale = lax.rsqrt(jnp.sum(h * h, axis=1, keepdims=True) / D + EPSILON)
    scaled = dxn * gain_ref[0:1, :]
    pull = jnp.sum(scaled * h, axis=1, keepdims=True) * (scale * scale * scale) / D
    total = flow_ref[...] + (scale * scaled - h * pull)
    out_ref[...] = total
    if low_ref:
        low_ref[0][...] = total.astype(BF16)
    dgain_ref[...] += partial8(dxn * (h * scale))


def norm_backward(dz, dxr, wz, wx, z_at, low, h, flowing, gain):
    tokens = dz.shape[0]
    rows = lambda width: pl.BlockSpec((NORM_BLOCK, width), lambda i: (i, 0))
    return pl.pallas_call(
        norm_back_kernel,
        grid=(tokens // NORM_BLOCK,),
        in_specs=[
            rows(INNER),
            rows(XR),
            pl.BlockSpec((D, INNER), lambda i: (0, z_at)),
            whole((D, XR)),
            rows(D),
            rows(D),
            whole((8, D)),
        ],
        out_specs=[rows(D), whole((8, D))] + [rows(D)] * low,
        out_shape=[jax.ShapeDtypeStruct((tokens, D), F32), jax.ShapeDtypeStruct((8, D), F32)]
        + [jax.ShapeDtypeStruct((tokens, D), BF16)] * low,
        compiler_params=pltpu.CompilerParams(vmem_limit_bytes=VMEM_LIMIT),
        cost_estimate=pl.CostEstimate(flops=1_000_000, bytes_accessed=1_000_000, transcendentals=0),
        name="norm_backward",
    )(dz, dxr, wz, wx, h, flowing, gain)


def finish_params(dgate, dpar, dskip, dhw):
    dtaps = jnp.sum(dpar.reshape(5, 8, CH), axis=1).reshape(5 * CH)
    dgate = jnp.sum(dgate, axis=0)
    dskip = jnp.sum(dskip.reshape(8, NHEADS, HEADDIM), axis=(0, 2))
    dh = jnp.sum(dhw.reshape(2, 8, LANES), axis=1)[:, :NHEADS]
    return jnp.concatenate([dgate, dtaps]), jnp.concatenate([dh, dskip[None]], axis=0)


class Net:
    def __init__(self, mesh):
        side = round((mesh.shape["dp"] // 2) ** 0.5)
        self.sizes = {"y": mesh.shape["dp"] // (2 * side), "x": side, "core": 2, "z": mesh.shape["fsdp"]}
        self.order = ("y", "x", "core", "z")

    def coordinates(self):
        at = lax.axis_index("dp")
        return {
            "y": at // (2 * self.sizes["x"]),
            "x": (at // 2) % self.sizes["x"],
            "core": at % 2,
            "z": lax.axis_index("fsdp"),
        }

    def shift(self, value, axis, by):
        n = self.sizes[axis]
        if axis == "z":
            return lax.ppermute(value, "fsdp", [(i, (i + by) % n) for i in range(n)])
        inner = {"y": 2 * self.sizes["x"], "x": 2, "core": 1}[axis]
        pairs = []
        for i in range(2 * self.sizes["y"] * self.sizes["x"]):
            at = (i // inner) % n
            pairs.append((i, i + ((at + by) % n - at) * inner))
        return lax.ppermute(value, "dp", pairs)

    def gather_axis(self, value, axis, at):
        n, dim = self.sizes[axis], self.order.index(axis)
        pieces = [value] + [self.shift(value, axis, d) for d in range(1, n)]
        rows = []
        for j in range(n):
            row = pieces[-j % n]
            for i in range(1, n):
                row = jnp.where(at == i, pieces[(i - j) % n], row)
            rows.append(row)
        return jnp.concatenate(rows, axis=dim)

    def gather(self, shard, axes):
        at = self.coordinates()
        value = shard[None, None, None, None]
        for axis in axes:
            value = self.gather_axis(value, axis, at[axis])
        return value.reshape(-1, shard.shape[1])

    def shift_xy(self, value, dy, dx):
        ny, nx = self.sizes["y"], self.sizes["x"]
        pairs = []
        for y in range(ny):
            for x in range(nx):
                for c in range(2):
                    pairs.append(((y * nx + x) * 2 + c, ((y + dy) % ny * nx + (x + dx) % nx) * 2 + c))
        return lax.ppermute(value, "dp", pairs)

    def steps_xy(self):
        return [(dy, dx) for dy in range(self.sizes["y"]) for dx in range(self.sizes["x"]) if dy or dx]

    def xy_sum(self, value, wire=F32):
        plane = self.sizes["y"] * self.sizes["x"]
        groups = [[2 * k + c for k in range(plane)] for c in range(2)]
        value = value.reshape(plane, *value.shape[3:]).astype(wire)
        got = lax.all_to_all(value, "dp", 0, 0, axis_index_groups=groups)
        return jnp.sum(got.astype(F32), axis=0)

    def z_sends(self, value, wire=F32):
        count, at = self.sizes["z"], lax.axis_index("fsdp")
        parts = [lax.dynamic_index_in_dim(value, (at + d) % count, 0, keepdims=False) for d in range(count)]
        return parts[:1] + [self.shift(parts[d].astype(wire), "z", d) for d in range(1, count)]

    def z_sum(self, value, wire=F32):
        return sum(v.astype(F32) for v in self.z_sends(value, wire))

    def core_send(self, value, at):
        return self.shift(lax.dynamic_index_in_dim(value, 1 - at["core"], 2), "core", 1)

    def core_sum(self, value, got, at):
        return lax.dynamic_index_in_dim(value, at["core"], 2) + got

    def blocks(self, whole):
        s = self.sizes
        return whole.reshape(s["y"], s["x"], s["core"], s["z"], -1, whole.shape[1])

    def total_core(self, value):
        return value + self.shift(value, "core", 1)

    def total_xy(self, value):
        return value + sum(self.shift_xy(value, dy, dx) for dy, dx in self.steps_xy())

    def total_z(self, value):
        return value + sum(self.shift(value, "z", d) for d in range(1, self.sizes["z"]))


AXES = ("dp", "fsdp")


def rms_norm(values, scales):
    return values * lax.rsqrt(jnp.mean(values * values, axis=-1, keepdims=True) + EPSILON) * scales


def side_by_side(value):
    r = value.shape[-2] // 2
    return jnp.concatenate([value[..., :r, :], value[..., r:, :]], axis=-1)


def norm_part(stream, gain):
    return rms_norm(stream, gain[None, :])


def on_device(
    net,
    hidden_in,
    cotangent,
    seq_lengths,
    in_weight,
    out_weight,
    vector_weight,
    head_weight,
    in_row_moment,
    in_col_moment,
    out_row_moment,
    out_col_moment,
    vector_moment,
    head_moment,
):
    token_count = hidden_in.shape[0]
    lengths = seq_lengths[0]
    e0 = lengths[0]
    e1 = e0 + lengths[1]
    e2 = e1 + lengths[2]
    e3 = e2 + lengths[3]
    ends = jnp.stack([e0, e1, e2, e3])
    valid = (jnp.arange(token_count, dtype=jnp.int32) < e3).astype(F32)
    spread, gather = spread_matrices()
    shard_rows = in_weight.shape[1]
    in_low = jnp.pad(in_weight.astype(BF16), ((0, 0), (0, 0), (0, INNER + XR - P_SIZE)))
    out_low = out_weight.astype(BF16).reshape(LAYERS, 2, shard_rows, D)
    vec_low = vector_weight.astype(BF16).reshape(-1)
    vec_low = jnp.pad(vec_low, (0, shard_rows * LANES - vec_low.shape[0])).reshape(shard_rows, LANES)
    first = net.gather(jnp.concatenate([in_low[0, :, INNER:], vec_low], axis=1), ("z", "x", "y", "core"))
    first_z = net.gather(in_low[0, :, :INNER], ("z", "y", "x", "core"))
    gap = jnp.zeros((shard_rows, 2 * INNER - XR - D), BF16)
    rest = [in_low[1, :, INNER:], out_low[0, 0], gap, in_low[1, :, :INNER], out_low[0, 1], out_low[1, 0], out_low[1, 1]]
    rest = lax.all_gather(jnp.concatenate(rest, axis=1), AXES, axis=0, tiled=True)
    devices = rest.shape[0] // shard_rows

    def out_rows(*starts):
        halves_of = [rest[:, k : k + D].reshape(devices, 1, shard_rows, D) for k in starts]
        return jnp.concatenate(halves_of, axis=1).reshape(INNER, D)

    after = 3 * INNER
    ins = [(first_z, first[:, :XR]), (rest[:, 2 * INNER : after], rest[:, :XR])]
    read_from = [(first_z, first, 0), (rest, rest, 2)]
    outs = [out_rows(XR, after), out_rows(after + D, after + 2 * D)]
    vector_full = first[:, XR:].reshape(devices, -1)[:, : LAYERS * VEC // devices]
    vector_full = vector_full.reshape(devices, LAYERS, -1).swapaxes(0, 1).reshape(LAYERS, VEC).astype(F32)
    stream = hidden_in.astype(F32)
    stored = []
    for l in range(LAYERS):
        tables = kernel_params(vector_full[l], head_weight[l])
        normed_from = hidden_in if l == 0 else stream
        normed = norm_part(stream, vector_full[l, :D]).astype(BF16)
        z = jnp.dot(normed, ins[l][0], preferred_element_type=F32)
        xr = jnp.dot(normed, ins[l][1], preferred_element_type=F32)
        gn, ys, st = mixer_forward(ends, xr, *tables, spread, z)
        stream = stream + jnp.dot(gn, outs[l], preferred_element_type=F32)
        stored.append((normed_from, normed, z, xr, gn, ys, st, tables))
    fence = lax.optimization_barrier
    blocks = token_count // SPAN
    at = net.coordinates()
    flowing = cotangent.astype(F32) * valid[:, None]
    small_parts = [None] * LAYERS
    in_sums = []
    low = []

    def product(a, b):
        return jnp.einsum("td,tp->dp", a, b, preferred_element_type=F32)

    for l in reversed(range(LAYERS)):
        normed_from, normed, z, xr, gn, ys, st, tables = stored[l]
        wire = BF16 if l == 0 else F32
        gb = low[0] if low else flowing.astype(BF16)
        grad_out = product(gn, gb)
        gb, grad_out = fence((gb, grad_out))
        got = net.core_send(net.blocks(grad_out), at)
        dgn = jnp.einsum("td,ed->te", gb, outs[l], preferred_element_type=F32)
        dgn, grad_out, got = fence((dgn, grad_out, got))
        out_sum = side_by_side(net.core_sum(net.blocks(grad_out), got, at))
        waiting = jnp.concatenate(in_sums + [out_sum], axis=-1).astype(wire)
        dgn, waiting = fence((dgn, waiting))
        waiting = net.xy_sum(waiting, wire)
        back = mixer_backward(ends, xr, ys, st, *tables, spread, gather, (z, dgn), 0, blocks)
        back, waiting = fence((back, waiting))
        if l > 0:
            out_one = waiting
        dxr, dz = back[0], back[6]
        grads = [product(normed, dxr), product(normed, dz)]
        dz, dxr, grads = fence((dz, dxr, grads))
        got = [net.core_send(net.blocks(g), at) for g in grads]
        if l == 0:
            grads, got, in_late, out_late, vector_late = fence((grads, got, in_weight, out_weight, vector_weight))
            in_sums = [net.core_sum(net.blocks(g), v, at) for g, v in zip(grads, got)]
            in_zero = jnp.concatenate(in_sums, axis=-1).astype(BF16)
            waiting = jnp.concatenate([waiting, out_one], axis=-1).astype(BF16)
            dz, dxr, in_zero, waiting = fence((dz, dxr, in_zero, waiting))
            in_zero = net.xy_sum(in_zero, BF16)
            arrived = net.z_sends(waiting, BF16)
            dz, dxr, arrived[1] = fence((dz, dxr, arrived[1]))
            arrived = sum(v.astype(F32) for v in arrived)
        gain = jnp.broadcast_to(vector_full[l, None, :D], (8, D))
        flowing, dnorm, *low = norm_backward(dz, dxr, *read_from[l], l > 0, normed_from, flowing, gain)
        if l > 0:
            flowing, grads, got = fence((flowing, grads, got))
            in_sums = [net.core_sum(net.blocks(g), v, at) for g, v in zip(grads, got)]
        dvec, dhead = finish_params(back[7], *back[1:4])
        small_parts[l] = jnp.concatenate([jnp.sum(dnorm, axis=0), dvec, dhead.reshape(-1)])
    small = jnp.stack(small_parts)
    small = jnp.pad(small, ((0, 0), (0, -small.shape[1] % LANES))).reshape(-1, LANES)
    layer_out = stream.astype(BF16)
    weight_squares = [jnp.sum(w * w, axis=tuple(range(1, w.ndim))) for w in (in_late, out_late, vector_late)]
    small = net.total_core(small)
    small, in_zero, arrived, flowing, layer_out, weight_squares = fence(
        (small, in_zero, arrived, flowing, layer_out, weight_squares)
    )
    in_zero = net.z_sum(in_zero, BF16)
    small = net.total_xy(small)
    in_zero, small = fence((in_zero, small))
    small = net.total_z(small).reshape(LAYERS, -1)
    head_total = small[:, VEC : VEC + 3 * NHEADS].reshape(LAYERS, 3, NHEADS)
    share = VEC // devices
    mine = lax.axis_index("dp") * lax.axis_size("fsdp") + lax.axis_index("fsdp")
    grad_vector = lax.dynamic_slice(small, (0, mine * share), (LAYERS, share))
    grad_in = jnp.stack(
        [jnp.concatenate([v[:, XR : XR + INNER], v[:, : P_SIZE - INNER]], axis=1) for v in (in_zero, arrived)]
    )
    out_from = XR + INNER
    grad_out = jnp.stack(
        [
            jnp.concatenate([arrived[:, k : k + D], arrived[:, k + D : k + 2 * D]], axis=0)
            for k in (out_from, out_from + 2 * D)
        ]
    )
    squares_in = grad_in * grad_in
    squares_out = grad_out * grad_out
    row_in = MOMENT_DECAY * in_row_moment + (1.0 - MOMENT_DECAY) * jnp.mean(squares_in, axis=2)
    row_out = MOMENT_DECAY * out_row_moment + (1.0 - MOMENT_DECAY) * jnp.mean(squares_out, axis=2)
    vector_new = MOMENT_DECAY * vector_moment + (1.0 - MOMENT_DECAY) * grad_vector * grad_vector
    vector_update = grad_vector * lax.rsqrt(vector_new)
    totals = jnp.stack(
        [
            jnp.sum(row_in, axis=1),
            jnp.sum(row_out, axis=1),
            *weight_squares,
            jnp.sum(vector_update * vector_update, axis=1),
        ],
        axis=1,
    )
    local = (
        jnp.sum(squares_in, axis=1),
        jnp.sum(squares_out, axis=1),
        jnp.sum(squares_in / row_in[:, :, None], axis=1),
        jnp.sum(squares_out / row_out[:, :, None], axis=1),
        totals,
    )
    edges = [0]
    for v in local:
        edges.append(edges[-1] + v.shape[1])
    summed = jnp.concatenate(local, axis=1)
    summed = jnp.pad(summed, ((0, 0), (0, -edges[-1] % LANES))).reshape(-1, LANES)
    summed = net.total_z(net.total_xy(net.total_core(summed))).reshape(LAYERS, -1)
    column_in, column_out, scaled_in, scaled_out, totals = [
        summed[:, a:b] for a, b in zip(edges[:-1], edges[1:])
    ]
    col_in = MOMENT_DECAY * in_col_moment + (1.0 - MOMENT_DECAY) * column_in / D
    col_out = MOMENT_DECAY * out_col_moment + (1.0 - MOMENT_DECAY) * column_out / INNER
    mean_in = totals[:, 0] / D
    mean_out = totals[:, 1] / INNER
    norm_in = jnp.sqrt(mean_in * jnp.sum(scaled_in / col_in, axis=1) / (D * P_SIZE))
    norm_out = jnp.sqrt(mean_out * jnp.sum(scaled_out / col_out, axis=1) / (INNER * D))
    norm_vector = jnp.sqrt(totals[:, 5] / VEC)
    head_new = MOMENT_DECAY * head_moment + (1.0 - MOMENT_DECAY) * head_total * head_total
    head_update = head_total * lax.rsqrt(head_new)
    norm_head = jnp.sqrt(jnp.mean(head_update * head_update, axis=(1, 2)))

    def step_of(square_mean, norm):
        return RELATIVE_STEP * jnp.sqrt(square_mean) / jnp.maximum(1.0, norm / CLIP_LIMIT)

    step_in = step_of(totals[:, 2] / (D * P_SIZE), norm_in)
    step_out = step_of(totals[:, 3] / (INNER * D), norm_out)
    step_vector = step_of(totals[:, 4] / VEC, norm_vector)
    step_head = step_of(jnp.mean(head_weight * head_weight, axis=(1, 2)), norm_head)
    update_in = grad_in * lax.rsqrt(row_in[:, :, None] * col_in[:, None, :] / mean_in[:, None, None])
    update_out = grad_out * lax.rsqrt(row_out[:, :, None] * col_out[:, None, :] / mean_out[:, None, None])
    new_in = in_weight - step_in[:, None, None] * update_in
    new_out = out_weight - step_out[:, None, None] * update_out
    new_vector = vector_weight - step_vector[:, None] * vector_update
    new_head = head_weight - step_head[:, None, None] * head_update
    update_rms = jnp.stack([norm_in, norm_out, norm_vector, norm_head], axis=1)
    return (
        layer_out,
        flowing,
        grad_in,
        grad_out,
        grad_vector,
        head_total,
        new_in,
        new_out,
        new_vector,
        new_head,
        new_in.astype(BF16),
        new_out.astype(BF16),
        new_vector.astype(BF16),
        new_head.astype(BF16),
        row_in,
        col_in,
        row_out,
        col_out,
        vector_new,
        head_new,
        update_rms,
    )


def solution(mesh):
    rows = P(AXES, None)
    mat = P(None, AXES, None)
    vec = P(None, AXES)
    one = P()
    return jax.shard_map(
        partial(on_device, Net(mesh)),
        mesh=mesh,
        in_specs=(rows, rows, rows, mat, mat, vec, one, vec, one, vec, one, vec, one),
        out_specs=(
            rows, rows, mat, mat, vec, one, mat, mat, vec, one, mat, mat, vec, one, vec, one, vec, one, vec, one, one,
        ),
        check_vma=False,
    )
```
